32 devices in a mesh: dp: 16 (over z, x, core), mp: 2 (over y).
Axes of the slice: x: 2, y: 2, z: 4, core: 2. Of those that a mesh axis runs over, the one named last changes fastest.
Arguments:
- query_states: bfloat16 [2048, 1024], P('dp'), may hold values from -41 to 41
- passage_states: bfloat16 [2048, 1024], P('dp'), may hold values from -41 to 41
- w_in: bfloat16 [1024, 4096], P(None, 'mp'), may hold values from -0.1875 to 0.1875
- w_out: bfloat16 [4096, 1024], P('mp'), may hold values from -0.09375 to 0.09375
- neg_owner: int32 [2048, 8], P('dp'), may hold values from 0 to 15, all different within a row; in each aligned block of 128 rows (0 to 127, 128 to 255, ...) at most 128 rows name the same one
- neg_mask: int32 [2048, 8], P('dp'), may hold values 0 or 1
- served_rows: int32 [16, 16, 128], P('dp'), may hold values from 0 to 127
- loss_scale: float32 [], replicated, may hold values from 32 to 128
Outputs:
- grad_query_states: bfloat16 [2048, 1024], P('dp', 'mp')
- grad_passage_states: bfloat16 [2048, 1024], P('dp', 'mp')
The draws below stay inside these ranges and needn't reach their ends.
Inputs may be any that keep to these rules, and one draw needn't show every extreme that they name: Within the queries of one owner (aligned blocks of 128 rows) no owner is named by more than 128 entries of neg_owner, and in some block one owner is named exactly 128 times; the 8 owners of one query are distinct.
All inputs are finite; a program needn't handle non-finite values. No bound on the sum of `neg_mask` on one device may be relied on, other than what follows from the above.
Results may differ from the reference program's by a relative error of at most 0.017.
Values may be sent and summed in bfloat16 or wider, within the bound.
No kernel may reach another device: no remote copies, remote signals or barrier semaphores. Data moves between devices by JAX's collectives and lax.ppermute only.
A program may use at most 64 MiB of HBM per device.

```python
import math
import jax
import jax.numpy as jnp
import numpy as np
from jax import lax

D = 1024
FF = 4096
NEG = 8
Q_DEV = 128
CAP = 128
QUERIES = 2048
PASSAGES = 2048
N_DP = 16


def state_draw(key, row_total, salt):
    keys = jax.random.split(jax.random.fold_in(key, salt), 3)
    base = jnp.clip(jax.random.normal(keys[0], (row_total, D), jnp.float32), -4.0, 4.0)
    span = math.log(10.0)
    row_scale = jnp.exp(jax.random.uniform(keys[1], (row_total, 1), jnp.float32, 0.0, span) - 0.5 * span)
    column_scale = jnp.exp(jax.random.uniform(keys[2], (1, D), jnp.float32, 0.0, span) - 0.5 * span)
    return base * row_scale * column_scale


def draw_query_states(key, part):
    return state_draw(key, QUERIES, 101).astype(jnp.bfloat16)


def draw_passage_states(key, part):
    return state_draw(key, PASSAGES, 202).astype(jnp.bfloat16)


def plant(result, key, low, high):
    longest = result.shape.index(max(result.shape))
    spots = []
    for shift in (0, 1):
        where = [jax.random.randint(jax.random.fold_in(key, axis), (), 0, length) for axis, length in enumerate(result.shape)]
        where[longest] = (where[longest] + shift) % result.shape[longest]
        spots.append(tuple(where))
    return result.at[spots[0]].set(low).at[spots[1]].set(high)


def level_of(own_key, dims, pieces, least, high):
    loudness, own = 1.0, jax.random.fold_in(own_key, 6)
    for axis_at, shards_of in pieces:
        heights = jnp.exp(jax.random.uniform(jax.random.fold_in(own, axis_at), (shards_of,), jnp.float32, least / len(pieces), high / len(pieces)))
        loudness = loudness * jnp.repeat(heights, dims[axis_at] // shards_of).reshape([-1 if axis == axis_at else 1 for axis in range(len(dims))])
    return loudness


def routed_block(own_key, own, number, rows, amount, top, most, skew):
    sequence = jax.random.permutation(own_key, amount)
    crowded, usual = load_shares(amount, rows * top, most, skew, True), load_shares(amount, rows * top, most, skew, False)
    places = jnp.arange(amount)

    def named(sizes, rotation):
        used = int((sizes > 0).sum())
        fixed = max(1, used // 4)
        shifted = fixed + (places - fixed + rotation * (used - fixed)) % max(1, amount - fixed)
        return jnp.zeros((amount,), jnp.int32).at[sequence[jnp.where(places < fixed, places, shifted)]].set(jnp.asarray(sizes, jnp.int32))

    sizes = jnp.where(number % 4 == 0, named(crowded, number // 4), named(usual, number - number // 4 - 1))
    mixed = jax.random.permutation(jax.random.fold_in(own, 3), amount)
    source_of, taker = mixed[0:amount // 2 * 2:2], mixed[1:amount // 2 * 2:2]
    margin = jnp.minimum(sizes[source_of] - 1, most - sizes[taker]) // 2
    margin = jnp.where((source_of == sequence[0]) | (taker == sequence[0]) | (sizes[taker] == 0), 0, jnp.maximum(margin, 0))
    shifted = jax.random.randint(jax.random.fold_in(own, 4), (amount // 2,), 0, 1 << 20) % (margin + 1)
    sizes = sizes.at[source_of].add(-shifted).at[taker].add(shifted)
    labels = jnp.searchsorted(jnp.cumsum(sizes), jnp.arange(rows * top), side="right").astype(jnp.int32)
    listing = labels.reshape(top, rows).T
    listing = listing[jax.random.permutation(jax.random.fold_in(own, 1), rows)]
    rotation = jax.random.randint(jax.random.fold_in(own, 2), (rows, 1), 0, top)
    return jnp.take_along_axis(listing, (jnp.arange(top)[None, :] + rotation) % top, axis=1)


def load_shares(count, total, most, lean, full):
    portions = [(1 << 20) // math.isqrt(rank ** lean) + 1 for rank in range(1, count + 1)]
    largest = most if full else min(most, max(-(-total // count), total * portions[0] // sum(portions)))
    least = 1 if total - largest >= count - 1 else 0
    holding, rest = [largest] + [least] * (count - 1), total - largest - least * (count - 1)
    while rest > 0:
        movable = [i for i in range(1, count) if holding[i] < largest] or [i for i in range(1, count) if holding[i] < most]
        pool, budget = sum([portions[i] for i in movable]), rest
        for i in movable:
            addition = min(most - holding[i], max(1, budget * portions[i] // pool), rest)
            holding[i] = holding[i] + addition
            rest = rest - addition
    return np.array(holding)


def normal_values(own_key, shape, scale, bound, cuts=(), held_as=jnp.bfloat16):
    loudness = level_of(own_key, shape, cuts, -0.22, 0.18) if cuts else 1.0
    array = jax.random.normal(own_key, shape, jnp.float32) * scale * loudness
    return jnp.minimum(jnp.maximum(array, -bound), bound).astype(held_as)


def setup_inputs(seed: int = 0) -> dict:
    key_list = jax.random.split(jax.random.key(seed), 9)
    query_states = draw_query_states(jax.random.fold_in(key_list[8], 71), 0)
    passage_states = draw_passage_states(jax.random.fold_in(key_list[8], 71), 0)
    w_in = normal_values(key_list[2], (D, FF), D ** -0.5, 0.1875, ((1, 2),))
    w_out = normal_values(key_list[3], (FF, D), FF ** -0.5, 0.09375, ((0, 2),))
    neg_owner_keys = jax.random.split(jax.random.fold_in(key_list[4], 1), QUERIES // Q_DEV)
    neg_owner_turns = jax.random.permutation(jax.random.fold_in(key_list[4], 3), QUERIES // Q_DEV)
    neg_owner = jax.vmap(lambda own, number: routed_block(jax.random.fold_in(key_list[4], 2), own, number, Q_DEV, N_DP, NEG, CAP, 2))(neg_owner_keys, neg_owner_turns).reshape((QUERIES, NEG))
    neg_mask = plant((jax.random.randint(key_list[5], (QUERIES, NEG), 0, 4) < 3).astype(jnp.int32), jax.random.fold_in(key_list[5], 1), 0, 1)
    served_rows = plant(jax.random.randint(key_list[6], (N_DP, N_DP, CAP), 0, Q_DEV), jax.random.fold_in(key_list[6], 1), 0, Q_DEV - 1).astype(jnp.int32)
    loss_scale = jnp.clip(jnp.exp(jax.random.uniform(key_list[7], (), jnp.float32, math.log(32.0), math.log(128.0))), 32.0, 128.0)
    return dict(query_states=query_states, passage_states=passage_states, w_in=w_in, w_out=w_out, neg_owner=neg_owner, neg_mask=neg_mask, served_rows=served_rows, loss_scale=loss_scale)


logit_scale = 50.0
norm_eps = 1e-06
root_half = 0.7071067811865476
inv_root_two_pi = 0.3989422804014327

def gelu_value(values):
    return 0.5 * values * (1.0 + lax.erf(values * root_half))

def gelu_slope(values):
    return 0.5 * (1.0 + lax.erf(values * root_half)) + values * jnp.exp(-0.5 * values * values) * inv_root_two_pi

def encode(states, w_in, w_out):
    pre_act = jnp.dot(states, w_in, preferred_element_type=jnp.float32)
    hidden = gelu_value(pre_act).astype(jnp.bfloat16)
    output = states.astype(jnp.float32) + jnp.dot(hidden, w_out, preferred_element_type=jnp.float32)
    inv_norm = lax.rsqrt(lax.optimization_barrier(jnp.sum(output * output, axis=1, keepdims=True)) + norm_eps)
    return (pre_act, output * inv_norm, inv_norm)

def decode(grad_emb, pre_act, unit_rows, inv_norm, w_in, w_out):
    grad_out = inv_norm * (grad_emb - unit_rows * lax.optimization_barrier(jnp.sum(unit_rows * grad_emb, axis=1, keepdims=True)))
    grad_hidden = jnp.dot(grad_out.astype(jnp.bfloat16), w_out.T, preferred_element_type=jnp.float32)
    grad_pre = (grad_hidden * gelu_slope(pre_act)).astype(jnp.bfloat16)
    return (grad_out + jnp.dot(grad_pre, w_in.T, preferred_element_type=jnp.float32)).astype(jnp.bfloat16)

def reference(query_states, passage_states, w_in, w_out, neg_owner, neg_mask, served_rows, loss_scale):
    pre_query, unit_query, inv_query = encode(query_states, w_in, w_out)
    pre_pass, unit_pass, inv_pass = encode(passage_states, w_in, w_out)
    emb_query = unit_query.astype(jnp.bfloat16).astype(jnp.float32)
    emb_pass = unit_pass.astype(jnp.bfloat16).astype(jnp.float32)
    owner_block = neg_owner.reshape(N_DP, Q_DEV * NEG)
    onehot = (owner_block[:, :, None] == jnp.arange(N_DP, dtype=jnp.int32)[None, None, :]).astype(jnp.int32)
    before = jnp.cumsum(onehot, axis=1, dtype=jnp.int32) - onehot
    slot_index = lax.optimization_barrier(jnp.sum(before * onehot, axis=2, dtype=jnp.int32)).astype(jnp.int32)
    source = jnp.broadcast_to(jnp.arange(N_DP, dtype=jnp.int32)[:, None], owner_block.shape)
    neg_rows = served_rows[owner_block, source, slot_index].astype(jnp.int32)
    neg_id = (owner_block * Q_DEV + neg_rows).reshape(QUERIES, NEG).astype(jnp.int32)
    neg_emb = emb_pass[neg_id]
    pos_score = lax.optimization_barrier(jnp.sum(emb_query * emb_pass, axis=1))
    neg_score = lax.optimization_barrier(jnp.sum(emb_query[:, None, :] * neg_emb, axis=2))
    exp_pos = jnp.exp(logit_scale * pos_score)
    exp_neg = neg_mask.astype(jnp.float32) * jnp.exp(logit_scale * neg_score)
    denominator = exp_pos + lax.optimization_barrier(jnp.sum(exp_neg, axis=1))
    factor = loss_scale * logit_scale
    grad_pos = factor * (exp_pos / denominator - 1.0)
    grad_neg = factor * exp_neg / denominator[:, None]
    grad_query_emb = grad_pos[:, None] * emb_pass + lax.optimization_barrier(jnp.sum(grad_neg[:, :, None] * neg_emb, axis=1))
    slot_terms = (grad_neg[:, :, None] * emb_query[:, None, :]).astype(jnp.bfloat16).astype(jnp.float32)
    returned = jax.ops.segment_sum(slot_terms.reshape(QUERIES * NEG, D), neg_id.reshape(-1), num_segments=PASSAGES)
    grad_pass_emb = grad_pos[:, None] * emb_query + returned
    grad_query_states = decode(grad_query_emb, pre_query, unit_query, inv_query, w_in, w_out)
    grad_passage_states = decode(grad_pass_emb, pre_pass, unit_pass, inv_pass, w_in, w_out)
    return (grad_query_states, grad_passage_states)
```

```python
import functools

import jax
import jax.numpy as jnp
from jax import lax
from jax.experimental import pallas as pl
from jax.experimental.pallas import tpu as pltpu
from jax.sharding import PartitionSpec as P

logit_scale = 50.0
norm_eps = 1e-06
root_half = 0.7071067811865476
inv_root_two_pi = 0.3989422804014327
f32, bf16 = jnp.float32, jnp.bfloat16
nt = (((1,), (1,)), ((), ()))
tn = (((0,), (0,)), ((), ()))
vmem = pl.BlockSpec(memory_space=pltpu.VMEM)
smem = pl.BlockSpec(memory_space=pltpu.SMEM)


def gelu_value(values):
    return 0.5 * values * (1.0 + lax.erf(values * root_half))


def gelu_slope(values):
    return (
        0.5 * (1.0 + lax.erf(values * root_half))
        + values * jnp.exp(-0.5 * values * values) * inv_root_two_pi
    )


def own_columns(values):
    column_width = values.shape[1] // lax.axis_size("mp")
    return lax.dynamic_slice_in_dim(values, lax.axis_index("mp") * column_width, column_width, 1)


def encode(states, w_in, w_out):
    pre_act = jnp.dot(states, w_in, preferred_element_type=jnp.float32)
    hidden = gelu_value(pre_act).astype(jnp.bfloat16)
    partial_out = jnp.dot(hidden, w_out, preferred_element_type=jnp.float32)
    mixed_sum = lax.psum(partial_out, "mp")
    output = states.astype(jnp.float32) + mixed_sum
    inv_norm = lax.rsqrt(jnp.sum(output * output, axis=1, keepdims=True) + norm_eps)
    return (pre_act, output * inv_norm, inv_norm)


def decode(grad_part, pre_act, unit_rows, inv_norm, w_in, w_out):
    grad_emb = lax.all_gather(grad_part.astype(jnp.bfloat16), "mp", axis=1, tiled=True).astype(
        grad_part.dtype
    )
    grad_out = inv_norm * (
        grad_emb - unit_rows * jnp.sum(unit_rows * grad_emb, axis=1, keepdims=True)
    )
    grad_hidden = lax.dot_general(
        grad_out.astype(jnp.bfloat16), w_out, nt, preferred_element_type=jnp.float32
    )
    grad_pre = (grad_hidden * gelu_slope(pre_act)).astype(jnp.bfloat16)
    partial_in = lax.dot_general(grad_pre, w_in, nt, preferred_element_type=jnp.float32)
    summed = lax.psum_scatter(
        partial_in.astype(jnp.bfloat16), "mp", scatter_dimension=1, tiled=True
    ).astype(jnp.float32)
    return (summed + own_columns(grad_out)).astype(jnp.bfloat16)


def general_shards(
    query_states, passage_states, w_in, w_out, neg_owner, neg_mask, served_rows, loss_scale
):
    owners = lax.axis_size("dp")
    row_count = query_states.shape[0]
    negatives = neg_owner.shape[1]
    capacity = served_rows.shape[2]
    pre_pass, unit_pass, inv_pass = encode(passage_states, w_in, w_out)
    emb_pass = own_columns(unit_pass).astype(jnp.bfloat16)
    column_width = emb_pass.shape[1]
    served = served_rows[0]
    flat_owner = neg_owner.reshape(-1)
    onehot = (flat_owner[:, None] == jnp.arange(owners, dtype=jnp.int32)[None, :]).astype(jnp.int32)
    before = jnp.cumsum(onehot, axis=0, dtype=jnp.int32) - onehot
    slot_index = jnp.sum(before * onehot, axis=1, dtype=jnp.int32)
    slot_place = flat_owner * capacity + slot_index
    every_emb = lax.all_gather(emb_pass, "dp", axis=0, tiled=True)
    rows_for_me = lax.all_to_all(
        served_rows, "dp", split_axis=1, concat_axis=0, tiled=True
    ).reshape(owners * capacity)
    neg_rows = jnp.take(rows_for_me, slot_place, axis=0)
    neg_emb = jnp.take(every_emb, flat_owner * row_count + neg_rows, axis=0)
    neg_emb = neg_emb.reshape(row_count, negatives, column_width)
    pre_query, unit_query, inv_query = encode(query_states, w_in, w_out)
    emb_query = own_columns(unit_query).astype(jnp.bfloat16)
    pos_part = jnp.einsum("qd,qd->q", emb_query, emb_pass, preferred_element_type=jnp.float32)
    neg_part = jnp.einsum("qd,qnd->qn", emb_query, neg_emb, preferred_element_type=jnp.float32)
    pos_score, neg_score = lax.psum((pos_part, neg_part), "mp")
    exp_pos = jnp.exp(logit_scale * pos_score)
    exp_neg = neg_mask.astype(jnp.float32) * jnp.exp(logit_scale * neg_score)
    denominator = exp_pos + jnp.sum(exp_neg, axis=1)
    factor = loss_scale * logit_scale
    grad_pos = factor * (exp_pos / denominator - 1.0)
    grad_neg = factor * exp_neg / denominator[:, None]
    query_values = emb_query.astype(jnp.float32)
    grad_query_emb = grad_pos[:, None] * emb_pass.astype(jnp.float32) + jnp.sum(
        grad_neg[:, :, None] * neg_emb.astype(jnp.float32), axis=1
    )
    slot_terms = (
        (grad_neg[:, :, None] * query_values[:, None, :])
        .astype(jnp.bfloat16)
        .reshape(-1, column_width)
    )
    outgoing_grad = (
        jnp.zeros((owners * capacity, column_width), jnp.bfloat16).at[slot_place].set(slot_terms)
    )
    returned = lax.all_to_all(
        outgoing_grad.reshape(owners, capacity, column_width),
        "dp",
        split_axis=0,
        concat_axis=0,
        tiled=True,
    )
    grad_query_states = decode(grad_query_emb, pre_query, unit_query, inv_query, w_in, w_out)
    gathered_back = (
        jnp.zeros((row_count, column_width), jnp.float32)
        .at[served.reshape(-1)]
        .add(returned.reshape(-1, column_width).astype(jnp.float32))
    )
    grad_pass_emb = grad_pos[:, None] * query_values + gathered_back
    grad_passage_states = decode(grad_pass_emb, pre_pass, unit_pass, inv_pass, w_in, w_out)
    return (grad_query_states, grad_passage_states)


both_bits, query_bits, pass_bits = (2, 1), (4,), (8,)


def swap(values, axis, bit):
    size = lax.axis_size(axis)
    return lax.ppermute(values, axis, [(i, i ^ bit) for i in range(size)])


def gather_blocks(block, bits):
    blocks = {0: block}
    for bit in bits:
        blocks.update({at | bit: swap(values, "dp", bit) for at, values in list(blocks.items())})
    return blocks


def halves(first, values):
    width = values.shape[1] // 2
    left, right = values[:, :width], values[:, width:]
    return jnp.where(first, left, right), jnp.where(first, right, left)


def encode_kernel(
    me, xq, xp, w_in, w_out, owner, mask, served,
    send_q, send_p, own_q, own_p, slope, slots_out, served_out,
    states, total,
):
    step = pl.program_id(0)
    rows = xq.shape[0]

    @pl.when(step == 0)
    def _():
        states[:rows, :] = xq[...]
        states[rows:, :] = xp[...]
        total[...] = jnp.zeros_like(total)
        lane = lax.broadcasted_iota(jnp.int32, (rows, 128), 1)
        named = jnp.zeros((rows, 128), f32)
        live = jnp.zeros((rows, 128), f32)
        for j in range(owner.shape[1]):
            hit = (owner[:, j : j + 1] == lane).astype(f32)
            named = named + hit
            live = live + hit * mask[:, j : j + 1].astype(f32)
        earlier = lax.broadcasted_iota(jnp.int32, (rows, rows), 0) < lax.broadcasted_iota(
            jnp.int32, (rows, rows), 1
        )
        slot = jnp.dot(
            named.T.astype(bf16), earlier.astype(f32).astype(bf16), preferred_element_type=f32
        )
        slot = jnp.where(live.T > 0.5, slot, -1.0)
        slots_out[...] = slot[: slots_out.shape[0], :].astype(bf16)
        served_out[...] = served[0].astype(f32).astype(bf16)

    pre = jnp.dot(states[...], w_in[...], preferred_element_type=f32)
    cdf = 0.5 * (1.0 + lax.erf(pre * root_half))
    slope[...] = (cdf + pre * jnp.exp(-0.5 * pre * pre) * inv_root_two_pi).astype(bf16)
    total[...] += jnp.dot((pre * cdf).astype(bf16), w_out[...], preferred_element_type=f32)

    @pl.when(step == pl.num_programs(0) - 1)
    def _():
        first = me[0] == 0
        for at, x, send, own in ((0, xq, send_q, own_q), (rows, xp, send_p, own_p)):
            mine, theirs = halves(first, total[at : at + rows, :])
            send[...] = theirs.astype(bf16)
            own[...] = mine + halves(first, x[...].astype(f32))[0]


def encode_both(me, xq, xp, w_in, w_out, owner, mask, served):
    rows, width = xq.shape
    hidden = w_in.shape[1]
    tile = min(512, hidden)
    owners = served.shape[1]

    def whole(shape):
        return pl.BlockSpec(shape, lambda t: (0,) * len(shape))

    half = (rows, width // 2)
    return pl.pallas_call(
        encode_kernel,
        grid=(hidden // tile,),
        in_specs=[
            smem,
            whole(xq.shape),
            whole(xp.shape),
            pl.BlockSpec((width, tile), lambda t: (0, t)),
            pl.BlockSpec((tile, width), lambda t: (t, 0)),
            whole(owner.shape),
            whole(mask.shape),
            whole(served.shape),
        ],
        out_specs=[
            whole(half),
            whole(half),
            whole(half),
            whole(half),
            pl.BlockSpec((2 * rows, tile), lambda t: (0, t)),
            whole((owners, rows)),
            whole((owners, served.shape[2])),
        ],
        out_shape=[
            jax.ShapeDtypeStruct(half, bf16),
            jax.ShapeDtypeStruct(half, bf16),
            jax.ShapeDtypeStruct(half, f32),
            jax.ShapeDtypeStruct(half, f32),
            jax.ShapeDtypeStruct((2 * rows, hidden), bf16),
            jax.ShapeDtypeStruct((owners, rows), bf16),
            jax.ShapeDtypeStruct((owners, served.shape[2]), bf16),
        ],
        scratch_shapes=[pltpu.VMEM((2 * rows, width), bf16), pltpu.VMEM((2 * rows, width), f32)],
        compiler_params=pltpu.CompilerParams(vmem_limit_bytes=24 << 20),
        name="encode_both",
    )(me, xq, xp, w_in, w_out, owner, mask, served)


def pack_kernel(own, other, numbers, out):
    rows = own.shape[0]
    out[:rows, :] = (own[...] + other[...].astype(f32)).astype(bf16)
    out[rows:, :] = jnp.zeros((out.shape[0] - rows, out.shape[1]), bf16)
    out[rows:, : numbers.shape[1]] = numbers[...]


def pack(own, other, numbers):
    return pl.pallas_call(
        pack_kernel,
        in_specs=[vmem] * 3,
        out_specs=vmem,
        out_shape=jax.ShapeDtypeStruct((own.shape[0] + numbers.shape[0], own.shape[1]), bf16),
        name="pack",
    )(own, other, numbers)


def eye_of(size):
    return (
        lax.broadcasted_iota(jnp.int32, (size, size), 0)
        == lax.broadcasted_iota(jnp.int32, (size, size), 1)
    ).astype(f32)


def score_kernel(q_at, p_at, owners, rows, ids, *refs):
    nq, npass = len(q_at), len(p_at)
    q_refs, p_refs = refs[:nq], refs[nq : nq + npass]
    table, valid, pick_p, pick_q, q_all, p_all, slots, served = refs[nq + npass :]
    for n, ref in enumerate(q_refs):
        q_all[n * rows : (n + 1) * rows, :] = ref[:rows, :]
        slots[n * owners : (n + 1) * owners, :] = ref[rows:, :128].astype(f32)
    for n, ref in enumerate(p_refs):
        p_all[n * rows : (n + 1) * rows, :] = ref[:rows, :]
        served[n * owners : (n + 1) * owners, :] = ref[rows:, :128].astype(f32)
    table[...] = jnp.zeros_like(table)
    eye = eye_of(rows)
    down = lax.broadcasted_iota(jnp.int32, (rows, rows), 0).astype(f32)
    queries = q_all[...]
    for b in range(nq):
        block = q_all[b * rows : (b + 1) * rows, :].astype(f32)
        square = jnp.sum(block * block, axis=1, keepdims=True)
        table[2 * npass : 2 * npass + 1, b * rows : (b + 1) * rows] = jnp.sum(
            eye * square, axis=0, keepdims=True
        )
    for a in range(npass):
        part = p_all[a * rows : (a + 1) * rows, :]
        block = part.astype(f32)
        square = jnp.sum(block * block, axis=1, keepdims=True)
        scores = lax.dot_general(part, queries, nt, preferred_element_type=f32)
        owner = ids[1, a]
        for b in range(nq):
            lanes = slice(b * rows, (b + 1) * rows)
            here = scores[:, lanes]
            if q_at[b] == p_at[a]:
                table[2 * npass + 1 : 2 * npass + 2, lanes] = jnp.sum(
                    eye * here, axis=0, keepdims=True
                )
                table[2 * npass + 2 : 2 * npass + 3, lanes] = jnp.sum(
                    eye * square, axis=0, keepdims=True
                )
            row_of = served[pl.ds(a * owners + ids[0, b], 1), :]
            slot_of = slots[pl.ds(b * owners + owner, 1), :]
            by_slot = (down == row_of).astype(f32).astype(bf16)
            by_query = (down == slot_of).astype(f32).astype(bf16)
            chosen = jnp.dot(by_slot, by_query, preferred_element_type=f32)
            table[a : a + 1, lanes] = jnp.sum(chosen * here, axis=0, keepdims=True)
            table[npass + a : npass + a + 1, lanes] = jnp.sum(
                chosen * square, axis=0, keepdims=True
            )
            valid[a : a + 1, lanes] = (slot_of >= 0.0).astype(f32)
            if p_at[a] in (0,) + pass_bits:
                n = ((0,) + pass_bits).index(p_at[a])
                pick_p[n * rows : (n + 1) * rows, lanes] = chosen.astype(bf16)
            if q_at[b] in (0,) + query_bits:
                n = ((0,) + query_bits).index(q_at[b])
                pick_q[a * rows : (a + 1) * rows, n * rows : (n + 1) * rows] = chosen.astype(bf16)


def score(ids, q_blocks, p_blocks, rows, owners):
    q_at, p_at = sorted(q_blocks), sorted(p_blocks)
    nq, npass = len(q_at), len(p_at)
    width = q_blocks[0].shape[1]
    table_rows = -(-(2 * npass + 3) // 8) * 8
    kernel = functools.partial(score_kernel, q_at, p_at, owners, rows)
    return pl.pallas_call(
        kernel,
        in_specs=[smem] + [vmem] * (nq + npass),
        out_specs=[vmem] * 6,
        out_shape=[
            jax.ShapeDtypeStruct((table_rows, nq * rows), f32),
            jax.ShapeDtypeStruct((npass, nq * rows), f32),
            jax.ShapeDtypeStruct(((1 + len(pass_bits)) * rows, nq * rows), bf16),
            jax.ShapeDtypeStruct((npass * rows, (1 + len(query_bits)) * rows), bf16),
            jax.ShapeDtypeStruct((nq * rows, width), bf16),
            jax.ShapeDtypeStruct((npass * rows, width), bf16),
        ],
        scratch_shapes=[pltpu.VMEM((nq * owners, 128), f32), pltpu.VMEM((npass * owners, 128), f32)],
        compiler_params=pltpu.CompilerParams(vmem_limit_bytes=32 << 20),
        name="score",
    )(ids, *[q_blocks[b] for b in q_at], *[p_blocks[a] for a in p_at])


def weigh_kernel(npass, has_pos, rows, table, other, valid, coefs, sums):
    full = table[...] + other[...]
    raw, square = full[:npass], full[npass : 2 * npass]
    inv_q = lax.rsqrt(full[2 * npass : 2 * npass + 1] + norm_eps)
    inv_pos = lax.rsqrt(full[2 * npass + 2 : 2 * npass + 3] + norm_eps)
    inv_neg = lax.rsqrt(square + norm_eps)
    exp_neg = valid[...] * jnp.exp(logit_scale * (raw * inv_q * inv_neg))
    lane = lax.broadcasted_iota(jnp.int32, inv_q.shape, 1)
    with_pos = lane < 0
    for n, has in enumerate(has_pos):
        if has:
            with_pos = with_pos | ((lane >= n * rows) & (lane < (n + 1) * rows))
    exp_pos = jnp.where(
        with_pos, jnp.exp(logit_scale * (full[2 * npass + 1 : 2 * npass + 2] * inv_q * inv_pos)), 0.0
    )
    coefs[...] = jnp.zeros_like(coefs)
    coefs[:npass] = exp_neg
    coefs[npass : 2 * npass] = exp_neg * inv_neg
    coefs[2 * npass : 2 * npass + 1] = inv_q
    coefs[2 * npass + 1 : 2 * npass + 2] = inv_pos
    neg_sum = jnp.sum(exp_neg, axis=0, keepdims=True)
    count = len(has_pos)
    for n in range(count):
        lanes = slice(n * rows, (n + 1) * rows)
        sums[n : n + 1, :] = neg_sum[:, lanes]
        sums[count + n : count + n + 1, :] = exp_pos[:, lanes]


def weigh(table, other, valid, has_pos, rows):
    return pl.pallas_call(
        functools.partial(weigh_kernel, valid.shape[0], has_pos, rows),
        in_specs=[vmem] * 3,
        out_specs=[vmem] * 2,
        out_shape=[
            jax.ShapeDtypeStruct(table.shape, f32),
            jax.ShapeDtypeStruct((2 * len(has_pos), rows), f32),
        ],
        name="weigh",
    )(table, other, valid)


def shares(sums, other, order, scale):
    count = len(order)
    theirs = jnp.concatenate([other[n : n + 1] for n in order], axis=0)
    theirs_pos = jnp.concatenate([other[count + n : count + n + 1] for n in order], axis=0)
    neg = sums[:count] + theirs
    total = neg + sums[count:] + theirs_pos
    share = scale * logit_scale / total
    return share, -share * neg


def grad_pass_kernel(order, q_at, npass, scale, coefs, sums, other, pick, q_all, own, send):
    rows = own.shape[0]
    share, pos = shares(sums[...], other[...], order, scale[0])
    share = jnp.concatenate([share[n : n + 1] for n in range(len(q_at))], axis=1)
    scaled = share * coefs[2 * npass : 2 * npass + 1]
    queries = q_all[...]
    for n, (a, out) in enumerate(((0, own), (npass // 2, send))):
        weights = pick[n * rows : (n + 1) * rows, :].astype(f32) * (coefs[a : a + 1] * scaled)
        if n == 0:
            diagonal = eye_of(rows) * (pos[:1] * coefs[2 * npass : 2 * npass + 1, :rows])
            weights = jnp.concatenate([weights[:, :rows] + diagonal, weights[:, rows:]], axis=1)
        out[...] = jnp.dot(weights.astype(bf16), queries, preferred_element_type=f32).astype(out.dtype)


def grad_query_kernel(order, q_at, npass, scale, coefs, sums, other, pick, p_all, own, send):
    rows = own.shape[0]
    share, pos = shares(sums[...], other[...], order, scale[0])
    passages = p_all[...]
    for n, (b, out) in enumerate(((0, own), (len(q_at) // 2, send))):
        lanes = slice(b * rows, (b + 1) * rows)
        pieces = []
        for a in range(npass):
            piece = pick[a * rows : (a + 1) * rows, n * rows : (n + 1) * rows].astype(f32) * (
                coefs[npass + a : npass + a + 1, lanes] * share[b : b + 1]
            )
            if n == 0 and a == 0:
                piece = piece + eye_of(rows) * (pos[:1] * coefs[2 * npass + 1 : 2 * npass + 2, :rows])
            pieces.append(piece.T.astype(bf16))
        weights = jnp.concatenate(pieces, axis=1)
        out[...] = jnp.dot(weights, passages, preferred_element_type=f32).astype(out.dtype)


def spread(kernel, name, scale, coefs, sums, other, pick, blocks, rows):
    half = (rows, blocks.shape[1])
    return pl.pallas_call(
        kernel,
        in_specs=[smem] + [vmem] * 5,
        out_specs=[vmem] * 2,
        out_shape=[jax.ShapeDtypeStruct(half, f32), jax.ShapeDtypeStruct(half, bf16)],
        compiler_params=pltpu.CompilerParams(vmem_limit_bytes=32 << 20),
        name=name,
    )(scale, coefs, sums, other, pick, blocks)


def add_kernel(own, other, out):
    out[...] = (own[...] + other[...].astype(f32)).astype(out.dtype)


def add_round(own, other, name):
    return pl.pallas_call(
        add_kernel,
        in_specs=[vmem] * 2,
        out_specs=vmem,
        out_shape=jax.ShapeDtypeStruct(own.shape, bf16),
        name=name,
    )(own, other)


def decode_kernel(
    me, grad, grad_other, raw, raw_other, slope, w_in, w_out, send, own, grad_out, total
):
    step = pl.program_id(0)
    first = me[0] == 0
    rows, width = grad.shape

    def joined(mine, theirs):
        mine, theirs = mine.astype(f32), theirs.astype(f32)
        return jnp.concatenate(
            [jnp.where(first, mine, theirs), jnp.where(first, theirs, mine)], axis=1
        )

    def out_grad():
        grads = joined(grad[...], grad_other[...])
        values = joined(raw[:rows, :], raw_other[:rows, :])
        inv_norm = lax.rsqrt(jnp.sum(values * values, axis=1, keepdims=True) + norm_eps)
        unit = values * inv_norm
        return inv_norm * (grads - unit * jnp.sum(unit * grads, axis=1, keepdims=True))

    @pl.when(step == 0)
    def _():
        grad_out[...] = out_grad()
        total[...] = jnp.zeros_like(total)

    hidden = lax.dot_general(
        grad_out[...].astype(bf16), w_out[...], nt, preferred_element_type=f32
    )
    grad_pre = (hidden * slope[...].astype(f32)).astype(bf16)
    total[...] += lax.dot_general(grad_pre, w_in[...], nt, preferred_element_type=f32)

    @pl.when(step == pl.num_programs(0) - 1)
    def _():
        mine, theirs = halves(first, total[...])
        send[...] = theirs.astype(bf16)
        own[...] = mine + halves(first, grad_out[...])[0]


def decode_one(me, grad, grad_other, raw, raw_other, slope, tower, w_in, w_out):
    rows, half = grad.shape
    width, hidden = w_in.shape
    tile = min(512, hidden)

    def whole(shape):
        return pl.BlockSpec(shape, lambda t: (0,) * len(shape))

    return pl.pallas_call(
        decode_kernel,
        grid=(hidden // tile,),
        in_specs=[
            smem,
            whole(grad.shape),
            whole(grad.shape),
            whole(raw.shape),
            whole(raw.shape),
            pl.BlockSpec((rows, tile), lambda t: (tower, t)),
            pl.BlockSpec((width, tile), lambda t: (0, t)),
            pl.BlockSpec((tile, width), lambda t: (t, 0)),
        ],
        out_specs=[whole(grad.shape)] * 2,
        out_shape=[
            jax.ShapeDtypeStruct(grad.shape, bf16),
            jax.ShapeDtypeStruct(grad.shape, f32),
        ],
        scratch_shapes=[pltpu.VMEM((rows, width), f32), pltpu.VMEM((rows, width), f32)],
        compiler_params=pltpu.CompilerParams(vmem_limit_bytes=24 << 20),
        name="decode_one",
    )(me, grad, grad_other, raw, raw_other, slope, w_in, w_out)


def paired_shards(
    query_states, passage_states, w_in, w_out, neg_owner, neg_mask, served_rows, loss_scale
):
    rows = query_states.shape[0]
    owners = served_rows.shape[1]
    me = lax.axis_index("mp").astype(jnp.int32).reshape(1)
    place = lax.axis_index("dp").astype(jnp.int32)
    send_q, send_p, own_q, own_p, slope, slots, served = encode_both(
        me, query_states, passage_states, w_in, w_out, neg_owner, neg_mask, served_rows
    )
    raw_q = pack(own_q, swap(send_q, "mp", 1), slots)
    raw_p = pack(own_p, swap(send_p, "mp", 1), served)
    q_blocks = gather_blocks(raw_q, query_bits + both_bits)
    p_blocks = gather_blocks(raw_p, pass_bits + both_bits)
    raw_q_other, raw_p_other = swap(raw_q, "mp", 1), swap(raw_p, "mp", 1)

    q_at, p_at = sorted(q_blocks), sorted(p_blocks)
    ids = jnp.stack([place ^ jnp.array(q_at, jnp.int32), place ^ jnp.array(p_at, jnp.int32)])
    table, valid, pick_p, pick_q, q_all, p_all = score(ids, q_blocks, p_blocks, rows, owners)
    has_pos = tuple(at in p_at for at in q_at)
    coefs, sums = weigh(table, swap(table, "mp", 1), valid, has_pos, rows)
    other = swap(sums, "dp", query_bits[0])
    order = tuple(q_at.index(at ^ query_bits[0]) for at in q_at)
    scale = loss_scale.reshape(1)
    pass_kernel = functools.partial(grad_pass_kernel, order, q_at, len(p_at))
    query_kernel = functools.partial(grad_query_kernel, order, q_at, len(p_at))
    mine_p, theirs_p = spread(
        pass_kernel, "grad_pass", scale, coefs, sums, other, pick_p, q_all, rows
    )
    mine_q, theirs_q = spread(
        query_kernel, "grad_query", scale, coefs, sums, other, pick_q, p_all, rows
    )
    grad_p = add_round(mine_p, swap(theirs_p, "dp", pass_bits[0]), "sum_pass")
    grad_q = add_round(mine_q, swap(theirs_q, "dp", query_bits[0]), "sum_query")
    send_q, own_q = decode_one(
        me, grad_q, swap(grad_q, "mp", 1), raw_q, raw_q_other, slope, 0, w_in, w_out
    )
    send_p, own_p = decode_one(
        me, grad_p, swap(grad_p, "mp", 1), raw_p, raw_p_other, slope, 1, w_in, w_out
    )
    return (
        add_round(own_q, swap(send_q, "mp", 1), "out_query"),
        add_round(own_p, swap(send_p, "mp", 1), "out_pass"),
    )


def solution(mesh):
    in_specs = (
        P("dp", None),
        P("dp", None),
        P(None, "mp"),
        P("mp", None),
        P("dp", None),
        P("dp", None),
        P("dp", None, None),
        P(),
    )
    out_specs = (P("dp", "mp"), P("dp", "mp"))
    gathered = sum(both_bits + query_bits + pass_bits) + 1
    paired = mesh.shape["mp"] == 2 and mesh.shape["dp"] == gathered
    shards = paired_shards if paired else general_shards
    return jax.shard_map(shards, mesh=mesh, in_specs=in_specs, out_specs=out_specs, check_vma=False)
```

```python
import functools

import jax
import jax.numpy as jnp
from jax import lax
from jax.experimental import pallas as pl
from jax.experimental.pallas import tpu as pltpu
from jax.sharding import PartitionSpec as P

logit_scale = 50.0
norm_eps = 1e-06
root_half = 0.7071067811865476
inv_root_two_pi = 0.3989422804014327
f32, bf16 = jnp.float32, jnp.bfloat16
nt = (((1,), (1,)), ((), ()))
tn = (((0,), (0,)), ((), ()))
vmem = pl.BlockSpec(memory_space=pltpu.VMEM)
smem = pl.BlockSpec(memory_space=pltpu.SMEM)
hbm = pl.BlockSpec(memory_space=pltpu.HBM)


def gelu_value(values):
    return 0.5 * values * (1.0 + lax.erf(values * root_half))


def gelu_slope(values):
    return (
        0.5 * (1.0 + lax.erf(values * root_half))
        + values * jnp.exp(-0.5 * values * values) * inv_root_two_pi
    )


def own_columns(values):
    column_width = values.shape[1] // lax.axis_size("mp")
    return lax.dynamic_slice_in_dim(values, lax.axis_index("mp") * column_width, column_width, 1)


def encode(states, w_in, w_out):
    pre_act = jnp.dot(states, w_in, preferred_element_type=jnp.float32)
    hidden = gelu_value(pre_act).astype(jnp.bfloat16)
    partial_out = jnp.dot(hidden, w_out, preferred_element_type=jnp.float32)
    mixed_sum = lax.psum(partial_out, "mp")
    output = states.astype(jnp.float32) + mixed_sum
    inv_norm = lax.rsqrt(jnp.sum(output * output, axis=1, keepdims=True) + norm_eps)
    return (pre_act, output * inv_norm, inv_norm)


def decode(grad_part, pre_act, unit_rows, inv_norm, w_in, w_out):
    grad_emb = lax.all_gather(grad_part.astype(jnp.bfloat16), "mp", axis=1, tiled=True).astype(
        grad_part.dtype
    )
    grad_out = inv_norm * (
        grad_emb - unit_rows * jnp.sum(unit_rows * grad_emb, axis=1, keepdims=True)
    )
    grad_hidden = lax.dot_general(
        grad_out.astype(jnp.bfloat16), w_out, nt, preferred_element_type=jnp.float32
    )
    grad_pre = (grad_hidden * gelu_slope(pre_act)).astype(jnp.bfloat16)
    partial_in = lax.dot_general(grad_pre, w_in, nt, preferred_element_type=jnp.float32)
    summed = lax.psum_scatter(
        partial_in.astype(jnp.bfloat16), "mp", scatter_dimension=1, tiled=True
    ).astype(jnp.float32)
    return (summed + own_columns(grad_out)).astype(jnp.bfloat16)


def general_shards(
    query_states, passage_states, w_in, w_out, neg_owner, neg_mask, served_rows, loss_scale
):
    owners = lax.axis_size("dp")
    row_count = query_states.shape[0]
    negatives = neg_owner.shape[1]
    capacity = served_rows.shape[2]
    pre_pass, unit_pass, inv_pass = encode(passage_states, w_in, w_out)
    emb_pass = own_columns(unit_pass).astype(jnp.bfloat16)
    column_width = emb_pass.shape[1]
    served = served_rows[0]
    flat_owner = neg_owner.reshape(-1)
    onehot = (flat_owner[:, None] == jnp.arange(owners, dtype=jnp.int32)[None, :]).astype(jnp.int32)
    before = jnp.cumsum(onehot, axis=0, dtype=jnp.int32) - onehot
    slot_index = jnp.sum(before * onehot, axis=1, dtype=jnp.int32)
    slot_place = flat_owner * capacity + slot_index
    every_emb = lax.all_gather(emb_pass, "dp", axis=0, tiled=True)
    rows_for_me = lax.all_to_all(
        served_rows, "dp", split_axis=1, concat_axis=0, tiled=True
    ).reshape(owners * capacity)
    neg_rows = jnp.take(rows_for_me, slot_place, axis=0)
    neg_emb = jnp.take(every_emb, flat_owner * row_count + neg_rows, axis=0)
    neg_emb = neg_emb.reshape(row_count, negatives, column_width)
    pre_query, unit_query, inv_query = encode(query_states, w_in, w_out)
    emb_query = own_columns(unit_query).astype(jnp.bfloat16)
    pos_part = jnp.einsum("qd,qd->q", emb_query, emb_pass, preferred_element_type=jnp.float32)
    neg_part = jnp.einsum("qd,qnd->qn", emb_query, neg_emb, preferred_element_type=jnp.float32)
    pos_score, neg_score = lax.psum((pos_part, neg_part), "mp")
    exp_pos = jnp.exp(logit_scale * pos_score)
    exp_neg = neg_mask.astype(jnp.float32) * jnp.exp(logit_scale * neg_score)
    denominator = exp_pos + jnp.sum(exp_neg, axis=1)
    factor = loss_scale * logit_scale
    grad_pos = factor * (exp_pos / denominator - 1.0)
    grad_neg = factor * exp_neg / denominator[:, None]
    query_values = emb_query.astype(jnp.float32)
    grad_query_emb = grad_pos[:, None] * emb_pass.astype(jnp.float32) + jnp.sum(
        grad_neg[:, :, None] * neg_emb.astype(jnp.float32), axis=1
    )
    slot_terms = (
        (grad_neg[:, :, None] * query_values[:, None, :])
        .astype(jnp.bfloat16)
        .reshape(-1, column_width)
    )
    outgoing_grad = (
        jnp.zeros((owners * capacity, column_width), jnp.bfloat16).at[slot_place].set(slot_terms)
    )
    returned = lax.all_to_all(
        outgoing_grad.reshape(owners, capacity, column_width),
        "dp",
        split_axis=0,
        concat_axis=0,
        tiled=True,
    )
    grad_query_states = decode(grad_query_emb, pre_query, unit_query, inv_query, w_in, w_out)
    gathered_back = (
        jnp.zeros((row_count, column_width), jnp.float32)
        .at[served.reshape(-1)]
        .add(returned.reshape(-1, column_width).astype(jnp.float32))
    )
    grad_pass_emb = grad_pos[:, None] * query_values + gathered_back
    grad_passage_states = decode(grad_pass_emb, pre_pass, unit_pass, inv_pass, w_in, w_out)
    return (grad_query_states, grad_passage_states)


query_bits, pass_bits = (4, 2), (8, 1)


def offsets(bits):
    found = [0]
    for bit in bits:
        found = found + [at | bit for at in found]
    return found


query_at, pass_at = offsets(query_bits), offsets(pass_bits)


def swap(values, axis, bit):
    size = lax.axis_size(axis)
    return lax.ppermute(values, axis, [(i, i ^ bit) for i in range(size)])


def gather_blocks(block, bits):
    blocks = [block]
    for bit in bits:
        blocks = blocks + [swap(values, "dp", bit) for values in blocks]
    return blocks


def halves(first, values):
    width = values.shape[1] // 2
    left, right = values[:, :width], values[:, width:]
    return jnp.where(first, left, right), jnp.where(first, right, left)


def eye_of(size):
    return (
        lax.broadcasted_iota(jnp.int32, (size, size), 0)
        == lax.broadcasted_iota(jnp.int32, (size, size), 1)
    ).astype(f32)


def local(kernel, name, outs, operands, mebibytes=1, scratch=(), scalars=()):
    return pl.pallas_call(
        kernel,
        in_specs=[smem] * len(scalars) + [vmem] * len(operands),
        out_specs=[vmem] * len(outs),
        out_shape=[pltpu.VMEM(shape, dtype) for shape, dtype in outs],
        scratch_shapes=list(scratch),
        compiler_params=pltpu.CompilerParams(vmem_limit_bytes=mebibytes << 20),
        name=name,
    )(*scalars, *[pltpu.with_memory_space_constraint(x, pltpu.VMEM) for x in operands])


def encode_kernel(
    tile, me, scale, xq, xp, w_in, w_out, owner, mask, served,
    send_q, send_p, own_q, own_p, slope, slots_out, served_out, scale_out, w_in_kept, w_out_kept,
    states, total, owner_held, mask_held, served_held, sems,
):
    rows = xq.shape[0]
    tiles = w_in.shape[1] // tile
    copies = [
        pltpu.make_async_copy(xq, states.at[:rows, :], sems.at[0]),
        pltpu.make_async_copy(xp, states.at[rows:, :], sems.at[1]),
        pltpu.make_async_copy(owner, owner_held, sems.at[2]),
        pltpu.make_async_copy(mask, mask_held, sems.at[3]),
        pltpu.make_async_copy(served, served_held, sems.at[4]),
    ]
    for t in range(tiles):
        at = slice(t * tile, (t + 1) * tile)
        copies.append(pltpu.make_async_copy(w_in.at[:, at], w_in_kept.at[:, at], sems.at[5 + 2 * t]))
        copies.append(pltpu.make_async_copy(w_out.at[at, :], w_out_kept.at[at, :], sems.at[6 + 2 * t]))
    for copy in copies:
        copy.start()
    for copy in copies[2:5]:
        copy.wait()
    owners = slots_out.shape[0]
    down = lax.broadcasted_iota(jnp.int32, (owners, rows), 0)
    named = jnp.zeros((owners, rows), f32)
    live = jnp.zeros((owners, rows), f32)
    for j in range(owner.shape[0]):
        hit = (owner_held[j : j + 1, :] == down).astype(f32)
        named = named + hit
        live = live + hit * mask_held[j : j + 1, :].astype(f32)
    earlier = lax.broadcasted_iota(jnp.int32, (rows, rows), 0) < lax.broadcasted_iota(
        jnp.int32, (rows, rows), 1
    )
    slot = jnp.dot(named.astype(bf16), earlier.astype(f32).astype(bf16), preferred_element_type=f32)
    slots_out[...] = jnp.where(live > 0.5, slot, -1.0).astype(bf16)
    served_out[...] = served_held[0].astype(f32).astype(bf16)
    scale_out[...] = jnp.zeros_like(scale_out) + scale[0] * logit_scale
    copies[0].wait()
    copies[1].wait()
    for t in range(tiles):
        at = slice(t * tile, (t + 1) * tile)
        copies[5 + 2 * t].wait()
        pre = jnp.dot(states[...], w_in_kept[:, at], preferred_element_type=f32)
        cdf = 0.5 * (1.0 + lax.erf(pre * root_half))
        slope[:, at] = (cdf + pre * jnp.exp(-0.5 * pre * pre) * inv_root_two_pi).astype(bf16)
        hidden = (pre * cdf).astype(bf16)
        copies[6 + 2 * t].wait()
        part = jnp.dot(hidden, w_out_kept[at, :], preferred_element_type=f32)
        if t == 0:
            total[...] = part
        else:
            total[...] += part
    first = me[0] == 0
    for at, send, own in ((0, send_q, own_q), (rows, send_p, own_p)):
        mine, theirs = halves(first, total[at : at + rows, :])
        send[...] = theirs.astype(bf16)
        own[...] = mine + halves(first, states[at : at + rows, :].astype(f32))[0]


def encode_both(me, scale, xq, xp, w_in, w_out, owner, mask, served):
    rows, width = xq.shape
    hidden = w_in.shape[1]
    tile = min(512, hidden)
    owners = served.shape[1]
    half = (rows, width // 2)
    operands = (xq, xp, w_in, w_out, owner.T, mask.T, served)
    return pl.pallas_call(
        functools.partial(encode_kernel, tile),
        in_specs=[smem] * 2 + [hbm] * 7,
        out_specs=[vmem] * 10,
        out_shape=[
            pltpu.VMEM(half, bf16),
            pltpu.VMEM(half, bf16),
            pltpu.VMEM(half, f32),
            pltpu.VMEM(half, f32),
            pltpu.VMEM((2 * rows, hidden), bf16),
            pltpu.VMEM((owners, rows), bf16),
            pltpu.VMEM((owners, served.shape[2]), bf16),
            pltpu.VMEM((8, rows), f32),
            pltpu.VMEM(w_in.shape, bf16),
            pltpu.VMEM(w_out.shape, bf16),
        ],
        scratch_shapes=[
            pltpu.VMEM((2 * rows, width), bf16),
            pltpu.VMEM((2 * rows, width), f32),
            pltpu.VMEM(owner.T.shape, jnp.int32),
            pltpu.VMEM(mask.T.shape, jnp.int32),
            pltpu.VMEM(served.shape, jnp.int32),
            pltpu.SemaphoreType.DMA((5 + 2 * (hidden // tile),)),
        ],
        compiler_params=pltpu.CompilerParams(vmem_limit_bytes=8 << 20),
        name="encode_both",
    )(me, scale, *[pltpu.with_memory_space_constraint(x, pltpu.HBM) for x in operands])


def pack_kernel(own, other, numbers, out):
    rows = own.shape[0]
    out[:rows, :] = (own[...] + other[...].astype(f32)).astype(bf16)
    out[rows:, :] = jnp.zeros((out.shape[0] - rows, out.shape[1]), bf16)
    out[rows:, : numbers.shape[1]] = numbers[...]


def pack(own, other, numbers):
    shape = (own.shape[0] + numbers.shape[0], own.shape[1])
    return local(pack_kernel, "pack", [(shape, bf16)], (own, other, numbers))[0]


def score_kernel(owners, rows, place, *refs):
    nq, npass = len(query_at), len(pass_at)
    q_refs, p_refs = refs[:nq], refs[nq : nq + npass]
    table, valid, pick, q_all, p_all, slots, served = refs[nq + npass :]
    for n, ref in enumerate(q_refs):
        q_all[n * rows : (n + 1) * rows, :] = ref[:rows, :]
        slots[n * owners : (n + 1) * owners, :] = ref[rows:, :rows].astype(f32)
    for n, ref in enumerate(p_refs):
        p_all[n * rows : (n + 1) * rows, :] = ref[:rows, :]
        served[n * owners : (n + 1) * owners, :] = ref[rows:, :rows].astype(f32)
    table[...] = jnp.zeros_like(table)
    eye = eye_of(rows)
    down = lax.broadcasted_iota(jnp.int32, (rows, rows), 0).astype(f32)
    queries = q_all[...]
    for b in range(nq):
        block = q_all[b * rows : (b + 1) * rows, :].astype(f32)
        square = jnp.sum(block * block, axis=1, keepdims=True)
        table[2 * npass : 2 * npass + 1, b * rows : (b + 1) * rows] = jnp.sum(
            eye * square, axis=0, keepdims=True
        )
    for a in range(npass):
        part = p_all[a * rows : (a + 1) * rows, :]
        block = part.astype(f32)
        square = jnp.sum(block * block, axis=1, keepdims=True)
        scores = lax.dot_general(part, queries, nt, preferred_element_type=f32)
        if a == 0:
            table[2 * npass + 1 : 2 * npass + 2, :rows] = jnp.sum(
                eye * scores[:, :rows], axis=0, keepdims=True
            )
            table[2 * npass + 2 : 2 * npass + 3, :rows] = jnp.sum(
                eye * square, axis=0, keepdims=True
            )
        for b in range(nq):
            lanes = slice(b * rows, (b + 1) * rows)
            row_of = served[pl.ds(a * owners + (place[0] ^ query_at[b]), 1), :]
            slot_of = slots[pl.ds(b * owners + (place[0] ^ pass_at[a]), 1), :]
            by_slot = (down == row_of).astype(f32).astype(bf16)
            by_query = (down == slot_of).astype(f32).astype(bf16)
            chosen = jnp.dot(by_slot, by_query, preferred_element_type=f32)
            table[a : a + 1, lanes] = jnp.sum(chosen * scores[:, lanes], axis=0, keepdims=True)
            table[npass + a : npass + a + 1, lanes] = jnp.sum(
                chosen * square, axis=0, keepdims=True
            )
            valid[a : a + 1, lanes] = (slot_of >= 0.0).astype(f32)
            pick[a * rows : (a + 1) * rows, lanes] = chosen.astype(bf16)


def score(place, q_blocks, p_blocks, rows, owners):
    nq, npass = len(query_at), len(pass_at)
    width = q_blocks[0].shape[1]
    return local(
        functools.partial(score_kernel, owners, rows),
        "score",
        [
            ((-(-(2 * npass + 3) // 8) * 8, nq * rows), f32),
            ((npass, nq * rows), f32),
            ((npass * rows, nq * rows), bf16),
            ((nq * rows, width), bf16),
            ((npass * rows, width), bf16),
        ],
        (*q_blocks, *p_blocks),
        3,
        [pltpu.VMEM((nq * owners, rows), f32), pltpu.VMEM((npass * owners, rows), f32)],
        [place],
    )


def weigh_kernel(rows, table, other, valid, coefs, sums):
    nq, npass = len(query_at), len(pass_at)
    full = table[...] + other[...]
    raw, square = full[:npass], full[npass : 2 * npass]
    inv_q = lax.rsqrt(full[2 * npass : 2 * npass + 1] + norm_eps)
    inv_pos = lax.rsqrt(full[2 * npass + 2 : 2 * npass + 3] + norm_eps)
    inv_neg = lax.rsqrt(square + norm_eps)
    exp_neg = valid[...] * jnp.exp(logit_scale * (raw * inv_q * inv_neg))
    pos_score = full[2 * npass + 1 : 2 * npass + 2] * inv_q * inv_pos
    coefs[...] = jnp.zeros_like(coefs)
    coefs[:npass] = exp_neg
    coefs[npass : 2 * npass] = exp_neg * inv_neg
    coefs[2 * npass : 2 * npass + 1] = inv_q
    coefs[2 * npass + 1 : 2 * npass + 2] = inv_pos
    neg_sum = jnp.sum(exp_neg, axis=0, keepdims=True)
    sums[...] = jnp.zeros_like(sums)
    for n in range(nq):
        sums[n : n + 1, :] = neg_sum[:, n * rows : (n + 1) * rows]
    sums[nq : nq + 1, :] = jnp.exp(logit_scale * pos_score[:, :rows])


def weigh(table, other, valid, rows):
    return local(
        functools.partial(weigh_kernel, rows),
        "weigh",
        [(table.shape, f32), ((2 * len(query_at), rows), f32)],
        (table, other, valid),
    )


def add_sums_kernel(bit, sums, other, out):
    nq = len(query_at)
    for n, at in enumerate(query_at):
        m = query_at.index(at ^ bit)
        for k, l in ((n, m), (nq + n, nq + m)):
            out[k : k + 1, :] = sums[k : k + 1, :] + other[l : l + 1, :]


def spread_query_kernel(rows, coefs, pick, p_all, kept, sent):
    npass = len(pass_at)
    passages = p_all[...]
    for b in range(len(query_at)):
        lanes = slice(b * rows, (b + 1) * rows)
        pieces = []
        for a in range(npass):
            piece = pick[a * rows : (a + 1) * rows, lanes].astype(f32)
            piece = piece * coefs[npass + a : npass + a + 1, lanes]
            pieces.append(piece.T.astype(bf16))
        weights = jnp.concatenate(pieces, axis=1)
        out, at = (kept, b) if b < len(query_at) // 2 else (sent, b - len(query_at) // 2)
        out[at * rows : (at + 1) * rows, :] = jnp.dot(
            weights, passages, preferred_element_type=f32
        ).astype(out.dtype)


def spread_pass_kernel(rows, scale, coefs, sums, pick, q_all, kept, sent):
    nq, npass = len(query_at), len(pass_at)
    total = sums[:nq] + sums[nq:]
    share = scale[:nq] / total
    pos = -share[:1] * sums[:1] * coefs[2 * npass : 2 * npass + 1, :rows]
    share = jnp.concatenate([share[n : n + 1] for n in range(nq)], axis=1)
    scaled = share * coefs[2 * npass : 2 * npass + 1]
    queries = q_all[...]
    for a in range(npass):
        weights = pick[a * rows : (a + 1) * rows, :].astype(f32) * (coefs[a : a + 1] * scaled)
        if a == 0:
            weights = jnp.concatenate(
                [weights[:, :rows] + eye_of(rows) * pos, weights[:, rows:]], axis=1
            )
        out, at = (kept, a) if a < npass // 2 else (sent, a - npass // 2)
        out[at * rows : (at + 1) * rows, :] = jnp.dot(
            weights.astype(bf16), queries, preferred_element_type=f32
        ).astype(out.dtype)


def spread(kernel, name, operands, rows, width, count):
    half = (count // 2 * rows, width)
    return local(functools.partial(kernel, rows), name, [(half, f32), (half, bf16)], operands, 3)


def fold_kernel(own, other, kept, sent):
    rows = kept.shape[0]
    total = own[...] + other[...].astype(f32)
    kept[...] = total[:rows]
    sent[...] = total[rows:].astype(bf16)


def fold(own, other, name):
    half = (own.shape[0] // 2, own.shape[1])
    return local(fold_kernel, name, [(half, f32), (half, bf16)], (own, other))


def add_kernel(own, other, out):
    out[...] = (own[...] + other[...].astype(f32)).astype(out.dtype)


def grad_query_kernel(own, other, scale, sums, coefs, raw_pass, out):
    nq, npass = len(query_at), len(pass_at)
    rows = own.shape[0]
    eye = eye_of(rows)
    share = scale[:1] / (sums[:1] + sums[nq : nq + 1])
    pos = sums[:1] * coefs[2 * npass + 1 : 2 * npass + 2, :rows]
    share = jnp.sum(eye * share, axis=1, keepdims=True)
    pos = jnp.sum(eye * pos, axis=1, keepdims=True)
    total = own[...] + other[...].astype(f32) - pos * raw_pass[:rows, :].astype(f32)
    out[...] = (share * total).astype(bf16)


def decode_kernel(
    tower, tile, me, grad, grad_other, raw, raw_other, slope, w_in, w_out, send, own, total
):
    first = me[0] == 0
    rows, width = grad.shape

    def joined(mine, theirs):
        mine, theirs = mine.astype(f32), theirs.astype(f32)
        return jnp.concatenate(
            [jnp.where(first, mine, theirs), jnp.where(first, theirs, mine)], axis=1
        )

    grads = joined(grad[...], grad_other[...])
    values = joined(raw[:rows, :], raw_other[:rows, :])
    inv_norm = lax.rsqrt(jnp.sum(values * values, axis=1, keepdims=True) + norm_eps)
    unit = values * inv_norm
    grad_out = inv_norm * (grads - unit * jnp.sum(unit * grads, axis=1, keepdims=True))
    own[...] = halves(first, grad_out)[0]
    rounded = grad_out.astype(bf16)
    for t in range(w_in.shape[1] // tile):
        at = slice(t * tile, (t + 1) * tile)
        hidden = lax.dot_general(rounded, w_out[at, :], nt, preferred_element_type=f32)
        grad_pre = (hidden * slope[tower * rows : (tower + 1) * rows, at].astype(f32)).astype(bf16)
        part = lax.dot_general(grad_pre, w_in[:, at], nt, preferred_element_type=f32)
        if t == 0:
            total[...] = part
        else:
            total[...] += part
    mine, theirs = halves(first, total[...])
    send[...] = theirs.astype(bf16)
    own[...] += mine


def decode_one(me, grad, grad_other, raw, raw_other, slope, tower, w_in, w_out):
    rows, width = grad.shape[0], w_in.shape[0]
    return local(
        functools.partial(decode_kernel, tower, min(512, w_in.shape[1])),
        "decode_one",
        [(grad.shape, bf16), (grad.shape, f32)],
        (grad, grad_other, raw, raw_other, slope, w_in, w_out),
        3,
        [pltpu.VMEM((rows, width), f32)],
        [me],
    )


def finish(own, other, name):
    return pl.pallas_call(
        add_kernel,
        in_specs=[vmem] * 2,
        out_specs=vmem,
        out_shape=jax.ShapeDtypeStruct(own.shape, bf16),
        compiler_params=pltpu.CompilerParams(vmem_limit_bytes=1 << 20),
        name=name,
    )(*[pltpu.with_memory_space_constraint(x, pltpu.VMEM) for x in (own, other)])


def paired_shards(
    query_states, passage_states, w_in, w_out, neg_owner, neg_mask, served_rows, loss_scale
):
    rows = query_states.shape[0]
    owners = served_rows.shape[1]
    me = lax.axis_index("mp").astype(jnp.int32).reshape(1)
    place = lax.axis_index("dp").astype(jnp.int32).reshape(1)
    send_q, send_p, own_q, own_p, slope, slots, served, scale, w_in, w_out = encode_both(
        me, loss_scale.reshape(1), query_states, passage_states, w_in, w_out, neg_owner, neg_mask, served_rows
    )
    raw_q = pack(own_q, swap(send_q, "mp", 1), slots)
    raw_p = pack(own_p, swap(send_p, "mp", 1), served)
    width = raw_q.shape[1]
    q_blocks = gather_blocks(raw_q, query_bits)
    p_blocks = gather_blocks(raw_p, pass_bits)
    raw_q_other, raw_p_other = swap(raw_q, "mp", 1), swap(raw_p, "mp", 1)

    table, valid, pick, q_all, p_all = score(place, q_blocks, p_blocks, rows, owners)
    coefs, sums = weigh(table, swap(table, "mp", 1), valid, rows)
    nq, npass = len(query_at), len(pass_at)
    kept_q, sent_q = spread(
        spread_query_kernel, "spread_query", (coefs, pick, p_all), rows, width, nq
    )
    for bit in query_bits:
        sums = local(
            functools.partial(add_sums_kernel, bit),
            "add_sums",
            [(sums.shape, f32)],
            (sums, swap(sums, "dp", bit)),
        )[0]
    kept_p, sent_p = spread(
        spread_pass_kernel, "spread_pass", (scale, coefs, sums, pick, q_all), rows, width, npass
    )
    half = ((rows, width), bf16)
    kept_p, sent_p = fold(kept_p, swap(sent_p, "dp", pass_bits[1]), "fold_pass")
    grad_p = local(add_kernel, "grad_pass", [half], (kept_p, swap(sent_p, "dp", pass_bits[0])))[0]
    kept_q, sent_q = fold(kept_q, swap(sent_q, "dp", query_bits[1]), "fold_query")
    grad_q = local(
        grad_query_kernel,
        "grad_query",
        [half],
        (kept_q, swap(sent_q, "dp", query_bits[0]), scale, sums, coefs, raw_p),
    )[0]
    send_q, own_q = decode_one(
        me, grad_q, swap(grad_q, "mp", 1), raw_q, raw_q_other, slope, 0, w_in, w_out
    )
    send_p, own_p = decode_one(
        me, grad_p, swap(grad_p, "mp", 1), raw_p, raw_p_other, slope, 1, w_in, w_out
    )
    return (
        finish(own_q, swap(send_q, "mp", 1), "out_query"),
        finish(own_p, swap(send_p, "mp", 1), "out_pass"),
    )


def solution(mesh):
    in_specs = (
        P("dp", None),
        P("dp", None),
        P(None, "mp"),
        P("mp", None),
        P("dp", None),
        P("dp", None),
        P("dp", None, None),
        P(),
    )
    out_specs = (P("dp", "mp"), P("dp", "mp"))
    gathered = len(query_at) * len(pass_at)
    paired = mesh.shape["mp"] == 2 and mesh.shape["dp"] == gathered
    shards = paired_shards if paired else general_shards
    return jax.shard_map(shards, mesh=mesh, in_specs=in_specs, out_specs=out_specs, check_vma=False)
```

```python
import functools

import jax
import jax.numpy as jnp
from jax import lax
from jax.experimental import pallas as pl
from jax.experimental.pallas import tpu as pltpu
from jax.sharding import PartitionSpec as P

logit_scale = 50.0
norm_eps = 1e-06
root_half = 0.7071067811865476
inv_root_two_pi = 0.3989422804014327
f32, bf16 = jnp.float32, jnp.bfloat16
nt = (((1,), (1,)), ((), ()))
tn = (((0,), (0,)), ((), ()))
vmem = pl.BlockSpec(memory_space=pltpu.VMEM)
smem = pl.BlockSpec(memory_space=pltpu.SMEM)
hbm = pl.BlockSpec(memory_space=pltpu.HBM)


def gelu_value(values):
    return 0.5 * values * (1.0 + lax.erf(values * root_half))


def gelu_slope(values):
    return (
        0.5 * (1.0 + lax.erf(values * root_half))
        + values * jnp.exp(-0.5 * values * values) * inv_root_two_pi
    )


def own_columns(values):
    column_width = values.shape[1] // lax.axis_size("mp")
    return lax.dynamic_slice_in_dim(values, lax.axis_index("mp") * column_width, column_width, 1)


def encode(states, w_in, w_out):
    pre_act = jnp.dot(states, w_in, preferred_element_type=jnp.float32)
    hidden = gelu_value(pre_act).astype(jnp.bfloat16)
    partial_out = jnp.dot(hidden, w_out, preferred_element_type=jnp.float32)
    mixed_sum = lax.psum(partial_out, "mp")
    output = states.astype(jnp.float32) + mixed_sum
    inv_norm = lax.rsqrt(jnp.sum(output * output, axis=1, keepdims=True) + norm_eps)
    return (pre_act, output * inv_norm, inv_norm)


def decode(grad_part, pre_act, unit_rows, inv_norm, w_in, w_out):
    grad_emb = lax.all_gather(grad_part.astype(jnp.bfloat16), "mp", axis=1, tiled=True).astype(
        grad_part.dtype
    )
    grad_out = inv_norm * (
        grad_emb - unit_rows * jnp.sum(unit_rows * grad_emb, axis=1, keepdims=True)
    )
    grad_hidden = lax.dot_general(
        grad_out.astype(jnp.bfloat16), w_out, nt, preferred_element_type=jnp.float32
    )
    grad_pre = (grad_hidden * gelu_slope(pre_act)).astype(jnp.bfloat16)
    partial_in = lax.dot_general(grad_pre, w_in, nt, preferred_element_type=jnp.float32)
    summed = lax.psum_scatter(
        partial_in.astype(jnp.bfloat16), "mp", scatter_dimension=1, tiled=True
    ).astype(jnp.float32)
    return (summed + own_columns(grad_out)).astype(jnp.bfloat16)


def general_shards(
    query_states, passage_states, w_in, w_out, neg_owner, neg_mask, served_rows, loss_scale
):
    owners = lax.axis_size("dp")
    row_count = query_states.shape[0]
    negatives = neg_owner.shape[1]
    capacity = served_rows.shape[2]
    pre_pass, unit_pass, inv_pass = encode(passage_states, w_in, w_out)
    emb_pass = own_columns(unit_pass).astype(jnp.bfloat16)
    column_width = emb_pass.shape[1]
    served = served_rows[0]
    flat_owner = neg_owner.reshape(-1)
    onehot = (flat_owner[:, None] == jnp.arange(owners, dtype=jnp.int32)[None, :]).astype(jnp.int32)
    before = jnp.cumsum(onehot, axis=0, dtype=jnp.int32) - onehot
    slot_index = jnp.sum(before * onehot, axis=1, dtype=jnp.int32)
    slot_place = flat_owner * capacity + slot_index
    every_emb = lax.all_gather(emb_pass, "dp", axis=0, tiled=True)
    rows_for_me = lax.all_to_all(
        served_rows, "dp", split_axis=1, concat_axis=0, tiled=True
    ).reshape(owners * capacity)
    neg_rows = jnp.take(rows_for_me, slot_place, axis=0)
    neg_emb = jnp.take(every_emb, flat_owner * row_count + neg_rows, axis=0)
    neg_emb = neg_emb.reshape(row_count, negatives, column_width)
    pre_query, unit_query, inv_query = encode(query_states, w_in, w_out)
    emb_query = own_columns(unit_query).astype(jnp.bfloat16)
    pos_part = jnp.einsum("qd,qd->q", emb_query, emb_pass, preferred_element_type=jnp.float32)
    neg_part = jnp.einsum("qd,qnd->qn", emb_query, neg_emb, preferred_element_type=jnp.float32)
    pos_score, neg_score = lax.psum((pos_part, neg_part), "mp")
    exp_pos = jnp.exp(logit_scale * pos_score)
    exp_neg = neg_mask.astype(jnp.float32) * jnp.exp(logit_scale * neg_score)
    denominator = exp_pos + jnp.sum(exp_neg, axis=1)
    factor = loss_scale * logit_scale
    grad_pos = factor * (exp_pos / denominator - 1.0)
    grad_neg = factor * exp_neg / denominator[:, None]
    query_values = emb_query.astype(jnp.float32)
    grad_query_emb = grad_pos[:, None] * emb_pass.astype(jnp.float32) + jnp.sum(
        grad_neg[:, :, None] * neg_emb.astype(jnp.float32), axis=1
    )
    slot_terms = (
        (grad_neg[:, :, None] * query_values[:, None, :])
        .astype(jnp.bfloat16)
        .reshape(-1, column_width)
    )
    outgoing_grad = (
        jnp.zeros((owners * capacity, column_width), jnp.bfloat16).at[slot_place].set(slot_terms)
    )
    returned = lax.all_to_all(
        outgoing_grad.reshape(owners, capacity, column_width),
        "dp",
        split_axis=0,
        concat_axis=0,
        tiled=True,
    )
    grad_query_states = decode(grad_query_emb, pre_query, unit_query, inv_query, w_in, w_out)
    gathered_back = (
        jnp.zeros((row_count, column_width), jnp.float32)
        .at[served.reshape(-1)]
        .add(returned.reshape(-1, column_width).astype(jnp.float32))
    )
    grad_pass_emb = grad_pos[:, None] * query_values + gathered_back
    grad_passage_states = decode(grad_pass_emb, pre_pass, unit_pass, inv_pass, w_in, w_out)
    return (grad_query_states, grad_passage_states)


query_bits, pass_bits = (4, 2), (8, 1)


def offsets(bits):
    found = [0]
    for bit in bits:
        found = found + [at | bit for at in found]
    return found


query_at, pass_at = offsets(query_bits), offsets(pass_bits)


def swap(values, axis, bit):
    size = lax.axis_size(axis)
    return lax.ppermute(values, axis, [(i, i ^ bit) for i in range(size)])


def gather_blocks(block, bits):
    blocks = [block]
    for bit in bits:
        blocks = blocks + [swap(values, "dp", bit) for values in blocks]
    return blocks


def halves(first, values):
    width = values.shape[1] // 2
    left, right = values[:, :width], values[:, width:]
    return jnp.where(first, left, right), jnp.where(first, right, left)


def eye_of(size):
    return (
        lax.broadcasted_iota(jnp.int32, (size, size), 0)
        == lax.broadcasted_iota(jnp.int32, (size, size), 1)
    ).astype(f32)


def local(kernel, name, outs, operands, mebibytes=1, scratch=(), scalars=()):
    return pl.pallas_call(
        kernel,
        in_specs=[smem] * len(scalars) + [vmem] * len(operands),
        out_specs=[vmem] * len(outs),
        out_shape=[pltpu.VMEM(shape, dtype) for shape, dtype in outs],
        scratch_shapes=list(scratch),
        compiler_params=pltpu.CompilerParams(vmem_limit_bytes=mebibytes << 20),
        cost_estimate=pl.CostEstimate(flops=1, bytes_accessed=1, transcendentals=0),
        name=name,
    )(*scalars, *[pltpu.with_memory_space_constraint(x, pltpu.VMEM) for x in operands])


def encode_kernel(
    tile, me, place, scale, xq, xp, w_in, w_out, owner, mask, served,
    send_q, send_p, own_q, own_p, pre_act, slots_out, served_out, scale_out, w_in_kept, w_out_kept,
    states, total, owner_held, mask_held, served_held, sems,
):
    rows = xq.shape[0]
    tiles = w_in.shape[1] // tile
    copies = [
        pltpu.make_async_copy(xq, states.at[:rows, :], sems.at[0]),
        pltpu.make_async_copy(xp, states.at[rows:, :], sems.at[1]),
        pltpu.make_async_copy(owner, owner_held, sems.at[2]),
        pltpu.make_async_copy(mask, mask_held, sems.at[3]),
        pltpu.make_async_copy(served, served_held, sems.at[4]),
    ]
    for t in range(tiles):
        at = slice(t * tile, (t + 1) * tile)
        copies.append(pltpu.make_async_copy(w_in.at[:, at], w_in_kept.at[:, at], sems.at[5 + 2 * t]))
        copies.append(pltpu.make_async_copy(w_out.at[at, :], w_out_kept.at[at, :], sems.at[6 + 2 * t]))
    for copy in copies:
        copy.start()
    for copy in copies[2:5]:
        copy.wait()
    owners = slots_out.shape[0]
    down = lax.broadcasted_iota(jnp.int32, (owners, rows), 0)
    named = jnp.zeros((owners, rows), f32)
    live = jnp.zeros((owners, rows), f32)
    for j in range(owner.shape[0]):
        hit = (owner_held[j : j + 1, :] == down).astype(f32)
        named = named + hit
        live = live + hit * mask_held[j : j + 1, :].astype(f32)
    earlier = lax.broadcasted_iota(jnp.int32, (rows, rows), 0) < lax.broadcasted_iota(
        jnp.int32, (rows, rows), 1
    )
    slot = jnp.dot(named.astype(bf16), earlier.astype(f32).astype(bf16), preferred_element_type=f32)
    slots_out[...] = jnp.where(live > 0.5, slot, -1.0).astype(bf16)
    served_out[...] = served_held[0].astype(f32).astype(bf16)
    scale_out[...] = jnp.zeros_like(scale_out) + scale[0] * logit_scale
    copies[0].wait()
    copies[1].wait()
    for t in range(tiles):
        at = slice(t * tile, (t + 1) * tile)
        copies[5 + 2 * t].wait()
        pre = jnp.dot(states[...], w_in_kept[:, at], preferred_element_type=f32)
        cdf = 0.5 * (1.0 + lax.erf(pre * root_half))
        pre_act[:, at] = pre
        hidden = (pre * cdf).astype(bf16)
        copies[6 + 2 * t].wait()
        part = jnp.dot(hidden, w_out_kept[at, :], preferred_element_type=f32)
        if t == 0:
            total[...] = part
        else:
            total[...] += part
    first = me[0] == 0
    for at, send, own in ((0, send_q, own_q), (rows, send_p, own_p)):
        mine, theirs = halves(first, total[at : at + rows, :])
        send[...] = theirs.astype(bf16)
        own[...] = mine + halves(first, states[at : at + rows, :].astype(f32))[0]


def encode_both(me, place, scale, xq, xp, w_in, w_out, owner, mask, served):
    rows, width = xq.shape
    hidden = w_in.shape[1]
    tile = min(512, hidden)
    owners = served.shape[1]
    half = (rows, width // 2)
    operands = (xq, xp, w_in, w_out, owner.T, mask.T, served)
    return pl.pallas_call(
        functools.partial(encode_kernel, tile),
        in_specs=[smem] * 3 + [hbm] * 7,
        out_specs=[vmem] * 10,
        out_shape=[
            pltpu.VMEM(half, bf16),
            pltpu.VMEM(half, bf16),
            pltpu.VMEM(half, f32),
            pltpu.VMEM(half, f32),
            pltpu.VMEM((2 * rows, hidden), f32),
            pltpu.VMEM((owners, rows), bf16),
            pltpu.VMEM((owners, served.shape[2]), bf16),
            pltpu.VMEM((8, rows), f32),
            pltpu.VMEM(w_in.shape, bf16),
            pltpu.VMEM(w_out.shape, bf16),
        ],
        scratch_shapes=[
            pltpu.VMEM((2 * rows, width), bf16),
            pltpu.VMEM((2 * rows, width), f32),
            pltpu.VMEM(owner.T.shape, jnp.int32),
            pltpu.VMEM(mask.T.shape, jnp.int32),
            pltpu.VMEM(served.shape, jnp.int32),
            pltpu.SemaphoreType.DMA((5 + 2 * (hidden // tile),)),
        ],
        compiler_params=pltpu.CompilerParams(vmem_limit_bytes=8 << 20),
        name="encode_both",
    )(me, place, scale, *[pltpu.with_memory_space_constraint(x, pltpu.HBM) for x in operands])


def slope_kernel(pre_act, slope):
    step = 32

    def body(n, carry):
        at = pl.ds(pl.multiple_of(n * step, step), step)
        slope[at, :] = gelu_slope(pre_act[at, :]).astype(bf16)
        return carry

    lax.fori_loop(0, pre_act.shape[0] // step, body, 0)


def pack_kernel(own, other, numbers, out):
    rows = own.shape[0]
    out[:rows, :] = (own[...] + other[...].astype(f32)).astype(bf16)
    out[rows:, :] = jnp.zeros((out.shape[0] - rows, out.shape[1]), bf16)
    out[rows:, : numbers.shape[1]] = numbers[...]


def pack(own, other, numbers):
    shape = (own.shape[0] + numbers.shape[0], own.shape[1])
    return local(pack_kernel, "pack", [(shape, bf16)], (own, other, numbers))[0]


def score_kernel(owners, rows, place, *refs):
    nq, npass = len(query_at), len(pass_at)
    q_refs, p_refs = refs[:nq], refs[nq : nq + npass]
    table, valid, pick, q_all, p_all, slots, served = refs[nq + npass :]
    for n, ref in enumerate(q_refs):
        q_all[n * rows : (n + 1) * rows, :] = ref[:rows, :]
        slots[n * owners : (n + 1) * owners, :] = ref[rows:, :rows].astype(f32)
    for n, ref in enumerate(p_refs):
        p_all[n * rows : (n + 1) * rows, :] = ref[:rows, :]
        served[n * owners : (n + 1) * owners, :] = ref[rows:, :rows].astype(f32)
    table[...] = jnp.zeros_like(table)
    eye = eye_of(rows)
    down = lax.broadcasted_iota(jnp.int32, (rows, rows), 0).astype(f32)
    queries = q_all[...]
    for b in range(nq):
        block = q_all[b * rows : (b + 1) * rows, :].astype(f32)
        square = jnp.sum(block * block, axis=1, keepdims=True)
        table[2 * npass : 2 * npass + 1, b * rows : (b + 1) * rows] = jnp.sum(
            eye * square, axis=0, keepdims=True
        )
    for a in range(npass):
        part = p_all[a * rows : (a + 1) * rows, :]
        block = part.astype(f32)
        square = jnp.sum(block * block, axis=1, keepdims=True)
        table[2 * npass + 2 : 2 * npass + 3, a * rows : (a + 1) * rows] = jnp.sum(
            eye * square, axis=0, keepdims=True
        )
        scores = lax.dot_general(part, queries, nt, preferred_element_type=f32)
        if a == 0:
            table[2 * npass + 1 : 2 * npass + 2, :rows] = jnp.sum(
                eye * scores[:, :rows], axis=0, keepdims=True
            )
        for b in range(nq):
            lanes = slice(b * rows, (b + 1) * rows)
            row_of = served[pl.ds(a * owners + (place[0] ^ query_at[b]), 1), :]
            slot_of = slots[pl.ds(b * owners + (place[0] ^ pass_at[a]), 1), :]
            by_slot = (down == row_of).astype(f32).astype(bf16)
            by_query = (down == slot_of).astype(f32).astype(bf16)
            chosen = jnp.dot(by_slot, by_query, preferred_element_type=f32)
            table[a : a + 1, lanes] = jnp.sum(chosen * scores[:, lanes], axis=0, keepdims=True)
            table[npass + a : npass + a + 1, lanes] = jnp.sum(
                chosen * square, axis=0, keepdims=True
            )
            valid[a : a + 1, lanes] = (slot_of >= 0.0).astype(f32)
            pick[a * rows : (a + 1) * rows, lanes] = chosen.astype(bf16)


def score(place, q_blocks, p_blocks, rows, owners):
    nq, npass = len(query_at), len(pass_at)
    width = q_blocks[0].shape[1]
    return local(
        functools.partial(score_kernel, owners, rows),
        "score",
        [
            ((-(-(2 * npass + 3) // 8) * 8, nq * rows), f32),
            ((npass, nq * rows), f32),
            ((npass * rows, nq * rows), bf16),
            ((nq * rows, width), bf16),
            ((npass * rows, width), bf16),
        ],
        (*q_blocks, *p_blocks),
        3,
        [pltpu.VMEM((nq * owners, rows), f32), pltpu.VMEM((npass * owners, rows), f32)],
        [place],
    )


def weigh_kernel(rows, table, other, valid, coefs, sums):
    nq, npass = len(query_at), len(pass_at)
    full = table[...] + other[...]
    raw, square = full[:npass], full[npass : 2 * npass]
    inv_q = lax.rsqrt(full[2 * npass : 2 * npass + 1] + norm_eps)
    inv_pass = lax.rsqrt(full[2 * npass + 2 : 2 * npass + 3] + norm_eps)
    inv_neg = lax.rsqrt(square + norm_eps)
    neg_score = raw * inv_q * inv_neg
    exp_neg = valid[...] * jnp.exp(logit_scale * neg_score)
    pos_score = full[2 * npass + 1 : 2 * npass + 2] * inv_q * inv_pass
    coefs[...] = jnp.zeros_like(coefs)
    coefs[:npass] = exp_neg
    coefs[npass : 2 * npass] = exp_neg * inv_neg
    coefs[2 * npass : 3 * npass] = exp_neg * neg_score
    coefs[3 * npass : 3 * npass + 1] = inv_q
    coefs[3 * npass + 1 : 3 * npass + 2] = inv_pass
    coefs[3 * npass + 2 : 3 * npass + 3] = pos_score
    neg_sum = jnp.sum(exp_neg, axis=0, keepdims=True)
    neg_dot = jnp.sum(exp_neg * neg_score, axis=0, keepdims=True)
    sums[...] = jnp.zeros_like(sums)
    for n in range(nq):
        sums[n : n + 1, :] = neg_sum[:, n * rows : (n + 1) * rows]
        sums[2 * nq + n : 2 * nq + n + 1, :] = neg_dot[:, n * rows : (n + 1) * rows]
    sums[nq : nq + 1, :] = jnp.exp(logit_scale * pos_score[:, :rows])


def weigh(table, other, valid, rows):
    nq, npass = len(query_at), len(pass_at)
    return local(
        functools.partial(weigh_kernel, rows),
        "weigh",
        [((-(-(3 * npass + 3) // 8) * 8, nq * rows), f32), ((-(-3 * nq // 8) * 8, rows), f32)],
        (table, other, valid),
    )


def add_sums_kernel(bit, sums, other, *refs):
    out = refs[-1]
    nq = len(query_at)
    out[...] = sums[...]
    for n, at in enumerate(query_at):
        m = query_at.index(at ^ bit)
        for first in (0, nq, 2 * nq):
            k, l = first + n, first + m
            out[k : k + 1, :] = sums[k : k + 1, :] + other[l : l + 1, :]


def exchange_sums(sums, bit, *after):
    kernel = functools.partial(add_sums_kernel, bit)
    return local(kernel, "add_sums", [(sums.shape, f32)], (sums, swap(sums, "dp", bit), *after))[0]


def spread_query_kernel(rows, coefs, pick, p_all, kept, sent):
    npass = len(pass_at)
    passages = p_all[...]
    near = [b for b, at in enumerate(query_at) if not at & query_bits[0]]
    far = [b for b, at in enumerate(query_at) if at & query_bits[0]]
    for b in near + far:
        lanes = slice(b * rows, (b + 1) * rows)
        pieces = []
        for a in range(npass):
            piece = pick[a * rows : (a + 1) * rows, lanes].astype(f32)
            piece = piece * coefs[npass + a : npass + a + 1, lanes]
            pieces.append(piece.T.astype(bf16))
        weights = jnp.concatenate(pieces, axis=1)
        values = jnp.dot(weights, passages, preferred_element_type=f32)
        out, at = (kept, near.index(b)) if b in near else (sent, far.index(b))
        out[at * rows : (at + 1) * rows, :] = values.astype(out.dtype)


def spread_query(coefs, pick, p_all, rows):
    half = (len(query_at) // 2 * rows, p_all.shape[1])
    return local(
        functools.partial(spread_query_kernel, rows),
        "spread_query",
        [(half, f32), (half, bf16)],
        (coefs, pick, p_all),
        3,
    )


def column_of(eye, row):
    return jnp.sum(eye * row, axis=1, keepdims=True)


def spread_pass_kernel(rows, scale, coefs, sums, pick, q_all, p_all, kept, *sent):
    nq, npass = len(query_at), len(pass_at)
    eye = eye_of(rows)
    share = scale[:nq] / (sums[:nq] + sums[nq : 2 * nq])
    pos = -share[:1] * sums[:1]
    share = jnp.concatenate([share[n : n + 1] for n in range(nq)], axis=1)
    scaled = share * coefs[3 * npass : 3 * npass + 1]
    queries = q_all[...]
    for a in range(npass):
        at = slice(a * rows, (a + 1) * rows)
        chosen = pick[at, :]
        weights = chosen.astype(f32) * (coefs[a : a + 1] * scaled)
        product = share * coefs[2 * npass + a : 2 * npass + a + 1]
        high = product.astype(bf16).astype(f32)
        parts = jnp.concatenate([high, product - high, jnp.zeros((14, nq * rows), f32)], axis=0)
        dots = lax.dot_general(parts.astype(bf16), chosen, nt, preferred_element_type=f32)
        dot = jnp.sum(dots, axis=0, keepdims=True)
        if a == 0:
            own = pos * coefs[3 * npass : 3 * npass + 1, :rows]
            weights = jnp.concatenate([weights[:, :rows] + eye * own, weights[:, rows:]], axis=1)
            dot = dot + pos * coefs[3 * npass + 2 : 3 * npass + 3, :rows]
        values = jnp.dot(weights.astype(bf16), queries, preferred_element_type=f32)
        along = column_of(eye, dot * coefs[3 * npass + 1 : 3 * npass + 2, at])
        values = values - along * p_all[at, :].astype(f32)
        if a < npass // 2:
            kept[at, :] = values
        else:
            sent[a - npass // 2][...] = values.astype(bf16)


def spread_pass(scale, coefs, sums, pick, q_all, p_all, rows):
    half, width = len(pass_at) // 2, q_all.shape[1]
    kept, *sent = local(
        functools.partial(spread_pass_kernel, rows),
        "spread_pass",
        [((half * rows, width), f32)] + [((rows, width), bf16)] * half,
        (scale, coefs, sums, pick, q_all, p_all),
        3,
    )
    return kept, sent


def fold_pass_kernel(own, first, second, kept, sent):
    rows = kept.shape[0]
    kept[...] = own[:rows, :] + first[...].astype(f32)
    sent[...] = (own[rows:, :] + second[...].astype(f32)).astype(bf16)


def fold_pass(own, first, second):
    half = (own.shape[0] // 2, own.shape[1])
    return local(fold_pass_kernel, "fold_pass", [(half, f32), (half, bf16)], (own, first, second))


def fold_query_kernel(own, other, kept, sent):
    rows = kept.shape[0]
    total = own[...] + other[...].astype(f32)
    kept[...] = total[:rows]
    sent[...] = total[rows:].astype(bf16)


def fold_query(own, other):
    half = (own.shape[0] // 2, own.shape[1])
    return local(fold_query_kernel, "fold_query", [(half, f32), (half, bf16)], (own, other))


def add_kernel(own, other, out):
    out[...] = (own[...] + other[...].astype(f32)).astype(out.dtype)


def grad_query_kernel(own, other, scale, sums, coefs, raw, raw_pass, grad, rounded):
    nq, npass = len(query_at), len(pass_at)
    rows = own.shape[0]
    eye = eye_of(rows)
    inv_norm = coefs[3 * npass : 3 * npass + 1, :rows]
    share = scale[:1] / (sums[:1] + sums[nq : nq + 1])
    pos = sums[:1] * coefs[3 * npass + 1 : 3 * npass + 2, :rows]
    dot = share * (sums[2 * nq : 2 * nq + 1] - sums[:1] * coefs[3 * npass + 2 : 3 * npass + 3, :rows])
    total = own[...] + other[...].astype(f32)
    total = total - column_of(eye, pos) * raw_pass[:rows, :].astype(f32)
    values = column_of(eye, share * inv_norm) * total
    values = values - column_of(eye, dot * inv_norm * inv_norm) * raw[:rows, :].astype(f32)
    grad[...] = values
    rounded[...] = values.astype(bf16)


def grad_pass_kernel(own, other, coefs, after, grad, rounded):
    npass = len(pass_at)
    rows = own.shape[0]
    inv_norm = column_of(eye_of(rows), coefs[3 * npass + 1 : 3 * npass + 2, :rows])
    values = inv_norm * (own[...] + other[...].astype(f32))
    grad[...] = values
    rounded[...] = values.astype(bf16)


def grad_out(kernel, name, own, operands):
    return local(kernel, name, [(own.shape, f32), (own.shape, bf16)], (own, *operands))


def decode_kernel(tower, tile, me, grad, mine, theirs, slope, w_in, w_out, *refs):
    send, own, total = refs[-3:]
    first = me[0] == 0
    rows = grad.shape[0]
    mine, theirs = mine[...], theirs[...]
    rounded = jnp.concatenate(
        [jnp.where(first, mine, theirs), jnp.where(first, theirs, mine)], axis=1
    )
    for t in range(w_in.shape[1] // tile):
        at = slice(t * tile, (t + 1) * tile)
        hidden = lax.dot_general(rounded, w_out[at, :], nt, preferred_element_type=f32)
        grad_pre = (hidden * slope[tower * rows : (tower + 1) * rows, at].astype(f32)).astype(bf16)
        part = lax.dot_general(grad_pre, w_in[:, at], nt, preferred_element_type=f32)
        if t == 0:
            total[...] = part
        else:
            total[...] += part
    mine, theirs = halves(first, total[...])
    send[...] = theirs.astype(bf16)
    own[...] = grad[...] + mine


def decode_one(me, grad, rounded, slope, tower, w_in, w_out, *after):
    rows, width = grad.shape[0], w_in.shape[0]
    return local(
        functools.partial(decode_kernel, tower, min(512, w_in.shape[1])),
        "decode_one",
        [(grad.shape, bf16), (grad.shape, f32)],
        (grad, rounded, swap(rounded, "mp", 1), slope, w_in, w_out, *after),
        3,
        [pltpu.VMEM((rows, width), f32)],
        [me],
    )


def finish(own, other, name):
    return pl.pallas_call(
        add_kernel,
        in_specs=[vmem] * 2,
        out_specs=vmem,
        out_shape=jax.ShapeDtypeStruct(own.shape, bf16),
        compiler_params=pltpu.CompilerParams(vmem_limit_bytes=1 << 20),
        name=name,
    )(*[pltpu.with_memory_space_constraint(x, pltpu.VMEM) for x in (own, other)])


def paired_shards(
    query_states, passage_states, w_in, w_out, neg_owner, neg_mask, served_rows, loss_scale
):
    rows = query_states.shape[0]
    owners = served_rows.shape[1]
    me = lax.axis_index("mp").astype(jnp.int32).reshape(1)
    place = lax.axis_index("dp").astype(jnp.int32).reshape(1)
    send_q, send_p, own_q, own_p, pre_act, slots, served, scale, w_in, w_out = encode_both(
        me, place, loss_scale.reshape(1), query_states, passage_states, w_in, w_out, neg_owner, neg_mask, served_rows
    )
    slope = local(slope_kernel, "slope", [(pre_act.shape, bf16)], (pre_act,))[0]
    raw_q = pack(own_q, swap(send_q, "mp", 1), slots)
    raw_p = pack(own_p, swap(send_p, "mp", 1), served)
    p_blocks = gather_blocks(raw_p, pass_bits)
    q_blocks = gather_blocks(raw_q, query_bits)

    table, valid, pick, q_all, p_all = score(place, q_blocks, p_blocks, rows, owners)
    coefs, sums = weigh(table, swap(table, "mp", 1), valid, rows)
    kept_q, sent_q = spread_query(coefs, pick, p_all, rows)
    sums = exchange_sums(sums, query_bits[1], sent_q)
    sums = exchange_sums(sums, query_bits[0])
    kept_p, sent_p = spread_pass(scale, coefs, sums, pick, q_all, p_all, rows)
    kept_p, sent_p = fold_pass(kept_p, *[swap(x, "dp", pass_bits[1]) for x in sent_p])
    kept_q, sent_q = fold_query(kept_q, swap(sent_q, "dp", query_bits[0]))
    grad_q, round_q = grad_out(
        grad_query_kernel,
        "grad_query",
        kept_q,
        (swap(sent_q, "dp", query_bits[1]), scale, sums, coefs, raw_q, raw_p),
    )
    grad_p, round_p = grad_out(
        grad_pass_kernel,
        "grad_pass",
        kept_p,
        (swap(sent_p, "dp", pass_bits[0]), coefs, round_q),
    )
    send_q, own_q = decode_one(me, grad_q, round_q, slope, 0, w_in, w_out)
    send_p, own_p = decode_one(me, grad_p, round_p, slope, 1, w_in, w_out, send_q)
    return (
        finish(own_q, swap(send_q, "mp", 1), "out_query"),
        finish(own_p, swap(send_p, "mp", 1), "out_pass"),
    )


def solution(mesh):
    in_specs = (
        P("dp", None),
        P("dp", None),
        P(None, "mp"),
        P("mp", None),
        P("dp", None),
        P("dp", None),
        P("dp", None, None),
        P(),
    )
    out_specs = (P("dp", "mp"), P("dp", "mp"))
    gathered = len(query_at) * len(pass_at)
    paired = mesh.shape["mp"] == 2 and mesh.shape["dp"] == gathered
    shards = paired_shards if paired else general_shards
    return jax.shard_map(shards, mesh=mesh, in_specs=in_specs, out_specs=out_specs, check_vma=False)
```

```python
import functools

import jax
import jax.numpy as jnp
from jax import lax
from jax.experimental import pallas as pl
from jax.experimental.pallas import tpu as pltpu
from jax.sharding import PartitionSpec as P

logit_scale = 50.0
norm_eps = 1e-06
root_half = 0.7071067811865476
inv_root_two_pi = 0.3989422804014327
f32, bf16 = jnp.float32, jnp.bfloat16
nt = (((1,), (1,)), ((), ()))
tn = (((0,), (0,)), ((), ()))
vmem = pl.BlockSpec(memory_space=pltpu.VMEM)
smem = pl.BlockSpec(memory_space=pltpu.SMEM)
hbm = pl.BlockSpec(memory_space=pltpu.HBM)


def gelu_value(values):
    return 0.5 * values * (1.0 + lax.erf(values * root_half))


def gelu_slope(values):
    return (
        0.5 * (1.0 + lax.erf(values * root_half))
        + values * jnp.exp(-0.5 * values * values) * inv_root_two_pi
    )


def own_columns(values):
    column_width = values.shape[1] // lax.axis_size("mp")
    return lax.dynamic_slice_in_dim(values, lax.axis_index("mp") * column_width, column_width, 1)


def encode(states, w_in, w_out):
    pre_act = jnp.dot(states, w_in, preferred_element_type=jnp.float32)
    hidden = gelu_value(pre_act).astype(jnp.bfloat16)
    partial_out = jnp.dot(hidden, w_out, preferred_element_type=jnp.float32)
    mixed_sum = lax.psum(partial_out, "mp")
    output = states.astype(jnp.float32) + mixed_sum
    inv_norm = lax.rsqrt(jnp.sum(output * output, axis=1, keepdims=True) + norm_eps)
    return (pre_act, output * inv_norm, inv_norm)


def decode(grad_part, pre_act, unit_rows, inv_norm, w_in, w_out):
    grad_emb = lax.all_gather(grad_part.astype(jnp.bfloat16), "mp", axis=1, tiled=True).astype(
        grad_part.dtype
    )
    grad_out = inv_norm * (
        grad_emb - unit_rows * jnp.sum(unit_rows * grad_emb, axis=1, keepdims=True)
    )
    grad_hidden = lax.dot_general(
        grad_out.astype(jnp.bfloat16), w_out, nt, preferred_element_type=jnp.float32
    )
    grad_pre = (grad_hidden * gelu_slope(pre_act)).astype(jnp.bfloat16)
    partial_in = lax.dot_general(grad_pre, w_in, nt, preferred_element_type=jnp.float32)
    summed = lax.psum_scatter(
        partial_in.astype(jnp.bfloat16), "mp", scatter_dimension=1, tiled=True
    ).astype(jnp.float32)
    return (summed + own_columns(grad_out)).astype(jnp.bfloat16)


def general_shards(
    query_states, passage_states, w_in, w_out, neg_owner, neg_mask, served_rows, loss_scale
):
    owners = lax.axis_size("dp")
    row_count = query_states.shape[0]
    negatives = neg_owner.shape[1]
    capacity = served_rows.shape[2]
    pre_pass, unit_pass, inv_pass = encode(passage_states, w_in, w_out)
    emb_pass = own_columns(unit_pass).astype(jnp.bfloat16)
    column_width = emb_pass.shape[1]
    served = served_rows[0]
    flat_owner = neg_owner.reshape(-1)
    onehot = (flat_owner[:, None] == jnp.arange(owners, dtype=jnp.int32)[None, :]).astype(jnp.int32)
    before = jnp.cumsum(onehot, axis=0, dtype=jnp.int32) - onehot
    slot_index = jnp.sum(before * onehot, axis=1, dtype=jnp.int32)
    slot_place = flat_owner * capacity + slot_index
    every_emb = lax.all_gather(emb_pass, "dp", axis=0, tiled=True)
    rows_for_me = lax.all_to_all(
        served_rows, "dp", split_axis=1, concat_axis=0, tiled=True
    ).reshape(owners * capacity)
    neg_rows = jnp.take(rows_for_me, slot_place, axis=0)
    neg_emb = jnp.take(every_emb, flat_owner * row_count + neg_rows, axis=0)
    neg_emb = neg_emb.reshape(row_count, negatives, column_width)
    pre_query, unit_query, inv_query = encode(query_states, w_in, w_out)
    emb_query = own_columns(unit_query).astype(jnp.bfloat16)
    pos_part = jnp.einsum("qd,qd->q", emb_query, emb_pass, preferred_element_type=jnp.float32)
    neg_part = jnp.einsum("qd,qnd->qn", emb_query, neg_emb, preferred_element_type=jnp.float32)
    pos_score, neg_score = lax.psum((pos_part, neg_part), "mp")
    exp_pos = jnp.exp(logit_scale * pos_score)
    exp_neg = neg_mask.astype(jnp.float32) * jnp.exp(logit_scale * neg_score)
    denominator = exp_pos + jnp.sum(exp_neg, axis=1)
    factor = loss_scale * logit_scale
    grad_pos = factor * (exp_pos / denominator - 1.0)
    grad_neg = factor * exp_neg / denominator[:, None]
    query_values = emb_query.astype(jnp.float32)
    grad_query_emb = grad_pos[:, None] * emb_pass.astype(jnp.float32) + jnp.sum(
        grad_neg[:, :, None] * neg_emb.astype(jnp.float32), axis=1
    )
    slot_terms = (
        (grad_neg[:, :, None] * query_values[:, None, :])
        .astype(jnp.bfloat16)
        .reshape(-1, column_width)
    )
    outgoing_grad = (
        jnp.zeros((owners * capacity, column_width), jnp.bfloat16).at[slot_place].set(slot_terms)
    )
    returned = lax.all_to_all(
        outgoing_grad.reshape(owners, capacity, column_width),
        "dp",
        split_axis=0,
        concat_axis=0,
        tiled=True,
    )
    grad_query_states = decode(grad_query_emb, pre_query, unit_query, inv_query, w_in, w_out)
    gathered_back = (
        jnp.zeros((row_count, column_width), jnp.float32)
        .at[served.reshape(-1)]
        .add(returned.reshape(-1, column_width).astype(jnp.float32))
    )
    grad_pass_emb = grad_pos[:, None] * query_values + gathered_back
    grad_passage_states = decode(grad_pass_emb, pre_pass, unit_pass, inv_pass, w_in, w_out)
    return (grad_query_states, grad_passage_states)


query_bits, pass_bits = (8, 1), (4, 2)


def offsets(bits):
    found = [0]
    for bit in bits:
        found = found + [at | bit for at in found]
    return found


query_at, pass_at = offsets(query_bits), offsets(pass_bits)


def swap(values, axis, bit):
    size = lax.axis_size(axis)
    return lax.ppermute(values, axis, [(i, i ^ bit) for i in range(size)])


def gather_blocks(block, bits):
    blocks = [block]
    for bit in bits:
        blocks = blocks + [swap(values, "dp", bit) for values in blocks]
    return blocks


def halves(first, values):
    width = values.shape[1] // 2
    left, right = values[:, :width], values[:, width:]
    return jnp.where(first, left, right), jnp.where(first, right, left)


def eye_of(size):
    return (
        lax.broadcasted_iota(jnp.int32, (size, size), 0)
        == lax.broadcasted_iota(jnp.int32, (size, size), 1)
    ).astype(f32)


def local(kernel, name, outs, operands, mebibytes=1, scratch=(), scalars=()):
    return pl.pallas_call(
        kernel,
        in_specs=[smem] * len(scalars) + [vmem] * len(operands),
        out_specs=[vmem] * len(outs),
        out_shape=[pltpu.VMEM(shape, dtype) for shape, dtype in outs],
        scratch_shapes=list(scratch),
        compiler_params=pltpu.CompilerParams(vmem_limit_bytes=mebibytes << 20),
        cost_estimate=pl.CostEstimate(flops=1, bytes_accessed=1, transcendentals=0),
        name=name,
    )(*scalars, *[pltpu.with_memory_space_constraint(x, pltpu.VMEM) for x in operands])


def encode_kernel(
    tile, me, place, scale, xq, xp, w_in, w_out, owner, mask, served,
    send_q, send_p, own_q, own_p, pre_act, slots_out, served_out, scale_out, w_in_kept, w_out_kept,
    states, hidden, total, owner_held, mask_held, served_held, sems,
):
    rows = xq.shape[0]
    tiles = w_in.shape[1] // tile
    copies = [
        pltpu.make_async_copy(xq, states.at[:rows, :], sems.at[0]),
        pltpu.make_async_copy(xp, states.at[rows:, :], sems.at[1]),
        pltpu.make_async_copy(owner, owner_held, sems.at[2]),
        pltpu.make_async_copy(mask, mask_held, sems.at[3]),
        pltpu.make_async_copy(served, served_held, sems.at[4]),
    ]
    for t in range(tiles):
        at = slice(t * tile, (t + 1) * tile)
        copies.append(pltpu.make_async_copy(w_in.at[:, at], w_in_kept.at[:, at], sems.at[5 + t]))
    for t in range(tiles):
        at = slice(t * tile, (t + 1) * tile)
        copies.append(
            pltpu.make_async_copy(w_out.at[at, :], w_out_kept.at[at, :], sems.at[5 + tiles + t])
        )
    for copy in copies:
        copy.start()
    for copy in copies[2:5]:
        copy.wait()
    owners = slots_out.shape[0]
    down = lax.broadcasted_iota(jnp.int32, (owners, rows), 0)
    named = jnp.zeros((owners, rows), f32)
    live = jnp.zeros((owners, rows), f32)
    for j in range(owner.shape[0]):
        hit = (owner_held[j : j + 1, :] == down).astype(f32)
        named = named + hit
        live = live + hit * mask_held[j : j + 1, :].astype(f32)
    earlier = lax.broadcasted_iota(jnp.int32, (rows, rows), 0) < lax.broadcasted_iota(
        jnp.int32, (rows, rows), 1
    )
    slot = jnp.dot(named.astype(bf16), earlier.astype(f32).astype(bf16), preferred_element_type=f32)
    slots_out[...] = jnp.where(live > 0.5, slot, -1.0).astype(bf16)
    served_out[...] = served_held[0].astype(f32).astype(bf16)
    scale_out[...] = jnp.zeros_like(scale_out) + scale[0] * logit_scale
    copies[0].wait()
    copies[1].wait()
    for t in range(tiles):
        at = slice(t * tile, (t + 1) * tile)
        copies[5 + t].wait()
        pre = jnp.dot(states[...], w_in_kept[:, at], preferred_element_type=f32)
        cdf = 0.5 * (1.0 + lax.erf(pre * root_half))
        pre_act[:, at] = pre
        hidden[:, at] = (pre * cdf).astype(bf16)
    for t in range(tiles):
        at = slice(t * tile, (t + 1) * tile)
        copies[5 + tiles + t].wait()
        part = jnp.dot(hidden[:, at], w_out_kept[at, :], preferred_element_type=f32)
        if t == 0:
            total[...] = part
        else:
            total[...] += part
    first = me[0] == 0
    for at, send, own in ((0, send_q, own_q), (rows, send_p, own_p)):
        mine, theirs = halves(first, total[at : at + rows, :])
        send[...] = theirs.astype(bf16)
        own[...] = mine + halves(first, states[at : at + rows, :].astype(f32))[0]


def encode_both(me, place, scale, xq, xp, w_in, w_out, owner, mask, served):
    rows, width = xq.shape
    hidden = w_in.shape[1]
    tile = min(512, hidden)
    owners = served.shape[1]
    half = (rows, width // 2)
    operands = (xq, xp, w_in, w_out, owner.T, mask.T, served)
    return pl.pallas_call(
        functools.partial(encode_kernel, tile),
        in_specs=[smem] * 3 + [hbm] * 7,
        out_specs=[vmem] * 10,
        out_shape=[
            pltpu.VMEM(half, bf16),
            pltpu.VMEM(half, bf16),
            pltpu.VMEM(half, f32),
            pltpu.VMEM(half, f32),
            pltpu.VMEM((2 * rows, hidden), f32),
            pltpu.VMEM((owners, rows), bf16),
            pltpu.VMEM((owners, served.shape[2]), bf16),
            pltpu.VMEM((8, rows), f32),
            pltpu.VMEM(w_in.shape, bf16),
            pltpu.VMEM(w_out.shape, bf16),
        ],
        scratch_shapes=[
            pltpu.VMEM((2 * rows, width), bf16),
            pltpu.VMEM((2 * rows, hidden), bf16),
            pltpu.VMEM((2 * rows, width), f32),
            pltpu.VMEM(owner.T.shape, jnp.int32),
            pltpu.VMEM(mask.T.shape, jnp.int32),
            pltpu.VMEM(served.shape, jnp.int32),
            pltpu.SemaphoreType.DMA((5 + 2 * (hidden // tile),)),
        ],
        compiler_params=pltpu.CompilerParams(vmem_limit_bytes=8 << 20),
        name="encode_both",
    )(me, place, scale, *[pltpu.with_memory_space_constraint(x, pltpu.HBM) for x in operands])


def slope_kernel(pre_act, slope):
    step = 32

    def body(n, carry):
        at = pl.ds(pl.multiple_of(n * step, step), step)
        slope[at, :] = gelu_slope(pre_act[at, :]).astype(bf16)
        return carry

    lax.fori_loop(0, pre_act.shape[0] // step, body, 0)


def flip_kernel(weights, out):
    rows, columns = weights.shape
    size = 256
    eye = eye_of(size).astype(bf16)
    for i in range(0, rows, size):
        for j in range(0, columns, size):
            out[j : j + size, i : i + size] = lax.dot_general(
                eye, weights[i : i + size, j : j + size], nt, preferred_element_type=f32
            ).astype(bf16)


def flip(weights, name):
    return local(flip_kernel, name, [(weights.shape[::-1], bf16)], (weights,), 2)[0]


def pack_kernel(own, other, numbers, *refs):
    out = refs[-1]
    rows = own.shape[0]
    out[:rows, :] = (own[...] + other[...].astype(f32)).astype(bf16)
    out[rows:, :] = jnp.zeros((out.shape[0] - rows, out.shape[1]), bf16)
    out[rows:, : numbers.shape[1]] = numbers[...]


def pack(own, other, numbers, *after):
    shape = (own.shape[0] + numbers.shape[0], own.shape[1])
    return local(pack_kernel, "pack", [(shape, bf16)], (own, other, numbers, *after))[0]


def score_kernel(owners, rows, place, *refs):
    nq, npass = len(query_at), len(pass_at)
    q_refs, p_refs = refs[:nq], refs[nq : nq + npass]
    table, valid, pick, q_all, p_all, slots, served = refs[nq + npass :]
    for n, ref in enumerate(q_refs):
        q_all[n * rows : (n + 1) * rows, :] = ref[:rows, :]
        slots[n * owners : (n + 1) * owners, :] = ref[rows:, :rows].astype(f32)
    for n, ref in enumerate(p_refs):
        p_all[n * rows : (n + 1) * rows, :] = ref[:rows, :]
        served[n * owners : (n + 1) * owners, :] = ref[rows:, :rows].astype(f32)
    table[...] = jnp.zeros_like(table)
    eye = eye_of(rows)
    down = lax.broadcasted_iota(jnp.int32, (rows, rows), 0).astype(f32)
    queries = q_all[...]
    for b in range(nq):
        block = q_all[b * rows : (b + 1) * rows, :].astype(f32)
        square = jnp.sum(block * block, axis=1, keepdims=True)
        table[2 * npass : 2 * npass + 1, b * rows : (b + 1) * rows] = jnp.sum(
            eye * square, axis=0, keepdims=True
        )
    for a in range(npass):
        part = p_all[a * rows : (a + 1) * rows, :]
        block = part.astype(f32)
        square = jnp.sum(block * block, axis=1, keepdims=True)
        table[2 * npass + 2 : 2 * npass + 3, a * rows : (a + 1) * rows] = jnp.sum(
            eye * square, axis=0, keepdims=True
        )
        scores = lax.dot_general(part, queries, nt, preferred_element_type=f32)
        if a == 0:
            table[2 * npass + 1 : 2 * npass + 2, :rows] = jnp.sum(
                eye * scores[:, :rows], axis=0, keepdims=True
            )
        for b in range(nq):
            lanes = slice(b * rows, (b + 1) * rows)
            row_of = served[pl.ds(a * owners + (place[0] ^ query_at[b]), 1), :]
            slot_of = slots[pl.ds(b * owners + (place[0] ^ pass_at[a]), 1), :]
            by_slot = (down == row_of).astype(f32).astype(bf16)
            by_query = (down == slot_of).astype(f32).astype(bf16)
            chosen = jnp.dot(by_slot, by_query, preferred_element_type=f32)
            table[a : a + 1, lanes] = jnp.sum(chosen * scores[:, lanes], axis=0, keepdims=True)
            table[npass + a : npass + a + 1, lanes] = jnp.sum(
                chosen * square, axis=0, keepdims=True
            )
            valid[a : a + 1, lanes] = (slot_of >= 0.0).astype(f32)
            pick[a * rows : (a + 1) * rows, lanes] = chosen.astype(bf16)


def score(place, q_blocks, p_blocks, rows, owners):
    nq, npass = len(query_at), len(pass_at)
    width = q_blocks[0].shape[1]
    return local(
        functools.partial(score_kernel, owners, rows),
        "score",
        [
            ((-(-(2 * npass + 3) // 8) * 8, nq * rows), f32),
            ((npass, nq * rows), f32),
            ((npass * rows, nq * rows), bf16),
            ((nq * rows, width), bf16),
            ((npass * rows, width), bf16),
        ],
        (*q_blocks, *p_blocks),
        3,
        [pltpu.VMEM((nq * owners, rows), f32), pltpu.VMEM((npass * owners, rows), f32)],
        [place],
    )


def weigh_kernel(rows, table, other, valid, coefs, sums):
    nq, npass = len(query_at), len(pass_at)
    full = table[...] + other[...]
    raw, square = full[:npass], full[npass : 2 * npass]
    inv_q = lax.rsqrt(full[2 * npass : 2 * npass + 1] + norm_eps)
    inv_pass = lax.rsqrt(full[2 * npass + 2 : 2 * npass + 3] + norm_eps)
    inv_neg = lax.rsqrt(square + norm_eps)
    neg_score = raw * inv_q * inv_neg
    exp_neg = valid[...] * jnp.exp(logit_scale * neg_score)
    pos_score = full[2 * npass + 1 : 2 * npass + 2] * inv_q * inv_pass
    coefs[...] = jnp.zeros_like(coefs)
    coefs[:npass] = exp_neg
    coefs[npass : 2 * npass] = exp_neg * inv_neg
    coefs[2 * npass : 3 * npass] = exp_neg * neg_score
    coefs[3 * npass : 3 * npass + 1] = inv_q
    coefs[3 * npass + 1 : 3 * npass + 2] = inv_pass
    coefs[3 * npass + 2 : 3 * npass + 3] = pos_score
    neg_sum = jnp.sum(exp_neg, axis=0, keepdims=True)
    neg_dot = jnp.sum(exp_neg * neg_score, axis=0, keepdims=True)
    sums[...] = jnp.zeros_like(sums)
    for n in range(nq):
        sums[n : n + 1, :] = neg_sum[:, n * rows : (n + 1) * rows]
        sums[2 * nq + n : 2 * nq + n + 1, :] = neg_dot[:, n * rows : (n + 1) * rows]
    sums[nq : nq + 1, :] = jnp.exp(logit_scale * pos_score[:, :rows])


def weigh(table, other, valid, rows):
    nq, npass = len(query_at), len(pass_at)
    return local(
        functools.partial(weigh_kernel, rows),
        "weigh",
        [((-(-(3 * npass + 3) // 8) * 8, nq * rows), f32), ((-(-3 * nq // 8) * 8, rows), f32)],
        (table, other, valid),
    )


def add_sums_kernel(bit, sums, other, *refs):
    out = refs[-1]
    nq = len(query_at)
    out[...] = sums[...]
    for n, at in enumerate(query_at):
        m = query_at.index(at ^ bit)
        for first in (0, nq, 2 * nq):
            k, l = first + n, first + m
            out[k : k + 1, :] = sums[k : k + 1, :] + other[l : l + 1, :]


def exchange_sums(sums, bit, *after):
    kernel = functools.partial(add_sums_kernel, bit)
    return local(kernel, "add_sums", [(sums.shape, f32)], (sums, swap(sums, "dp", bit), *after))[0]


def spread_query_kernel(rows, coefs, pick, p_all, kept, sent):
    npass = len(pass_at)
    passages = p_all[...]
    near = [b for b, at in enumerate(query_at) if not at & query_bits[1]]
    far = [b for b, at in enumerate(query_at) if at & query_bits[1]]
    for b in near + far:
        lanes = slice(b * rows, (b + 1) * rows)
        pieces = []
        for a in range(npass):
            piece = pick[a * rows : (a + 1) * rows, lanes].astype(f32)
            piece = piece * coefs[npass + a : npass + a + 1, lanes]
            pieces.append(piece.T.astype(bf16))
        weights = jnp.concatenate(pieces, axis=1)
        values = jnp.dot(weights, passages, preferred_element_type=f32)
        out, at = (kept, near.index(b)) if b in near else (sent, far.index(b))
        out[at * rows : (at + 1) * rows, :] = values.astype(out.dtype)


def spread_query(coefs, pick, p_all, rows):
    half = (len(query_at) // 2 * rows, p_all.shape[1])
    return local(
        functools.partial(spread_query_kernel, rows),
        "spread_query",
        [(half, f32), (half, bf16)],
        (coefs, pick, p_all),
        3,
    )


def column_of(eye, row):
    return jnp.sum(eye * row, axis=1, keepdims=True)


def spread_pass_kernel(rows, scale, coefs, sums, pick, q_all, p_all, kept, *sent):
    nq, npass = len(query_at), len(pass_at)
    eye = eye_of(rows)
    share = scale[:nq] / (sums[:nq] + sums[nq : 2 * nq])
    pos = -share[:1] * sums[:1]
    share = jnp.concatenate([share[n : n + 1] for n in range(nq)], axis=1)
    scaled = share * coefs[3 * npass : 3 * npass + 1]
    queries = q_all[...]
    for a in range(npass):
        at = slice(a * rows, (a + 1) * rows)
        chosen = pick[at, :]
        weights = chosen.astype(f32) * (coefs[a : a + 1] * scaled)
        product = share * coefs[2 * npass + a : 2 * npass + a + 1]
        high = product.astype(bf16).astype(f32)
        parts = jnp.concatenate([high, product - high, jnp.zeros((14, nq * rows), f32)], axis=0)
        dots = lax.dot_general(parts.astype(bf16), chosen, nt, preferred_element_type=f32)
        dot = jnp.sum(dots, axis=0, keepdims=True)
        if a == 0:
            own = pos * coefs[3 * npass : 3 * npass + 1, :rows]
            weights = jnp.concatenate([weights[:, :rows] + eye * own, weights[:, rows:]], axis=1)
            dot = dot + pos * coefs[3 * npass + 2 : 3 * npass + 3, :rows]
        values = jnp.dot(weights.astype(bf16), queries, preferred_element_type=f32)
        along = column_of(eye, dot * coefs[3 * npass + 1 : 3 * npass + 2, at])
        values = values - along * p_all[at, :].astype(f32)
        if a == 0:
            kept[...] = values
        else:
            sent[a - 1][...] = values.astype(bf16)


def spread_pass(scale, coefs, sums, pick, q_all, p_all, rows):
    block = (rows, q_all.shape[1])
    kept, *sent = local(
        functools.partial(spread_pass_kernel, rows),
        "spread_pass",
        [(block, f32)] + [(block, bf16)] * (len(pass_at) - 1),
        (scale, coefs, sums, pick, q_all, p_all),
        3,
    )
    return kept, sent


def fold_query_kernel(own, other, kept, sent):
    rows = kept.shape[0]
    total = own[...] + other[...].astype(f32)
    kept[...] = total[:rows]
    sent[...] = total[rows:].astype(bf16)


def fold_query(own, other):
    half = (own.shape[0] // 2, own.shape[1])
    return local(fold_query_kernel, "fold_query", [(half, f32), (half, bf16)], (own, other))


def grad_query_kernel(own, other, scale, sums, coefs, raw, raw_pass, grad, rounded):
    nq, npass = len(query_at), len(pass_at)
    rows = own.shape[0]
    eye = eye_of(rows)
    inv_norm = coefs[3 * npass : 3 * npass + 1, :rows]
    share = scale[:1] / (sums[:1] + sums[nq : nq + 1])
    pos = sums[:1] * coefs[3 * npass + 1 : 3 * npass + 2, :rows]
    dot = share * (sums[2 * nq : 2 * nq + 1] - sums[:1] * coefs[3 * npass + 2 : 3 * npass + 3, :rows])
    total = own[...] + other[...].astype(f32)
    total = total - column_of(eye, pos) * raw_pass[:rows, :].astype(f32)
    values = column_of(eye, share * inv_norm) * total
    values = values - column_of(eye, dot * inv_norm * inv_norm) * raw[:rows, :].astype(f32)
    grad[...] = values
    rounded[...] = values.astype(bf16)


def grad_pass_kernel(own, first, second, third, coefs, after, grad, rounded):
    npass = len(pass_at)
    rows = own.shape[0]
    inv_norm = column_of(eye_of(rows), coefs[3 * npass + 1 : 3 * npass + 2, :rows])
    others = first[...].astype(f32) + second[...].astype(f32) + third[...].astype(f32)
    values = inv_norm * (own[...] + others)
    grad[...] = values
    rounded[...] = values.astype(bf16)


def grad_out(kernel, name, own, operands):
    return local(kernel, name, [(own.shape, f32), (own.shape, bf16)], (own, *operands))


def decode_kernel(tower, tile, me, grad, mine, theirs, slope, w_in, w_out, *refs):
    send, own, total = refs[-3:]
    first = me[0] == 0
    rows = grad.shape[0]
    mine, theirs = mine[...], theirs[...]
    rounded = jnp.concatenate(
        [jnp.where(first, mine, theirs), jnp.where(first, theirs, mine)], axis=1
    )
    for t in range(w_in.shape[0] // tile):
        at = slice(t * tile, (t + 1) * tile)
        hidden = jnp.dot(rounded, w_out[:, at], preferred_element_type=f32)
        grad_pre = (hidden * slope[tower * rows : (tower + 1) * rows, at].astype(f32)).astype(bf16)
        part = jnp.dot(grad_pre, w_in[at, :], preferred_element_type=f32)
        if t == 0:
            total[...] = part
        else:
            total[...] += part
    mine, theirs = halves(first, total[...])
    send[...] = theirs.astype(bf16)
    own[...] = grad[...] + mine


def decode_one(me, grad, rounded, slope, tower, w_in, w_out, *after):
    hidden, width = w_in.shape
    return local(
        functools.partial(decode_kernel, tower, min(512, hidden)),
        "decode_one",
        [(grad.shape, bf16), (grad.shape, f32)],
        (grad, rounded, swap(rounded, "mp", 1), slope, w_in, w_out, *after),
        3,
        [pltpu.VMEM((grad.shape[0], width), f32)],
        [me],
    )


def finish_kernel(own, other, *refs):
    out, done = refs[-2:]
    out[...] = (own[...] + other[...].astype(f32)).astype(bf16)
    done[...] = jnp.zeros_like(done)


def finish(own, other, name, *after):
    return pl.pallas_call(
        finish_kernel,
        in_specs=[vmem] * (2 + len(after)),
        out_specs=[vmem] * 2,
        out_shape=[jax.ShapeDtypeStruct(own.shape, bf16), pltpu.VMEM((8, 128), f32)],
        compiler_params=pltpu.CompilerParams(vmem_limit_bytes=1 << 20),
        name=name,
    )(*[pltpu.with_memory_space_constraint(x, pltpu.VMEM) for x in (own, other, *after)])


def paired_shards(
    query_states, passage_states, w_in, w_out, neg_owner, neg_mask, served_rows, loss_scale
):
    rows = query_states.shape[0]
    owners = served_rows.shape[1]
    me = lax.axis_index("mp").astype(jnp.int32).reshape(1)
    place = lax.axis_index("dp").astype(jnp.int32).reshape(1)
    send_q, send_p, own_q, own_p, pre_act, slots, served, scale, w_in, w_out = encode_both(
        me, place, loss_scale.reshape(1), query_states, passage_states, w_in, w_out, neg_owner, neg_mask, served_rows
    )
    slope = local(slope_kernel, "slope", [(pre_act.shape, bf16)], (pre_act,))[0]
    w_in, w_out = flip(w_in, "flip_in"), flip(w_out, "flip_out")
    raw_q = pack(own_q, swap(send_q, "mp", 1), slots, slope, w_in, w_out)
    raw_p = pack(own_p, swap(send_p, "mp", 1), served)
    p_blocks = gather_blocks(raw_p, pass_bits)
    q_blocks = gather_blocks(raw_q, query_bits)

    table, valid, pick, q_all, p_all = score(place, q_blocks, p_blocks, rows, owners)
    coefs, sums = weigh(table, swap(table, "mp", 1), valid, rows)
    kept_q, sent_q = spread_query(coefs, pick, p_all, rows)
    sums = exchange_sums(sums, query_bits[1], sent_q)
    kept_q, sent_q = fold_query(kept_q, swap(sent_q, "dp", query_bits[1]))
    sums = exchange_sums(sums, query_bits[0], sent_q)
    kept_p, sent_p = spread_pass(scale, coefs, sums, pick, q_all, p_all, rows)
    others_p = [swap(x, "dp", at) for x, at in zip(sent_p, pass_at[1:])]
    grad_q, round_q = grad_out(
        grad_query_kernel,
        "grad_query",
        kept_q,
        (swap(sent_q, "dp", query_bits[0]), scale, sums, coefs, raw_q, raw_p),
    )
    grad_p, round_p = grad_out(
        grad_pass_kernel,
        "grad_pass",
        kept_p,
        (*others_p, coefs, round_q),
    )
    send_q, own_q = decode_one(me, grad_q, round_q, slope, 0, w_in, w_out)
    send_p, own_p = decode_one(me, grad_p, round_p, slope, 1, w_in, w_out, send_q)
    out_q, done_q = finish(own_q, swap(send_q, "mp", 1), "out_query")
    out_p, _ = finish(own_p, swap(send_p, "mp", 1), "out_pass", done_q)
    return (out_q, out_p)


def solution(mesh):
    in_specs = (
        P("dp", None),
        P("dp", None),
        P(None, "mp"),
        P("mp", None),
        P("dp", None),
        P("dp", None),
        P("dp", None, None),
        P(),
    )
    out_specs = (P("dp", "mp"), P("dp", "mp"))
    gathered = len(query_at) * len(pass_at)
    paired = mesh.shape["mp"] == 2 and mesh.shape["dp"] == gathered
    shards = paired_shards if paired else general_shards
    return jax.shard_map(shards, mesh=mesh, in_specs=in_specs, out_specs=out_specs, check_vma=False)
```

```python
import functools

import jax
import jax.numpy as jnp
from jax import lax
from jax.experimental import pallas as pl
from jax.experimental.pallas import tpu as pltpu
from jax.sharding import PartitionSpec as P

logit_scale = 50.0
norm_eps = 1e-06
root_half = 0.7071067811865476
inv_root_two_pi = 0.3989422804014327
f32, bf16 = jnp.float32, jnp.bfloat16
nt = (((1,), (1,)), ((), ()))
tn = (((0,), (0,)), ((), ()))
vmem = pl.BlockSpec(memory_space=pltpu.VMEM)
smem = pl.BlockSpec(memory_space=pltpu.SMEM)
hbm = pl.BlockSpec(memory_space=pltpu.HBM)


def gelu_value(values):
    return 0.5 * values * (1.0 + lax.erf(values * root_half))


def gelu_slope(values):
    return (
        0.5 * (1.0 + lax.erf(values * root_half))
        + values * jnp.exp(-0.5 * values * values) * inv_root_two_pi
    )


def own_columns(values):
    column_width = values.shape[1] // lax.axis_size("mp")
    return lax.dynamic_slice_in_dim(values, lax.axis_index("mp") * column_width, column_width, 1)


def encode(states, w_in, w_out):
    pre_act = jnp.dot(states, w_in, preferred_element_type=jnp.float32)
    hidden = gelu_value(pre_act).astype(jnp.bfloat16)
    partial_out = jnp.dot(hidden, w_out, preferred_element_type=jnp.float32)
    mixed_sum = lax.psum(partial_out, "mp")
    output = states.astype(jnp.float32) + mixed_sum
    inv_norm = lax.rsqrt(jnp.sum(output * output, axis=1, keepdims=True) + norm_eps)
    return (pre_act, output * inv_norm, inv_norm)


def decode(grad_part, pre_act, unit_rows, inv_norm, w_in, w_out):
    grad_emb = lax.all_gather(grad_part.astype(jnp.bfloat16), "mp", axis=1, tiled=True).astype(
        grad_part.dtype
    )
    grad_out = inv_norm * (
        grad_emb - unit_rows * jnp.sum(unit_rows * grad_emb, axis=1, keepdims=True)
    )
    grad_hidden = lax.dot_general(
        grad_out.astype(jnp.bfloat16), w_out, nt, preferred_element_type=jnp.float32
    )
    grad_pre = (grad_hidden * gelu_slope(pre_act)).astype(jnp.bfloat16)
    partial_in = lax.dot_general(grad_pre, w_in, nt, preferred_element_type=jnp.float32)
    summed = lax.psum_scatter(
        partial_in.astype(jnp.bfloat16), "mp", scatter_dimension=1, tiled=True
    ).astype(jnp.float32)
    return (summed + own_columns(grad_out)).astype(jnp.bfloat16)


def general_shards(
    query_states, passage_states, w_in, w_out, neg_owner, neg_mask, served_rows, loss_scale
):
    owners = lax.axis_size("dp")
    row_count = query_states.shape[0]
    negatives = neg_owner.shape[1]
    capacity = served_rows.shape[2]
    pre_pass, unit_pass, inv_pass = encode(passage_states, w_in, w_out)
    emb_pass = own_columns(unit_pass).astype(jnp.bfloat16)
    column_width = emb_pass.shape[1]
    served = served_rows[0]
    flat_owner = neg_owner.reshape(-1)
    onehot = (flat_owner[:, None] == jnp.arange(owners, dtype=jnp.int32)[None, :]).astype(jnp.int32)
    before = jnp.cumsum(onehot, axis=0, dtype=jnp.int32) - onehot
    slot_index = jnp.sum(before * onehot, axis=1, dtype=jnp.int32)
    slot_place = flat_owner * capacity + slot_index
    every_emb = lax.all_gather(emb_pass, "dp", axis=0, tiled=True)
    rows_for_me = lax.all_to_all(
        served_rows, "dp", split_axis=1, concat_axis=0, tiled=True
    ).reshape(owners * capacity)
    neg_rows = jnp.take(rows_for_me, slot_place, axis=0)
    neg_emb = jnp.take(every_emb, flat_owner * row_count + neg_rows, axis=0)
    neg_emb = neg_emb.reshape(row_count, negatives, column_width)
    pre_query, unit_query, inv_query = encode(query_states, w_in, w_out)
    emb_query = own_columns(unit_query).astype(jnp.bfloat16)
    pos_part = jnp.einsum("qd,qd->q", emb_query, emb_pass, preferred_element_type=jnp.float32)
    neg_part = jnp.einsum("qd,qnd->qn", emb_query, neg_emb, preferred_element_type=jnp.float32)
    pos_score, neg_score = lax.psum((pos_part, neg_part), "mp")
    exp_pos = jnp.exp(logit_scale * pos_score)
    exp_neg = neg_mask.astype(jnp.float32) * jnp.exp(logit_scale * neg_score)
    denominator = exp_pos + jnp.sum(exp_neg, axis=1)
    factor = loss_scale * logit_scale
    grad_pos = factor * (exp_pos / denominator - 1.0)
    grad_neg = factor * exp_neg / denominator[:, None]
    query_values = emb_query.astype(jnp.float32)
    grad_query_emb = grad_pos[:, None] * emb_pass.astype(jnp.float32) + jnp.sum(
        grad_neg[:, :, None] * neg_emb.astype(jnp.float32), axis=1
    )
    slot_terms = (
        (grad_neg[:, :, None] * query_values[:, None, :])
        .astype(jnp.bfloat16)
        .reshape(-1, column_width)
    )
    outgoing_grad = (
        jnp.zeros((owners * capacity, column_width), jnp.bfloat16).at[slot_place].set(slot_terms)
    )
    returned = lax.all_to_all(
        outgoing_grad.reshape(owners, capacity, column_width),
        "dp",
        split_axis=0,
        concat_axis=0,
        tiled=True,
    )
    grad_query_states = decode(grad_query_emb, pre_query, unit_query, inv_query, w_in, w_out)
    gathered_back = (
        jnp.zeros((row_count, column_width), jnp.float32)
        .at[served.reshape(-1)]
        .add(returned.reshape(-1, column_width).astype(jnp.float32))
    )
    grad_pass_emb = grad_pos[:, None] * query_values + gathered_back
    grad_passage_states = decode(grad_pass_emb, pre_pass, unit_pass, inv_pass, w_in, w_out)
    return (grad_query_states, grad_passage_states)


query_bits, pass_bits = (8, 1), (4, 2)


def offsets(bits):
    found = [0]
    for bit in bits:
        found = found + [at | bit for at in found]
    return found


query_at, pass_at = offsets(query_bits), offsets(pass_bits)


def swap(values, axis, bit):
    size = lax.axis_size(axis)
    return lax.ppermute(values, axis, [(i, i ^ bit) for i in range(size)])


def gather_blocks(block, bits):
    blocks = [block]
    for bit in bits:
        blocks = blocks + [swap(values, "dp", bit) for values in blocks]
    return blocks


def halves(first, values):
    width = values.shape[1] // 2
    left, right = values[:, :width], values[:, width:]
    return jnp.where(first, left, right), jnp.where(first, right, left)


def eye_of(size):
    return (
        lax.broadcasted_iota(jnp.int32, (size, size), 0)
        == lax.broadcasted_iota(jnp.int32, (size, size), 1)
    ).astype(f32)


def local(kernel, name, outs, operands, mebibytes=1, scratch=(), scalars=(), aliases=None):
    return pl.pallas_call(
        kernel,
        in_specs=[smem] * len(scalars) + [vmem] * len(operands),
        out_specs=[vmem] * len(outs),
        out_shape=[pltpu.VMEM(shape, dtype) for shape, dtype in outs],
        scratch_shapes=list(scratch),
        input_output_aliases=aliases or {},
        compiler_params=pltpu.CompilerParams(vmem_limit_bytes=mebibytes << 20),
        cost_estimate=pl.CostEstimate(flops=1, bytes_accessed=1, transcendentals=0),
        name=name,
    )(*scalars, *[pltpu.with_memory_space_constraint(x, pltpu.VMEM) for x in operands])


def encode_far_kernel(
    tile, me, place, scale, xq, xp, w_in, w_out,
    send_q, send_p, states, hidden, pre_act, scale_out, w_in_kept, w_out_far, total, sems,
):
    rows = xq.shape[0]
    tiles = w_in.shape[1] // tile
    half = w_out_far.shape[1]
    far = pl.ds(pl.multiple_of((1 - me[0]) * half, 128), half)
    slices = [slice(t * tile, (t + 1) * tile) for t in range(tiles)]
    copies = [
        pltpu.make_async_copy(xq, states.at[:rows, :], sems.at[0]),
        pltpu.make_async_copy(xp, states.at[rows:, :], sems.at[1]),
    ]
    for t, at in enumerate(slices):
        copies.append(pltpu.make_async_copy(w_in.at[:, at], w_in_kept.at[:, at], sems.at[2 + t]))
    for t, at in enumerate(slices):
        copies.append(
            pltpu.make_async_copy(w_out.at[at, far], w_out_far.at[at, :], sems.at[2 + tiles + t])
        )
    for copy in copies:
        copy.start()
    scale_out[...] = jnp.zeros_like(scale_out) + scale[0] * logit_scale

    def up(t):
        copies[2 + t].wait()
        return jnp.dot(states[...], w_in_kept[:, slices[t]], preferred_element_type=f32)

    def down(t):
        copies[2 + tiles + t].wait()
        return jnp.dot(hidden[:, slices[t]], w_out_far[slices[t], :], preferred_element_type=f32)

    copies[0].wait()
    copies[1].wait()
    for t, at in enumerate(slices):
        pre = up(t)
        pre_act[:, at] = pre
        cdf = 0.5 * (1.0 + lax.erf(pre * root_half))
        hidden[:, at] = (pre * cdf).astype(bf16)
    for t in range(tiles):
        part = down(t)
        if t == 0:
            total[...] = part
        elif t < tiles - 1:
            total[...] += part
        else:
            part = total[...] + part
    send_q[...] = part[:rows].astype(bf16)
    send_p[...] = part[rows:].astype(bf16)


def in_hbm(*values):
    return [pltpu.with_memory_space_constraint(x, pltpu.HBM) for x in values]


def encode_far(me, place, scale, xq, xp, w_in, w_out):
    rows, width = xq.shape
    hidden = w_in.shape[1]
    tile = min(512, hidden)
    half = (rows, width // 2)
    return pl.pallas_call(
        functools.partial(encode_far_kernel, tile),
        in_specs=[smem] * 3 + [hbm] * 4,
        out_specs=[vmem] * 8,
        out_shape=[
            pltpu.VMEM(half, bf16),
            pltpu.VMEM(half, bf16),
            pltpu.VMEM((2 * rows, width), bf16),
            pltpu.VMEM((2 * rows, hidden), bf16),
            pltpu.VMEM((2 * rows, hidden), f32),
            pltpu.VMEM((8, rows), f32),
            pltpu.VMEM(w_in.shape, bf16),
            pltpu.VMEM((hidden, width // 2), bf16),
        ],
        scratch_shapes=[
            pltpu.VMEM((2 * rows, width // 2), f32),
            pltpu.SemaphoreType.DMA((2 + 2 * (hidden // tile),)),
        ],
        compiler_params=pltpu.CompilerParams(vmem_limit_bytes=8 << 20),
        name="encode_far",
    )(me, place, scale, *in_hbm(xq, xp, w_in, w_out))


def encode_near_kernel(
    tile, me, w_out, owner, mask, served, hidden, states,
    own_q, own_p, w_out_near, slots_out, served_out, total, owner_held, mask_held, served_held, sems,
):
    rows, half = own_q.shape
    tiles = hidden.shape[1] // tile
    near = pl.ds(pl.multiple_of(me[0] * half, 128), half)
    copies = []
    for t in range(tiles):
        at = slice(t * tile, (t + 1) * tile)
        copies.append(pltpu.make_async_copy(w_out.at[at, near], w_out_near.at[at, :], sems.at[t]))
    numbers = [
        pltpu.make_async_copy(owner, owner_held, sems.at[tiles]),
        pltpu.make_async_copy(mask, mask_held, sems.at[tiles + 1]),
        pltpu.make_async_copy(served, served_held, sems.at[tiles + 2]),
    ]
    for copy in numbers + copies:
        copy.start()
    total[...] = halves(me[0] == 0, states[...].astype(f32))[0]
    for copy in numbers:
        copy.wait()
    owners = slots_out.shape[0]
    down = lax.broadcasted_iota(jnp.int32, (owners, rows), 0)
    named = jnp.zeros((owners, rows), f32)
    live = jnp.zeros((owners, rows), f32)
    for j in range(owner.shape[0]):
        hit = (owner_held[j : j + 1, :] == down).astype(f32)
        named = named + hit
        live = live + hit * mask_held[j : j + 1, :].astype(f32)
    earlier = lax.broadcasted_iota(jnp.int32, (rows, rows), 0) < lax.broadcasted_iota(
        jnp.int32, (rows, rows), 1
    )
    slot = jnp.dot(named.astype(bf16), earlier.astype(f32).astype(bf16), preferred_element_type=f32)
    slots_out[...] = jnp.where(live > 0.5, slot, -1.0).astype(bf16)
    served_out[...] = served_held[0].astype(f32).astype(bf16)
    for t in range(tiles):
        at = slice(t * tile, (t + 1) * tile)
        copies[t].wait()
        total[...] += jnp.dot(hidden[:, at], w_out_near[at, :], preferred_element_type=f32)
    own_q[...] = total[:rows, :]
    own_p[...] = total[rows:, :]


def encode_near(me, w_out, owner, mask, served, hidden, states):
    rows, width = states.shape[0] // 2, states.shape[1]
    owners = served.shape[1]
    tile = min(512, hidden.shape[1])
    half = (rows, width // 2)
    return pl.pallas_call(
        functools.partial(encode_near_kernel, tile),
        in_specs=[smem] + [hbm] * 4 + [vmem] * 2,
        out_specs=[vmem] * 5,
        out_shape=[
            pltpu.VMEM(half, f32),
            pltpu.VMEM(half, f32),
            pltpu.VMEM((w_out.shape[0], width // 2), bf16),
            pltpu.VMEM((owners, rows), bf16),
            pltpu.VMEM((owners, served.shape[2]), bf16),
        ],
        scratch_shapes=[
            pltpu.VMEM((2 * rows, width // 2), f32),
            pltpu.VMEM(owner.T.shape, jnp.int32),
            pltpu.VMEM(mask.T.shape, jnp.int32),
            pltpu.VMEM(served.shape, jnp.int32),
            pltpu.SemaphoreType.DMA((hidden.shape[1] // tile + 3,)),
        ],
        compiler_params=pltpu.CompilerParams(vmem_limit_bytes=3 << 20),
        cost_estimate=pl.CostEstimate(flops=1, bytes_accessed=1, transcendentals=0),
        name="encode_near",
    )(
        me,
        *in_hbm(w_out, owner.T, mask.T, served),
        *[pltpu.with_memory_space_constraint(x, pltpu.VMEM) for x in (hidden, states)],
    )


def slope_kernel(pre_act, slope):
    step = 32

    def body(n, carry):
        at = pl.ds(pl.multiple_of(n * step, step), step)
        slope[at, :] = gelu_slope(pre_act[at, :]).astype(bf16)
        return carry

    lax.fori_loop(0, pre_act.shape[0] // step, body, 0)


def flip_kernel(weights, out):
    rows, columns = weights.shape
    size = 256
    eye = eye_of(size).astype(bf16)
    for i in range(0, rows, size):
        for j in range(0, columns, size):
            out[j : j + size, i : i + size] = lax.dot_general(
                eye, weights[i : i + size, j : j + size], nt, preferred_element_type=f32
            ).astype(bf16)


def flip(weights, name):
    return local(flip_kernel, name, [(weights.shape[::-1], bf16)], (weights,), 2)[0]


def flip_rows_kernel(far, me, weights, out):
    half, columns = out.shape[1], out.shape[0]
    size = 256
    eye = eye_of(size).astype(bf16)
    first = (1 - me[0] if far else me[0]) * half
    for i in range(0, half, size):
        rows = pl.ds(pl.multiple_of(first + i, size), size)
        for j in range(0, columns, size):
            out[j : j + size, i : i + size] = lax.dot_general(
                eye, weights[rows, j : j + size], nt, preferred_element_type=f32
            ).astype(bf16)


def flip_rows(me, weights, far, name):
    out = ((weights.shape[1], weights.shape[0] // 2), bf16)
    return local(functools.partial(flip_rows_kernel, far), name, [out], (weights,), 2, scalars=[me])[0]


def pack_kernel(own, other, numbers, *refs):
    out = refs[-1]
    rows = own.shape[0]
    out[:rows, :] = (own[...] + other[...].astype(f32)).astype(bf16)
    out[rows:, :] = jnp.zeros((out.shape[0] - rows, out.shape[1]), bf16)
    out[rows:, : numbers.shape[1]] = numbers[...]


def pack(own, other, numbers, *after):
    shape = (own.shape[0] + numbers.shape[0], own.shape[1])
    return local(pack_kernel, "pack", [(shape, bf16)], (own, other, numbers, *after))[0]


def score_block(a, owners, rows, place, ref, q_all, slots, table, valid, pick, p_all, served):
    npass = len(pass_at)
    p_all[a * rows : (a + 1) * rows, :] = ref[:rows, :]
    served[...] = ref[rows:, :rows].astype(f32)
    eye = eye_of(rows)
    down = lax.broadcasted_iota(jnp.int32, (rows, rows), 0).astype(f32)
    part = ref[:rows, :]
    block = part.astype(f32)
    square = jnp.sum(block * block, axis=1, keepdims=True)
    table[2 * npass + 2 : 2 * npass + 3, a * rows : (a + 1) * rows] = jnp.sum(
        eye * square, axis=0, keepdims=True
    )
    scores = lax.dot_general(part, q_all[...], nt, preferred_element_type=f32)
    if a == 0:
        table[2 * npass + 1 : 2 * npass + 2, :rows] = jnp.sum(
            eye * scores[:, :rows], axis=0, keepdims=True
        )
    for b, at in enumerate(query_at):
        lanes = slice(b * rows, (b + 1) * rows)
        row_of = served[pl.ds(place[0] ^ at, 1), :]
        slot_of = slots[pl.ds(b * owners + (place[0] ^ pass_at[a]), 1), :]
        by_slot = (down == row_of).astype(f32).astype(bf16)
        by_query = (down == slot_of).astype(f32).astype(bf16)
        chosen = jnp.dot(by_slot, by_query, preferred_element_type=f32)
        table[a : a + 1, lanes] = jnp.sum(chosen * scores[:, lanes], axis=0, keepdims=True)
        table[npass + a : npass + a + 1, lanes] = jnp.sum(chosen * square, axis=0, keepdims=True)
        valid[a : a + 1, lanes] = (slot_of >= 0.0).astype(f32)
        pick[a * rows : (a + 1) * rows, lanes] = chosen.astype(bf16)


def score_early_kernel(owners, rows, place, *refs):
    nq, npass = len(query_at), len(pass_at)
    q_refs, p_refs = refs[:nq], refs[nq : nq + npass - 1]
    table, valid, pick, p_all, q_all, slots = refs[-7:-1]
    served = refs[-1]
    table[...] = jnp.zeros_like(table)
    for n, ref in enumerate(q_refs):
        lanes = slice(n * rows, (n + 1) * rows)
        q_all[lanes, :] = ref[:rows, :]
        slots[n * owners : (n + 1) * owners, :] = ref[rows:, :rows].astype(f32)
        block = ref[:rows, :].astype(f32)
        square = jnp.sum(block * block, axis=1, keepdims=True)
        table[2 * npass : 2 * npass + 1, lanes] = jnp.sum(
            eye_of(rows) * square, axis=0, keepdims=True
        )
    for a, ref in enumerate(p_refs):
        score_block(a, owners, rows, place, ref, q_all, slots, table, valid, pick, p_all, served)


def score_last_kernel(owners, rows, place, ref, q_all, slots, *refs):
    table, valid, pick, p_all, served = refs[-5:]
    last = len(pass_at) - 1
    score_block(last, owners, rows, place, ref, q_all, slots, table, valid, pick, p_all, served)


def score(place, q_blocks, p_blocks, rows, owners, *after):
    nq, npass = len(query_at), len(pass_at)
    width = q_blocks[0].shape[1]
    outs = [
        ((-(-(2 * npass + 3) // 8) * 8, nq * rows), f32),
        ((8, nq * rows), f32),
        ((npass * rows, nq * rows), bf16),
        ((npass * rows, width), bf16),
    ]
    scratch = [pltpu.VMEM((owners, rows), f32)]
    *parts, q_all, slots = local(
        functools.partial(score_early_kernel, owners, rows),
        "score_early",
        outs + [((nq * rows, width), bf16), ((nq * owners, rows), f32)],
        (*q_blocks, *p_blocks[:-1], *after),
        3,
        scratch,
        [place],
    )
    parts = local(
        functools.partial(score_last_kernel, owners, rows),
        "score_last",
        outs,
        (p_blocks[-1], q_all, slots, *parts),
        3,
        scratch,
        [place],
        {4 + n: n for n in range(len(parts))},
    )
    return (*parts, q_all)


def weigh_kernel(rows, table, other, valid, *refs):
    coefs, sums = refs[-2:]
    nq, npass = len(query_at), len(pass_at)
    full = table[...] + other[...]
    raw, square = full[:npass], full[npass : 2 * npass]
    inv_q = lax.rsqrt(full[2 * npass : 2 * npass + 1] + norm_eps)
    inv_pass = lax.rsqrt(full[2 * npass + 2 : 2 * npass + 3] + norm_eps)
    inv_neg = lax.rsqrt(square + norm_eps)
    neg_score = raw * inv_q * inv_neg
    exp_neg = valid[:npass] * jnp.exp(logit_scale * neg_score)
    pos_score = full[2 * npass + 1 : 2 * npass + 2] * inv_q * inv_pass
    coefs[...] = jnp.zeros_like(coefs)
    coefs[:npass] = exp_neg
    coefs[npass : 2 * npass] = exp_neg * inv_neg
    coefs[2 * npass : 3 * npass] = exp_neg * neg_score
    coefs[3 * npass : 3 * npass + 1] = inv_q
    coefs[3 * npass + 1 : 3 * npass + 2] = inv_pass
    coefs[3 * npass + 2 : 3 * npass + 3] = pos_score
    neg_sum = jnp.sum(exp_neg, axis=0, keepdims=True)
    neg_dot = jnp.sum(exp_neg * neg_score, axis=0, keepdims=True)
    sums[...] = jnp.zeros_like(sums)
    for n in range(nq):
        sums[n : n + 1, :] = neg_sum[:, n * rows : (n + 1) * rows]
        sums[2 * nq + n : 2 * nq + n + 1, :] = neg_dot[:, n * rows : (n + 1) * rows]
    sums[nq : nq + 1, :] = jnp.exp(logit_scale * pos_score[:, :rows])


def weigh(table, other, valid, rows, *after):
    nq, npass = len(query_at), len(pass_at)
    return local(
        functools.partial(weigh_kernel, rows),
        "weigh",
        [((-(-(3 * npass + 3) // 8) * 8, nq * rows), f32), ((-(-3 * nq // 8) * 8, rows), f32)],
        (table, other, valid, *after),
    )


def add_sums_kernel(bit, sums, other, *refs):
    out = refs[-1]
    nq = len(query_at)
    out[...] = sums[...]
    for n, at in enumerate(query_at):
        m = query_at.index(at ^ bit)
        for first in (0, nq, 2 * nq):
            k, l = first + n, first + m
            out[k : k + 1, :] = sums[k : k + 1, :] + other[l : l + 1, :]


def exchange_sums(sums, bit, *after):
    kernel = functools.partial(add_sums_kernel, bit)
    return local(kernel, "add_sums", [(sums.shape, f32)], (sums, swap(sums, "dp", bit), *after))[0]


def spread_query_kernel(rows, far, coefs, pick, p_all, *refs):
    out = refs[-1]
    npass = len(pass_at)
    passages = p_all[...]
    blocks = [b for b, at in enumerate(query_at) if bool(at & query_bits[1]) == far]
    for n, b in enumerate(blocks):
        lanes = slice(b * rows, (b + 1) * rows)
        pieces = []
        for a in range(npass):
            piece = pick[a * rows : (a + 1) * rows, lanes].astype(f32)
            piece = piece * coefs[npass + a : npass + a + 1, lanes]
            pieces.append(piece.T.astype(bf16))
        weights = jnp.concatenate(pieces, axis=1)
        values = jnp.dot(weights, passages, preferred_element_type=f32)
        out[n * rows : (n + 1) * rows, :] = values.astype(out.dtype)


def spread_query(coefs, pick, p_all, rows, far, *after):
    half = (len(query_at) // 2 * rows, p_all.shape[1])
    return local(
        functools.partial(spread_query_kernel, rows, far),
        "spread_query",
        [(half, bf16 if far else f32)],
        (coefs, pick, p_all, *after),
        3,
    )[0]


def column_of(eye, row):
    return jnp.sum(eye * row, axis=1, keepdims=True)


def spread_pass_kernel(rows, blocks, scale, coefs, sums, pick, q_all, p_all, *outs):
    nq, npass = len(query_at), len(pass_at)
    eye = eye_of(rows)
    share = scale[:nq] / (sums[:nq] + sums[nq : 2 * nq])
    pos = -share[:1] * sums[:1]
    share = jnp.concatenate([share[n : n + 1] for n in range(nq)], axis=1)
    scaled = share * coefs[3 * npass : 3 * npass + 1]
    queries = q_all[...]
    for out, a in zip(outs, blocks):
        at = slice(a * rows, (a + 1) * rows)
        chosen = pick[at, :]
        weights = chosen.astype(f32) * (coefs[a : a + 1] * scaled)
        product = share * coefs[2 * npass + a : 2 * npass + a + 1]
        high = product.astype(bf16).astype(f32)
        parts = jnp.concatenate([high, product - high, jnp.zeros((14, nq * rows), f32)], axis=0)
        dots = lax.dot_general(parts.astype(bf16), chosen, nt, preferred_element_type=f32)
        dot = jnp.sum(dots, axis=0, keepdims=True)
        if a == 0:
            own = pos * coefs[3 * npass : 3 * npass + 1, :rows]
            weights = jnp.concatenate([weights[:, :rows] + eye * own, weights[:, rows:]], axis=1)
            dot = dot + pos * coefs[3 * npass + 2 : 3 * npass + 3, :rows]
        values = jnp.dot(weights.astype(bf16), queries, preferred_element_type=f32)
        along = column_of(eye, dot * coefs[3 * npass + 1 : 3 * npass + 2, at])
        values = values - along * p_all[at, :].astype(f32)
        out[...] = values.astype(out.dtype)


def spread_pass(scale, coefs, sums, pick, q_all, p_all, rows, blocks, dtype):
    block = (rows, q_all.shape[1])
    return local(
        functools.partial(spread_pass_kernel, rows, blocks),
        "spread_pass",
        [(block, dtype)] * len(blocks),
        (scale, coefs, sums, pick, q_all, p_all),
        3,
    )


def fold_query_kernel(own, other, kept, sent):
    rows = kept.shape[0]
    total = own[...] + other[...].astype(f32)
    kept[...] = total[:rows]
    sent[...] = total[rows:].astype(bf16)


def fold_query(own, other):
    half = (own.shape[0] // 2, own.shape[1])
    return local(fold_query_kernel, "fold_query", [(half, f32), (half, bf16)], (own, other))


def grad_query_kernel(own, other, scale, sums, coefs, raw, raw_pass, grad, rounded):
    nq, npass = len(query_at), len(pass_at)
    rows = own.shape[0]
    eye = eye_of(rows)
    inv_norm = coefs[3 * npass : 3 * npass + 1, :rows]
    share = scale[:1] / (sums[:1] + sums[nq : nq + 1])
    pos = sums[:1] * coefs[3 * npass + 1 : 3 * npass + 2, :rows]
    dot = share * (sums[2 * nq : 2 * nq + 1] - sums[:1] * coefs[3 * npass + 2 : 3 * npass + 3, :rows])
    total = own[...] + other[...].astype(f32)
    total = total - column_of(eye, pos) * raw_pass[:rows, :].astype(f32)
    values = column_of(eye, share * inv_norm) * total
    values = values - column_of(eye, dot * inv_norm * inv_norm) * raw[:rows, :].astype(f32)
    grad[...] = values
    rounded[...] = values.astype(bf16)


def grad_pass_kernel(own, first, second, third, coefs, after, grad, rounded):
    npass = len(pass_at)
    rows = own.shape[0]
    inv_norm = column_of(eye_of(rows), coefs[3 * npass + 1 : 3 * npass + 2, :rows])
    others = first[...].astype(f32) + second[...].astype(f32) + third[...].astype(f32)
    values = inv_norm * (own[...] + others)
    grad[...] = values
    rounded[...] = values.astype(bf16)


def grad_out(kernel, name, own, operands):
    return local(kernel, name, [(own.shape, f32), (own.shape, bf16)], (own, *operands))


def decode_near_kernel(tile, mine, w_out, out):
    for t in range(w_out.shape[1] // tile):
        at = slice(t * tile, (t + 1) * tile)
        out[:, at] = jnp.dot(mine[...], w_out[:, at], preferred_element_type=f32)


def decode_far_kernel(tower, tile, near, theirs, slope, w_out, w_in, *refs):
    grad_pre, send = refs[-2:]
    rows = theirs.shape[0]
    for t in range(w_out.shape[1] // tile):
        at = slice(t * tile, (t + 1) * tile)
        hidden = near[:, at] + jnp.dot(theirs[...], w_out[:, at], preferred_element_type=f32)
        grad_pre[:, at] = (hidden * slope[tower * rows : (tower + 1) * rows, at].astype(f32)).astype(bf16)
    send[...] = jnp.dot(grad_pre[...], w_in[...], preferred_element_type=f32).astype(bf16)


def decode_own_kernel(grad, grad_pre, w_in, *refs):
    refs[-1][...] = grad[...] + jnp.dot(grad_pre[...], w_in[...], preferred_element_type=f32)


def decode_far(rounded, slope, tower, w_out_near, w_out_far, w_in_far, *after):
    rows, hidden = rounded.shape[0], slope.shape[1]
    tile = min(512, hidden)
    near = local(
        functools.partial(decode_near_kernel, tile),
        "decode_near",
        [((rows, hidden), f32)],
        (rounded, w_out_near),
        2,
    )[0]
    return local(
        functools.partial(decode_far_kernel, tower, tile),
        "decode_far",
        [((rows, hidden), bf16), (rounded.shape, bf16)],
        (near, swap(rounded, "mp", 1), slope, w_out_far, w_in_far, *after),
        2,
    )


def decode_own(grad, grad_pre, w_in_near, *after):
    return local(
        decode_own_kernel, "decode_own", [(grad.shape, f32)], (grad, grad_pre, w_in_near, *after), 2
    )[0]


def finish_kernel(own, other, *refs):
    out, done = refs[-2:]
    out[...] = (own[...] + other[...].astype(f32)).astype(bf16)
    done[...] = jnp.zeros_like(done)


def finish(own, other, name, *after):
    return pl.pallas_call(
        finish_kernel,
        in_specs=[vmem] * (2 + len(after)),
        out_specs=[vmem] * 2,
        out_shape=[jax.ShapeDtypeStruct(own.shape, bf16), pltpu.VMEM((8, 128), f32)],
        compiler_params=pltpu.CompilerParams(vmem_limit_bytes=1 << 20),
        name=name,
    )(*[pltpu.with_memory_space_constraint(x, pltpu.VMEM) for x in (own, other, *after)])


def paired_shards(
    query_states, passage_states, w_in, w_out, neg_owner, neg_mask, served_rows, loss_scale
):
    rows = query_states.shape[0]
    owners = served_rows.shape[1]
    me = lax.axis_index("mp").astype(jnp.int32).reshape(1)
    place = lax.axis_index("dp").astype(jnp.int32).reshape(1)
    send_q, send_p, states, hidden, pre_act, scale, w_in, w_out_far = encode_far(
        me, place, loss_scale.reshape(1), query_states, passage_states, w_in, w_out
    )
    own_q, own_p, w_out_near, slots, served = encode_near(
        me, w_out, neg_owner, neg_mask, served_rows, hidden, states
    )
    slope = local(slope_kernel, "slope", [(pre_act.shape, bf16)], (pre_act,))[0]
    w_in_far = flip_rows(me, w_in, True, "flip_in_far")
    w_in_near = flip_rows(me, w_in, False, "flip_in_near")
    w_out_far, w_out_near = flip(w_out_far, "flip_out_far"), flip(w_out_near, "flip_out_near")
    raw_q = pack(own_q, swap(send_q, "mp", 1), slots)
    raw_p = pack(own_p, swap(send_p, "mp", 1), served)
    q_blocks = gather_blocks(raw_q, query_bits)
    p_blocks = gather_blocks(raw_p, pass_bits)

    table, valid, pick, p_all, q_all = score(
        place, q_blocks, p_blocks, rows, owners, w_out_near, slope, w_in_far
    )
    coefs, sums = weigh(table, swap(table, "mp", 1), valid, rows, w_out_far, w_in_near)
    sent_q = spread_query(coefs, pick, p_all, rows, True)
    sums = exchange_sums(sums, query_bits[1], sent_q)
    kept_q = spread_query(coefs, pick, p_all, rows, False)
    kept_q, sent_q = fold_query(kept_q, swap(sent_q, "dp", query_bits[1]))
    sums = exchange_sums(sums, query_bits[0], sent_q)
    operands = (scale, coefs, sums, pick, q_all, p_all, rows)
    sent_p = spread_pass(*operands, tuple(range(1, len(pass_at))), bf16)
    kept_p = spread_pass(*operands, (0,), f32)[0]
    others_p = [swap(x, "dp", at) for x, at in zip(sent_p, pass_at[1:])]
    grad_q, round_q = grad_out(
        grad_query_kernel,
        "grad_query",
        kept_q,
        (swap(sent_q, "dp", query_bits[0]), scale, sums, coefs, raw_q, raw_p),
    )
    grad_p, round_p = grad_out(
        grad_pass_kernel,
        "grad_pass",
        kept_p,
        (*others_p, coefs, round_q),
    )
    pre_q, send_q = decode_far(round_q, slope, 0, w_out_near, w_out_far, w_in_far)
    pre_p, send_p = decode_far(round_p, slope, 1, w_out_near, w_out_far, w_in_far, send_q)
    own_q = decode_own(grad_q, pre_q, w_in_near, send_p)
    own_p = decode_own(grad_p, pre_p, w_in_near)
    out_q, done_q = finish(own_q, swap(send_q, "mp", 1), "out_query")
    out_p, _ = finish(own_p, swap(send_p, "mp", 1), "out_pass", done_q)
    return (out_q, out_p)


def solution(mesh):
    in_specs = (
        P("dp", None),
        P("dp", None),
        P(None, "mp"),
        P("mp", None),
        P("dp", None),
        P("dp", None),
        P("dp", None, None),
        P(),
    )
    out_specs = (P("dp", "mp"), P("dp", "mp"))
    gathered = len(query_at) * len(pass_at)
    paired = mesh.shape["mp"] == 2 and mesh.shape["dp"] == gathered
    shards = paired_shards if paired else general_shards
    return jax.shard_map(shards, mesh=mesh, in_specs=in_specs, out_specs=out_specs, check_vma=False)
```

```python
import functools

import jax
import jax.numpy as jnp
from jax import lax
from jax.experimental import pallas as pl
from jax.experimental.pallas import tpu as pltpu
from jax.sharding import PartitionSpec as P

logit_scale = 50.0
norm_eps = 1e-06
root_half = 0.7071067811865476
inv_root_two_pi = 0.3989422804014327
f32, bf16 = jnp.float32, jnp.bfloat16
nt = (((1,), (1,)), ((), ()))
tn = (((0,), (0,)), ((), ()))
vmem = pl.BlockSpec(memory_space=pltpu.VMEM)
smem = pl.BlockSpec(memory_space=pltpu.SMEM)
hbm = pl.BlockSpec(memory_space=pltpu.HBM)


def gelu_value(values):
    return 0.5 * values * (1.0 + lax.erf(values * root_half))


def gelu_slope(values):
    return (
        0.5 * (1.0 + lax.erf(values * root_half))
        + values * jnp.exp(-0.5 * values * values) * inv_root_two_pi
    )


def own_columns(values):
    column_width = values.shape[1] // lax.axis_size("mp")
    return lax.dynamic_slice_in_dim(values, lax.axis_index("mp") * column_width, column_width, 1)


def encode(states, w_in, w_out):
    pre_act = jnp.dot(states, w_in, preferred_element_type=jnp.float32)
    hidden = gelu_value(pre_act).astype(jnp.bfloat16)
    partial_out = jnp.dot(hidden, w_out, preferred_element_type=jnp.float32)
    mixed_sum = lax.psum(partial_out, "mp")
    output = states.astype(jnp.float32) + mixed_sum
    inv_norm = lax.rsqrt(jnp.sum(output * output, axis=1, keepdims=True) + norm_eps)
    return (pre_act, output * inv_norm, inv_norm)


def decode(grad_part, pre_act, unit_rows, inv_norm, w_in, w_out):
    grad_emb = lax.all_gather(grad_part.astype(jnp.bfloat16), "mp", axis=1, tiled=True).astype(
        grad_part.dtype
    )
    grad_out = inv_norm * (
        grad_emb - unit_rows * jnp.sum(unit_rows * grad_emb, axis=1, keepdims=True)
    )
    grad_hidden = lax.dot_general(
        grad_out.astype(jnp.bfloat16), w_out, nt, preferred_element_type=jnp.float32
    )
    grad_pre = (grad_hidden * gelu_slope(pre_act)).astype(jnp.bfloat16)
    partial_in = lax.dot_general(grad_pre, w_in, nt, preferred_element_type=jnp.float32)
    summed = lax.psum_scatter(
        partial_in.astype(jnp.bfloat16), "mp", scatter_dimension=1, tiled=True
    ).astype(jnp.float32)
    return (summed + own_columns(grad_out)).astype(jnp.bfloat16)


def general_shards(
    query_states, passage_states, w_in, w_out, neg_owner, neg_mask, served_rows, loss_scale
):
    owners = lax.axis_size("dp")
    row_count = query_states.shape[0]
    negatives = neg_owner.shape[1]
    capacity = served_rows.shape[2]
    pre_pass, unit_pass, inv_pass = encode(passage_states, w_in, w_out)
    emb_pass = own_columns(unit_pass).astype(jnp.bfloat16)
    column_width = emb_pass.shape[1]
    served = served_rows[0]
    flat_owner = neg_owner.reshape(-1)
    onehot = (flat_owner[:, None] == jnp.arange(owners, dtype=jnp.int32)[None, :]).astype(jnp.int32)
    before = jnp.cumsum(onehot, axis=0, dtype=jnp.int32) - onehot
    slot_index = jnp.sum(before * onehot, axis=1, dtype=jnp.int32)
    slot_place = flat_owner * capacity + slot_index
    every_emb = lax.all_gather(emb_pass, "dp", axis=0, tiled=True)
    rows_for_me = lax.all_to_all(
        served_rows, "dp", split_axis=1, concat_axis=0, tiled=True
    ).reshape(owners * capacity)
    neg_rows = jnp.take(rows_for_me, slot_place, axis=0)
    neg_emb = jnp.take(every_emb, flat_owner * row_count + neg_rows, axis=0)
    neg_emb = neg_emb.reshape(row_count, negatives, column_width)
    pre_query, unit_query, inv_query = encode(query_states, w_in, w_out)
    emb_query = own_columns(unit_query).astype(jnp.bfloat16)
    pos_part = jnp.einsum("qd,qd->q", emb_query, emb_pass, preferred_element_type=jnp.float32)
    neg_part = jnp.einsum("qd,qnd->qn", emb_query, neg_emb, preferred_element_type=jnp.float32)
    pos_score, neg_score = lax.psum((pos_part, neg_part), "mp")
    exp_pos = jnp.exp(logit_scale * pos_score)
    exp_neg = neg_mask.astype(jnp.float32) * jnp.exp(logit_scale * neg_score)
    denominator = exp_pos + jnp.sum(exp_neg, axis=1)
    factor = loss_scale * logit_scale
    grad_pos = factor * (exp_pos / denominator - 1.0)
    grad_neg = factor * exp_neg / denominator[:, None]
    query_values = emb_query.astype(jnp.float32)
    grad_query_emb = grad_pos[:, None] * emb_pass.astype(jnp.float32) + jnp.sum(
        grad_neg[:, :, None] * neg_emb.astype(jnp.float32), axis=1
    )
    slot_terms = (
        (grad_neg[:, :, None] * query_values[:, None, :])
        .astype(jnp.bfloat16)
        .reshape(-1, column_width)
    )
    outgoing_grad = (
        jnp.zeros((owners * capacity, column_width), jnp.bfloat16).at[slot_place].set(slot_terms)
    )
    returned = lax.all_to_all(
        outgoing_grad.reshape(owners, capacity, column_width),
        "dp",
        split_axis=0,
        concat_axis=0,
        tiled=True,
    )
    grad_query_states = decode(grad_query_emb, pre_query, unit_query, inv_query, w_in, w_out)
    gathered_back = (
        jnp.zeros((row_count, column_width), jnp.float32)
        .at[served.reshape(-1)]
        .add(returned.reshape(-1, column_width).astype(jnp.float32))
    )
    grad_pass_emb = grad_pos[:, None] * query_values + gathered_back
    grad_passage_states = decode(grad_pass_emb, pre_pass, unit_pass, inv_pass, w_in, w_out)
    return (grad_query_states, grad_passage_states)


query_bits, pass_bits = (8, 1), (4, 2)


def offsets(bits):
    found = [0]
    for bit in bits:
        found = found + [at | bit for at in found]
    return found


query_at, pass_at = offsets(query_bits), offsets(pass_bits)


def swap(values, axis, bit):
    size = lax.axis_size(axis)
    return lax.ppermute(values, axis, [(i, i ^ bit) for i in range(size)])


def gather_blocks(block, bits):
    blocks = [block]
    for bit in bits:
        blocks = blocks + [swap(values, "dp", bit) for values in blocks]
    return blocks


def halves(first, values):
    width = values.shape[1] // 2
    left, right = values[:, :width], values[:, width:]
    return jnp.where(first, left, right), jnp.where(first, right, left)


def eye_of(size):
    return (
        lax.broadcasted_iota(jnp.int32, (size, size), 0)
        == lax.broadcasted_iota(jnp.int32, (size, size), 1)
    ).astype(f32)


def local(kernel, name, outs, operands, mebibytes=1, scratch=(), scalars=(), aliases=None):
    return pl.pallas_call(
        kernel,
        in_specs=[smem] * len(scalars) + [vmem] * len(operands),
        out_specs=[vmem] * len(outs),
        out_shape=[pltpu.VMEM(shape, dtype) for shape, dtype in outs],
        scratch_shapes=list(scratch),
        input_output_aliases=aliases or {},
        compiler_params=pltpu.CompilerParams(vmem_limit_bytes=mebibytes << 20),
        cost_estimate=pl.CostEstimate(flops=1, bytes_accessed=1, transcendentals=0),
        name=name,
    )(*scalars, *[pltpu.with_memory_space_constraint(x, pltpu.VMEM) for x in operands])


def encode_far_kernel(
    tile, me, place, scale, xq, xp, w_in, w_out,
    send_q, send_p, states, hidden, pre_act, scale_out, w_in_kept, w_out_far, total, sems,
):
    rows = xq.shape[0]
    tiles = w_in.shape[1] // tile
    half = w_out_far.shape[1]
    far = pl.ds(pl.multiple_of((1 - me[0]) * half, 128), half)
    slices = [slice(t * tile, (t + 1) * tile) for t in range(tiles)]
    copies = [
        pltpu.make_async_copy(xq, states.at[:rows, :], sems.at[0]),
        pltpu.make_async_copy(xp, states.at[rows:, :], sems.at[1]),
    ]
    for t, at in enumerate(slices):
        copies.append(pltpu.make_async_copy(w_in.at[:, at], w_in_kept.at[:, at], sems.at[2 + t]))
    for t, at in enumerate(slices):
        copies.append(
            pltpu.make_async_copy(w_out.at[at, far], w_out_far.at[at, :], sems.at[2 + tiles + t])
        )
    for copy in copies:
        copy.start()
    scale_out[...] = jnp.zeros_like(scale_out) + scale[0] * logit_scale

    def up(t):
        copies[2 + t].wait()
        return jnp.dot(states[...], w_in_kept[:, slices[t]], preferred_element_type=f32)

    def down(t):
        copies[2 + tiles + t].wait()
        return jnp.dot(hidden[:, slices[t]], w_out_far[slices[t], :], preferred_element_type=f32)

    copies[0].wait()
    copies[1].wait()
    for t, at in enumerate(slices):
        pre = up(t)
        pre_act[:, at] = pre
        cdf = 0.5 * (1.0 + lax.erf(pre * root_half))
        hidden[:, at] = (pre * cdf).astype(bf16)
    for t in range(tiles):
        part = down(t)
        if t == 0:
            total[...] = part
        elif t < tiles - 1:
            total[...] += part
        else:
            part = total[...] + part
    send_q[...] = part[:rows].astype(bf16)
    send_p[...] = part[rows:].astype(bf16)


def in_hbm(*values):
    return [pltpu.with_memory_space_constraint(x, pltpu.HBM) for x in values]


def encode_far(me, place, scale, xq, xp, w_in, w_out):
    rows, width = xq.shape
    hidden = w_in.shape[1]
    tile = min(512, hidden)
    half = (rows, width // 2)
    return pl.pallas_call(
        functools.partial(encode_far_kernel, tile),
        in_specs=[smem] * 3 + [hbm] * 4,
        out_specs=[vmem] * 8,
        out_shape=[
            pltpu.VMEM(half, bf16),
            pltpu.VMEM(half, bf16),
            pltpu.VMEM((2 * rows, width), bf16),
            pltpu.VMEM((2 * rows, hidden), bf16),
            pltpu.VMEM((2 * rows, hidden), f32),
            pltpu.VMEM((8, rows), f32),
            pltpu.VMEM(w_in.shape, bf16),
            pltpu.VMEM((hidden, width // 2), bf16),
        ],
        scratch_shapes=[
            pltpu.VMEM((2 * rows, width // 2), f32),
            pltpu.SemaphoreType.DMA((2 + 2 * (hidden // tile),)),
        ],
        compiler_params=pltpu.CompilerParams(vmem_limit_bytes=8 << 20),
        name="encode_far",
    )(me, place, scale, *in_hbm(xq, xp, w_in, w_out))


def encode_near_kernel(
    tile, me, w_out, owner, mask, served, hidden, states,
    own_q, own_p, w_out_near, slots_out, served_out, total, owner_held, mask_held, served_held, sems,
):
    rows, half = own_q.shape
    tiles = hidden.shape[1] // tile
    near = pl.ds(pl.multiple_of(me[0] * half, 128), half)
    copies = []
    for t in range(tiles):
        at = slice(t * tile, (t + 1) * tile)
        copies.append(pltpu.make_async_copy(w_out.at[at, near], w_out_near.at[at, :], sems.at[t]))
    numbers = [
        pltpu.make_async_copy(owner, owner_held, sems.at[tiles]),
        pltpu.make_async_copy(mask, mask_held, sems.at[tiles + 1]),
        pltpu.make_async_copy(served, served_held, sems.at[tiles + 2]),
    ]
    for copy in numbers + copies:
        copy.start()
    total[...] = halves(me[0] == 0, states[...].astype(f32))[0]
    for copy in numbers:
        copy.wait()
    owners = slots_out.shape[0]
    down = lax.broadcasted_iota(jnp.int32, (owners, rows), 0)
    named = jnp.zeros((owners, rows), f32)
    live = jnp.zeros((owners, rows), f32)
    for j in range(owner.shape[0]):
        hit = (owner_held[j : j + 1, :] == down).astype(f32)
        named = named + hit
        live = live + hit * mask_held[j : j + 1, :].astype(f32)
    earlier = lax.broadcasted_iota(jnp.int32, (rows, rows), 0) < lax.broadcasted_iota(
        jnp.int32, (rows, rows), 1
    )
    slot = jnp.dot(named.astype(bf16), earlier.astype(f32).astype(bf16), preferred_element_type=f32)
    slots_out[...] = jnp.where(live > 0.5, slot, -1.0).astype(bf16)
    served_out[...] = served_held[0].astype(f32).astype(bf16)
    for t in range(tiles):
        at = slice(t * tile, (t + 1) * tile)
        copies[t].wait()
        total[...] += jnp.dot(hidden[:, at], w_out_near[at, :], preferred_element_type=f32)
    own_q[...] = total[:rows, :]
    own_p[...] = total[rows:, :]


def encode_near(me, w_out, owner, mask, served, hidden, states):
    rows, width = states.shape[0] // 2, states.shape[1]
    owners = served.shape[1]
    tile = min(512, hidden.shape[1])
    half = (rows, width // 2)
    return pl.pallas_call(
        functools.partial(encode_near_kernel, tile),
        in_specs=[smem] + [hbm] * 4 + [vmem] * 2,
        out_specs=[vmem] * 5,
        out_shape=[
            pltpu.VMEM(half, f32),
            pltpu.VMEM(half, f32),
            pltpu.VMEM((w_out.shape[0], width // 2), bf16),
            pltpu.VMEM((owners, rows), bf16),
            pltpu.VMEM((owners, served.shape[2]), bf16),
        ],
        scratch_shapes=[
            pltpu.VMEM((2 * rows, width // 2), f32),
            pltpu.VMEM(owner.T.shape, jnp.int32),
            pltpu.VMEM(mask.T.shape, jnp.int32),
            pltpu.VMEM(served.shape, jnp.int32),
            pltpu.SemaphoreType.DMA((hidden.shape[1] // tile + 3,)),
        ],
        compiler_params=pltpu.CompilerParams(vmem_limit_bytes=3 << 20),
        cost_estimate=pl.CostEstimate(flops=1, bytes_accessed=1, transcendentals=0),
        name="encode_near",
    )(
        me,
        *in_hbm(w_out, owner.T, mask.T, served),
        *[pltpu.with_memory_space_constraint(x, pltpu.VMEM) for x in (hidden, states)],
    )


def slope_kernel(pre_act, slope):
    step = 32

    def body(n, carry):
        at = pl.ds(pl.multiple_of(n * step, step), step)
        slope[at, :] = gelu_slope(pre_act[at, :]).astype(bf16)
        return carry

    lax.fori_loop(0, pre_act.shape[0] // step, body, 0)


def flip_kernel(weights, out):
    rows, columns = weights.shape
    size = 256
    eye = eye_of(size).astype(bf16)
    for i in range(0, rows, size):
        for j in range(0, columns, size):
            out[j : j + size, i : i + size] = lax.dot_general(
                eye, weights[i : i + size, j : j + size], nt, preferred_element_type=f32
            ).astype(bf16)


def flip(weights, name):
    return local(flip_kernel, name, [(weights.shape[::-1], bf16)], (weights,), 2)[0]


def flip_rows_kernel(far, me, weights, out):
    half, columns = out.shape[1], out.shape[0]
    size = 256
    eye = eye_of(size).astype(bf16)
    first = (1 - me[0] if far else me[0]) * half
    for i in range(0, half, size):
        rows = pl.ds(pl.multiple_of(first + i, size), size)
        for j in range(0, columns, size):
            out[j : j + size, i : i + size] = lax.dot_general(
                eye, weights[rows, j : j + size], nt, preferred_element_type=f32
            ).astype(bf16)


def flip_rows(me, weights, far, name):
    out = ((weights.shape[1], weights.shape[0] // 2), bf16)
    return local(functools.partial(flip_rows_kernel, far), name, [out], (weights,), 2, scalars=[me])[0]


def pack_kernel(own, other, numbers, *refs):
    out = refs[-1]
    rows = own.shape[0]
    out[:rows, :] = (own[...] + other[...].astype(f32)).astype(bf16)
    out[rows:, :] = jnp.zeros((out.shape[0] - rows, out.shape[1]), bf16)
    out[rows:, : numbers.shape[1]] = numbers[...]


def pack(own, other, numbers, *after):
    shape = (own.shape[0] + numbers.shape[0], own.shape[1])
    return local(pack_kernel, "pack", [(shape, bf16)], (own, other, numbers, *after))[0]


def score_block(a, owners, rows, place, ref, q_all, slots, table, valid, pick, p_all, served):
    npass = len(pass_at)
    p_all[a * rows : (a + 1) * rows, :] = ref[:rows, :]
    served[...] = ref[rows:, :rows].astype(f32)
    eye = eye_of(rows)
    down = lax.broadcasted_iota(jnp.int32, (rows, rows), 0).astype(f32)
    part = ref[:rows, :]
    block = part.astype(f32)
    square = jnp.sum(block * block, axis=1, keepdims=True)
    table[2 * npass + 2 : 2 * npass + 3, a * rows : (a + 1) * rows] = jnp.sum(
        eye * square, axis=0, keepdims=True
    )
    scores = lax.dot_general(part, q_all[...], nt, preferred_element_type=f32)
    if a == 0:
        table[2 * npass + 1 : 2 * npass + 2, :rows] = jnp.sum(
            eye * scores[:, :rows], axis=0, keepdims=True
        )
    for b, at in enumerate(query_at):
        lanes = slice(b * rows, (b + 1) * rows)
        row_of = served[pl.ds(place[0] ^ at, 1), :]
        slot_of = slots[pl.ds(b * owners + (place[0] ^ pass_at[a]), 1), :]
        by_slot = (down == row_of).astype(f32).astype(bf16)
        by_query = (down == slot_of).astype(f32).astype(bf16)
        chosen = jnp.dot(by_slot, by_query, preferred_element_type=f32)
        table[a : a + 1, lanes] = jnp.sum(chosen * scores[:, lanes], axis=0, keepdims=True)
        table[npass + a : npass + a + 1, lanes] = jnp.sum(chosen * square, axis=0, keepdims=True)
        valid[a : a + 1, lanes] = (slot_of >= 0.0).astype(f32)
        pick[a * rows : (a + 1) * rows, lanes] = chosen.astype(bf16)


def score_early_kernel(owners, rows, place, *refs):
    nq, npass = len(query_at), len(pass_at)
    q_refs, p_refs = refs[:nq], refs[nq : nq + npass - 1]
    table, valid, pick, p_all, q_all, slots = refs[-7:-1]
    served = refs[-1]
    table[...] = jnp.zeros_like(table)
    for n, ref in enumerate(q_refs):
        lanes = slice(n * rows, (n + 1) * rows)
        q_all[lanes, :] = ref[:rows, :]
        slots[n * owners : (n + 1) * owners, :] = ref[rows:, :rows].astype(f32)
        block = ref[:rows, :].astype(f32)
        square = jnp.sum(block * block, axis=1, keepdims=True)
        table[2 * npass : 2 * npass + 1, lanes] = jnp.sum(
            eye_of(rows) * square, axis=0, keepdims=True
        )
    for a, ref in enumerate(p_refs):
        score_block(a, owners, rows, place, ref, q_all, slots, table, valid, pick, p_all, served)


def score_last_kernel(owners, rows, place, ref, q_all, slots, *refs):
    table, valid, pick, p_all, served = refs[-5:]
    last = len(pass_at) - 1
    score_block(last, owners, rows, place, ref, q_all, slots, table, valid, pick, p_all, served)


def score(place, q_blocks, p_blocks, rows, owners, *after):
    nq, npass = len(query_at), len(pass_at)
    width = q_blocks[0].shape[1]
    outs = [
        ((-(-(2 * npass + 3) // 8) * 8, nq * rows), f32),
        ((8, nq * rows), f32),
        ((npass * rows, nq * rows), bf16),
        ((npass * rows, width), bf16),
    ]
    scratch = [pltpu.VMEM((owners, rows), f32)]
    *parts, q_all, slots = local(
        functools.partial(score_early_kernel, owners, rows),
        "score_early",
        outs + [((nq * rows, width), bf16), ((nq * owners, rows), f32)],
        (*q_blocks, *p_blocks[:-1], *after),
        3,
        scratch,
        [place],
    )
    parts = local(
        functools.partial(score_last_kernel, owners, rows),
        "score_last",
        outs,
        (p_blocks[-1], q_all, slots, *parts),
        3,
        scratch,
        [place],
        {4 + n: n for n in range(len(parts))},
    )
    return (*parts, q_all)


def weigh_kernel(rows, table, other, valid, *refs):
    coefs, sums = refs[-2:]
    nq, npass = len(query_at), len(pass_at)
    full = table[...] + other[...]
    raw, square = full[:npass], full[npass : 2 * npass]
    inv_q = lax.rsqrt(full[2 * npass : 2 * npass + 1] + norm_eps)
    inv_pass = lax.rsqrt(full[2 * npass + 2 : 2 * npass + 3] + norm_eps)
    inv_neg = lax.rsqrt(square + norm_eps)
    neg_score = raw * inv_q * inv_neg
    exp_neg = valid[:npass] * jnp.exp(logit_scale * neg_score)
    pos_score = full[2 * npass + 1 : 2 * npass + 2] * inv_q * inv_pass
    coefs[...] = jnp.zeros_like(coefs)
    coefs[:npass] = exp_neg
    coefs[npass : 2 * npass] = exp_neg * inv_neg
    coefs[2 * npass : 3 * npass] = exp_neg * neg_score
    coefs[3 * npass : 3 * npass + 1] = inv_q
    coefs[3 * npass + 1 : 3 * npass + 2] = inv_pass
    coefs[3 * npass + 2 : 3 * npass + 3] = pos_score
    neg_sum = jnp.sum(exp_neg, axis=0, keepdims=True)
    neg_dot = jnp.sum(exp_neg * neg_score, axis=0, keepdims=True)
    sums[...] = jnp.zeros_like(sums)
    for n in range(nq):
        sums[n : n + 1, :] = neg_sum[:, n * rows : (n + 1) * rows]
        sums[2 * nq + n : 2 * nq + n + 1, :] = neg_dot[:, n * rows : (n + 1) * rows]
    sums[nq : nq + 1, :] = jnp.exp(logit_scale * pos_score[:, :rows])


def weigh(table, other, valid, rows, *after):
    nq, npass = len(query_at), len(pass_at)
    return local(
        functools.partial(weigh_kernel, rows),
        "weigh",
        [((-(-(3 * npass + 3) // 8) * 8, nq * rows), f32), ((-(-3 * nq // 8) * 8, rows), f32)],
        (table, other, valid, *after),
    )


def add_sums_kernel(bit, sums, other, *refs):
    out = refs[-1]
    nq = len(query_at)
    out[...] = sums[...]
    for n, at in enumerate(query_at):
        m = query_at.index(at ^ bit)
        for first in (0, nq, 2 * nq):
            k, l = first + n, first + m
            out[k : k + 1, :] = sums[k : k + 1, :] + other[l : l + 1, :]


def exchange_sums(sums, bit, *after):
    kernel = functools.partial(add_sums_kernel, bit)
    return local(kernel, "add_sums", [(sums.shape, f32)], (sums, swap(sums, "dp", bit), *after))[0]


def spread_query_kernel(rows, far, coefs, pick, p_all, *refs):
    out = refs[-1]
    npass = len(pass_at)
    passages = p_all[...]
    blocks = [b for b, at in enumerate(query_at) if bool(at & query_bits[1]) == far]
    for n, b in enumerate(blocks):
        lanes = slice(b * rows, (b + 1) * rows)
        pieces = []
        for a in range(npass):
            piece = pick[a * rows : (a + 1) * rows, lanes].astype(f32)
            piece = piece * coefs[npass + a : npass + a + 1, lanes]
            pieces.append(piece.T.astype(bf16))
        weights = jnp.concatenate(pieces, axis=1)
        values = jnp.dot(weights, passages, preferred_element_type=f32)
        out[n * rows : (n + 1) * rows, :] = values.astype(out.dtype)


def spread_query(coefs, pick, p_all, rows, far, *after):
    half = (len(query_at) // 2 * rows, p_all.shape[1])
    return local(
        functools.partial(spread_query_kernel, rows, far),
        "spread_query",
        [(half, bf16 if far else f32)],
        (coefs, pick, p_all, *after),
        3,
    )[0]


def column_of(eye, row):
    return jnp.sum(eye * row, axis=1, keepdims=True)


def spread_pass_kernel(rows, blocks, scale, coefs, sums, pick, q_all, p_all, *outs):
    nq, npass = len(query_at), len(pass_at)
    eye = eye_of(rows)
    share = scale[:nq] / (sums[:nq] + sums[nq : 2 * nq])
    pos = -share[:1] * sums[:1]
    share = jnp.concatenate([share[n : n + 1] for n in range(nq)], axis=1)
    scaled = share * coefs[3 * npass : 3 * npass + 1]
    queries = q_all[...]
    for out, a in zip(outs, blocks):
        at = slice(a * rows, (a + 1) * rows)
        chosen = pick[at, :]
        weights = chosen.astype(f32) * (coefs[a : a + 1] * scaled)
        product = share * coefs[2 * npass + a : 2 * npass + a + 1]
        high = product.astype(bf16).astype(f32)
        parts = jnp.concatenate([high, product - high, jnp.zeros((14, nq * rows), f32)], axis=0)
        dots = lax.dot_general(parts.astype(bf16), chosen, nt, preferred_element_type=f32)
        dot = jnp.sum(dots, axis=0, keepdims=True)
        if a == 0:
            own = pos * coefs[3 * npass : 3 * npass + 1, :rows]
            weights = jnp.concatenate([weights[:, :rows] + eye * own, weights[:, rows:]], axis=1)
            dot = dot + pos * coefs[3 * npass + 2 : 3 * npass + 3, :rows]
        values = jnp.dot(weights.astype(bf16), queries, preferred_element_type=f32)
        along = column_of(eye, dot * coefs[3 * npass + 1 : 3 * npass + 2, at])
        values = values - along * p_all[at, :].astype(f32)
        out[...] = values.astype(out.dtype)


def spread_pass(scale, coefs, sums, pick, q_all, p_all, rows, blocks, dtype):
    block = (rows, q_all.shape[1])
    return local(
        functools.partial(spread_pass_kernel, rows, blocks),
        "spread_pass",
        [(block, dtype)] * len(blocks),
        (scale, coefs, sums, pick, q_all, p_all),
        3,
    )


def fold_query_kernel(own, other, kept, sent):
    rows = kept.shape[0]
    total = own[...] + other[...].astype(f32)
    kept[...] = total[:rows]
    sent[...] = total[rows:].astype(bf16)


def fold_query(own, other):
    half = (own.shape[0] // 2, own.shape[1])
    return local(fold_query_kernel, "fold_query", [(half, f32), (half, bf16)], (own, other))


def grad_query_kernel(own, other, scale, sums, coefs, raw, raw_pass, grad, rounded):
    nq, npass = len(query_at), len(pass_at)
    rows = own.shape[0]
    eye = eye_of(rows)
    inv_norm = coefs[3 * npass : 3 * npass + 1, :rows]
    share = scale[:1] / (sums[:1] + sums[nq : nq + 1])
    pos = sums[:1] * coefs[3 * npass + 1 : 3 * npass + 2, :rows]
    dot = share * (sums[2 * nq : 2 * nq + 1] - sums[:1] * coefs[3 * npass + 2 : 3 * npass + 3, :rows])
    total = own[...] + other[...].astype(f32)
    total = total - column_of(eye, pos) * raw_pass[:rows, :].astype(f32)
    values = column_of(eye, share * inv_norm) * total
    values = values - column_of(eye, dot * inv_norm * inv_norm) * raw[:rows, :].astype(f32)
    grad[...] = values
    rounded[...] = values.astype(bf16)


def grad_pass_kernel(own, first, second, third, coefs, after, grad, rounded):
    npass = len(pass_at)
    rows = own.shape[0]
    inv_norm = column_of(eye_of(rows), coefs[3 * npass + 1 : 3 * npass + 2, :rows])
    others = first[...].astype(f32) + second[...].astype(f32) + third[...].astype(f32)
    values = inv_norm * (own[...] + others)
    grad[...] = values
    rounded[...] = values.astype(bf16)


def grad_out(kernel, name, own, operands):
    return local(kernel, name, [(own.shape, f32), (own.shape, bf16)], (own, *operands))


def decode_near_kernel(tile, mine, w_out, out):
    for t in range(w_out.shape[1] // tile):
        at = slice(t * tile, (t + 1) * tile)
        out[:, at] = jnp.dot(mine[...], w_out[:, at], preferred_element_type=f32)


def decode_far_kernel(tower, tile, near, theirs, slope, w_out, w_in, *refs):
    grad_pre, send = refs[-2:]
    rows = theirs.shape[0]
    for t in range(w_out.shape[1] // tile):
        at = slice(t * tile, (t + 1) * tile)
        hidden = near[:, at] + jnp.dot(theirs[...], w_out[:, at], preferred_element_type=f32)
        grad_pre[:, at] = (hidden * slope[tower * rows : (tower + 1) * rows, at].astype(f32)).astype(bf16)
    send[...] = jnp.dot(grad_pre[...], w_in[...], preferred_element_type=f32).astype(bf16)


def decode_own_kernel(grad, grad_pre, w_in, *refs):
    refs[-1][...] = grad[...] + jnp.dot(grad_pre[...], w_in[...], preferred_element_type=f32)


def decode_far(rounded, slope, tower, w_out_near, w_out_far, w_in_far, *after):
    rows, hidden = rounded.shape[0], slope.shape[1]
    tile = min(512, hidden)
    near = local(
        functools.partial(decode_near_kernel, tile),
        "decode_near",
        [((rows, hidden), f32)],
        (rounded, w_out_near),
        2,
    )[0]
    return local(
        functools.partial(decode_far_kernel, tower, tile),
        "decode_far",
        [((rows, hidden), bf16), (rounded.shape, bf16)],
        (near, swap(rounded, "mp", 1), slope, w_out_far, w_in_far, *after),
        2,
    )


def decode_own(grad, grad_pre, w_in_near, *after):
    return local(
        decode_own_kernel, "decode_own", [(grad.shape, f32)], (grad, grad_pre, w_in_near, *after), 2
    )[0]


def finish_kernel(own, other, *refs):
    out, done = refs[-2:]
    out[...] = (own[...] + other[...].astype(f32)).astype(bf16)
    done[...] = jnp.zeros_like(done)


def finish(own, other, name, *after):
    return pl.pallas_call(
        finish_kernel,
        in_specs=[vmem] * (2 + len(after)),
        out_specs=[vmem] * 2,
        out_shape=[jax.ShapeDtypeStruct(own.shape, bf16), pltpu.VMEM((8, 128), f32)],
        compiler_params=pltpu.CompilerParams(vmem_limit_bytes=1 << 20),
        name=name,
    )(*[pltpu.with_memory_space_constraint(x, pltpu.VMEM) for x in (own, other, *after)])


def paired_shards(
    query_states, passage_states, w_in, w_out, neg_owner, neg_mask, served_rows, loss_scale
):
    rows = query_states.shape[0]
    owners = served_rows.shape[1]
    me = lax.axis_index("mp").astype(jnp.int32).reshape(1)
    place = lax.axis_index("dp").astype(jnp.int32).reshape(1)
    send_q, send_p, states, hidden, pre_act, scale, w_in, w_out_far = encode_far(
        me, place, loss_scale.reshape(1), query_states, passage_states, w_in, w_out
    )
    own_q, own_p, w_out_near, slots, served = encode_near(
        me, w_out, neg_owner, neg_mask, served_rows, hidden, states
    )
    slope = local(slope_kernel, "slope", [(pre_act.shape, bf16)], (pre_act,))[0]
    w_in_far = flip_rows(me, w_in, True, "flip_in_far")
    w_in_near = flip_rows(me, w_in, False, "flip_in_near")
    w_out_far, w_out_near = flip(w_out_far, "flip_out_far"), flip(w_out_near, "flip_out_near")
    raw_q = pack(own_q, swap(send_q, "mp", 1), slots)
    raw_p = pack(own_p, swap(send_p, "mp", 1), served)
    q_blocks = gather_blocks(raw_q, query_bits)
    p_blocks = gather_blocks(raw_p, pass_bits)

    table, valid, pick, p_all, q_all = score(
        place, q_blocks, p_blocks, rows, owners, w_out_near, slope, w_in_far
    )
    coefs, sums = weigh(table, swap(table, "mp", 1), valid, rows, w_out_far, w_in_near)
    sent_q = spread_query(coefs, pick, p_all, rows, True)
    sums = exchange_sums(sums, query_bits[1], sent_q)
    kept_q = spread_query(coefs, pick, p_all, rows, False)
    kept_q, sent_q = fold_query(kept_q, swap(sent_q, "dp", query_bits[1]))
    sums = exchange_sums(sums, query_bits[0], sent_q)
    operands = (scale, coefs, sums, pick, q_all, p_all, rows)
    sent_p = spread_pass(*operands, tuple(range(1, len(pass_at))), bf16)
    kept_p = spread_pass(*operands, (0,), f32)[0]
    others_p = [swap(sent_p[n - 1], "dp", pass_at[n]) for n in (3, 2, 1)]
    grad_q, round_q = grad_out(
        grad_query_kernel,
        "grad_query",
        kept_q,
        (swap(sent_q, "dp", query_bits[0]), scale, sums, coefs, raw_q, raw_p),
    )
    grad_p, round_p = grad_out(
        grad_pass_kernel,
        "grad_pass",
        kept_p,
        (*others_p, coefs, round_q),
    )
    pre_q, send_q = decode_far(round_q, slope, 0, w_out_near, w_out_far, w_in_far)
    pre_p, send_p = decode_far(round_p, slope, 1, w_out_near, w_out_far, w_in_far, send_q)
    own_q = decode_own(grad_q, pre_q, w_in_near, send_p)
    own_p = decode_own(grad_p, pre_p, w_in_near)
    out_q, done_q = finish(own_q, swap(send_q, "mp", 1), "out_query")
    out_p, _ = finish(own_p, swap(send_p, "mp", 1), "out_pass", done_q)
    return (out_q, out_p)


def solution(mesh):
    in_specs = (
        P("dp", None),
        P("dp", None),
        P(None, "mp"),
        P("mp", None),
        P("dp", None),
        P("dp", None),
        P("dp", None, None),
        P(),
    )
    out_specs = (P("dp", "mp"), P("dp", "mp"))
    gathered = len(query_at) * len(pass_at)
    paired = mesh.shape["mp"] == 2 and mesh.shape["dp"] == gathered
    shards = paired_shards if paired else general_shards
    return jax.shard_map(shards, mesh=mesh, in_specs=in_specs, out_specs=out_specs, check_vma=False)
```

```python
import functools

import jax
import jax.numpy as jnp
from jax import lax
from jax.experimental import pallas as pl
from jax.experimental.pallas import tpu as pltpu
from jax.sharding import PartitionSpec as P

logit_scale = 50.0
norm_eps = 1e-06
root_half = 0.7071067811865476
inv_root_two_pi = 0.3989422804014327
f32, bf16 = jnp.float32, jnp.bfloat16
nt = (((1,), (1,)), ((), ()))
tn = (((0,), (0,)), ((), ()))
vmem = pl.BlockSpec(memory_space=pltpu.VMEM)
smem = pl.BlockSpec(memory_space=pltpu.SMEM)
hbm = pl.BlockSpec(memory_space=pltpu.HBM)


def gelu_value(values):
    return 0.5 * values * (1.0 + lax.erf(values * root_half))


def gelu_slope(values):
    return (
        0.5 * (1.0 + lax.erf(values * root_half))
        + values * jnp.exp(-0.5 * values * values) * inv_root_two_pi
    )


def own_columns(values):
    column_width = values.shape[1] // lax.axis_size("mp")
    return lax.dynamic_slice_in_dim(values, lax.axis_index("mp") * column_width, column_width, 1)


def encode(states, w_in, w_out):
    pre_act = jnp.dot(states, w_in, preferred_element_type=jnp.float32)
    hidden = gelu_value(pre_act).astype(jnp.bfloat16)
    partial_out = jnp.dot(hidden, w_out, preferred_element_type=jnp.float32)
    mixed_sum = lax.psum(partial_out, "mp")
    output = states.astype(jnp.float32) + mixed_sum
    inv_norm = lax.rsqrt(jnp.sum(output * output, axis=1, keepdims=True) + norm_eps)
    return (pre_act, output * inv_norm, inv_norm)


def decode(grad_part, pre_act, unit_rows, inv_norm, w_in, w_out):
    grad_emb = lax.all_gather(grad_part.astype(jnp.bfloat16), "mp", axis=1, tiled=True).astype(
        grad_part.dtype
    )
    grad_out = inv_norm * (
        grad_emb - unit_rows * jnp.sum(unit_rows * grad_emb, axis=1, keepdims=True)
    )
    grad_hidden = lax.dot_general(
        grad_out.astype(jnp.bfloat16), w_out, nt, preferred_element_type=jnp.float32
    )
    grad_pre = (grad_hidden * gelu_slope(pre_act)).astype(jnp.bfloat16)
    partial_in = lax.dot_general(grad_pre, w_in, nt, preferred_element_type=jnp.float32)
    summed = lax.psum_scatter(
        partial_in.astype(jnp.bfloat16), "mp", scatter_dimension=1, tiled=True
    ).astype(jnp.float32)
    return (summed + own_columns(grad_out)).astype(jnp.bfloat16)


def general_shards(
    query_states, passage_states, w_in, w_out, neg_owner, neg_mask, served_rows, loss_scale
):
    owners = lax.axis_size("dp")
    row_count = query_states.shape[0]
    negatives = neg_owner.shape[1]
    capacity = served_rows.shape[2]
    pre_pass, unit_pass, inv_pass = encode(passage_states, w_in, w_out)
    emb_pass = own_columns(unit_pass).astype(jnp.bfloat16)
    column_width = emb_pass.shape[1]
    served = served_rows[0]
    flat_owner = neg_owner.reshape(-1)
    onehot = (flat_owner[:, None] == jnp.arange(owners, dtype=jnp.int32)[None, :]).astype(jnp.int32)
    before = jnp.cumsum(onehot, axis=0, dtype=jnp.int32) - onehot
    slot_index = jnp.sum(before * onehot, axis=1, dtype=jnp.int32)
    slot_place = flat_owner * capacity + slot_index
    every_emb = lax.all_gather(emb_pass, "dp", axis=0, tiled=True)
    rows_for_me = lax.all_to_all(
        served_rows, "dp", split_axis=1, concat_axis=0, tiled=True
    ).reshape(owners * capacity)
    neg_rows = jnp.take(rows_for_me, slot_place, axis=0)
    neg_emb = jnp.take(every_emb, flat_owner * row_count + neg_rows, axis=0)
    neg_emb = neg_emb.reshape(row_count, negatives, column_width)
    pre_query, unit_query, inv_query = encode(query_states, w_in, w_out)
    emb_query = own_columns(unit_query).astype(jnp.bfloat16)
    pos_part = jnp.einsum("qd,qd->q", emb_query, emb_pass, preferred_element_type=jnp.float32)
    neg_part = jnp.einsum("qd,qnd->qn", emb_query, neg_emb, preferred_element_type=jnp.float32)
    pos_score, neg_score = lax.psum((pos_part, neg_part), "mp")
    exp_pos = jnp.exp(logit_scale * pos_score)
    exp_neg = neg_mask.astype(jnp.float32) * jnp.exp(logit_scale * neg_score)
    denominator = exp_pos + jnp.sum(exp_neg, axis=1)
    factor = loss_scale * logit_scale
    grad_pos = factor * (exp_pos / denominator - 1.0)
    grad_neg = factor * exp_neg / denominator[:, None]
    query_values = emb_query.astype(jnp.float32)
    grad_query_emb = grad_pos[:, None] * emb_pass.astype(jnp.float32) + jnp.sum(
        grad_neg[:, :, None] * neg_emb.astype(jnp.float32), axis=1
    )
    slot_terms = (
        (grad_neg[:, :, None] * query_values[:, None, :])
        .astype(jnp.bfloat16)
        .reshape(-1, column_width)
    )
    outgoing_grad = (
        jnp.zeros((owners * capacity, column_width), jnp.bfloat16).at[slot_place].set(slot_terms)
    )
    returned = lax.all_to_all(
        outgoing_grad.reshape(owners, capacity, column_width),
        "dp",
        split_axis=0,
        concat_axis=0,
        tiled=True,
    )
    grad_query_states = decode(grad_query_emb, pre_query, unit_query, inv_query, w_in, w_out)
    gathered_back = (
        jnp.zeros((row_count, column_width), jnp.float32)
        .at[served.reshape(-1)]
        .add(returned.reshape(-1, column_width).astype(jnp.float32))
    )
    grad_pass_emb = grad_pos[:, None] * query_values + gathered_back
    grad_passage_states = decode(grad_pass_emb, pre_pass, unit_pass, inv_pass, w_in, w_out)
    return (grad_query_states, grad_passage_states)


query_bits, pass_bits = (8, 1), (4, 2)


def offsets(bits):
    found = [0]
    for bit in bits:
        found = found + [at | bit for at in found]
    return found


query_at, pass_at = offsets(query_bits), offsets(pass_bits)


def swap(values, axis, bit, odd_bit=None):
    size = lax.axis_size(axis)
    bits = (bit, bit if odd_bit is None else odd_bit)
    return lax.ppermute(values, axis, [(i, i ^ bits[i % 2]) for i in range(size)])


def gather_blocks(block, bits):
    blocks = [block]
    for bit in bits:
        blocks = blocks + [swap(values, "dp", bit) for values in blocks]
    return blocks


def halves(first, values):
    width = values.shape[1] // 2
    left, right = values[:, :width], values[:, width:]
    return jnp.where(first, left, right), jnp.where(first, right, left)


def eye_of(size):
    return (
        lax.broadcasted_iota(jnp.int32, (size, size), 0)
        == lax.broadcasted_iota(jnp.int32, (size, size), 1)
    ).astype(f32)


def local(kernel, name, outs, operands, mebibytes=1, scratch=(), scalars=(), aliases=None):
    return pl.pallas_call(
        kernel,
        in_specs=[smem] * len(scalars) + [vmem] * len(operands),
        out_specs=[vmem] * len(outs),
        out_shape=[pltpu.VMEM(shape, dtype) for shape, dtype in outs],
        scratch_shapes=list(scratch),
        input_output_aliases=aliases or {},
        compiler_params=pltpu.CompilerParams(vmem_limit_bytes=mebibytes << 20),
        cost_estimate=pl.CostEstimate(flops=1, bytes_accessed=1, transcendentals=0),
        name=name,
    )(*scalars, *[pltpu.with_memory_space_constraint(x, pltpu.VMEM) for x in operands])


def encode_far_kernel(
    tile, me, place, scale, xq, xp, w_in, w_out,
    send_q, send_p, states, hidden, pre_act, scale_out, w_in_kept, w_out_far, total, sems,
):
    rows = xq.shape[0]
    tiles = w_in.shape[1] // tile
    half = w_out_far.shape[1]
    far = pl.ds(pl.multiple_of((1 - me[0]) * half, 128), half)
    slices = [slice(t * tile, (t + 1) * tile) for t in range(tiles)]
    copies = [
        pltpu.make_async_copy(xq, states.at[:rows, :], sems.at[0]),
        pltpu.make_async_copy(xp, states.at[rows:, :], sems.at[1]),
    ]
    for t, at in enumerate(slices):
        copies.append(pltpu.make_async_copy(w_in.at[:, at], w_in_kept.at[:, at], sems.at[2 + t]))
    for t, at in enumerate(slices):
        copies.append(
            pltpu.make_async_copy(w_out.at[at, far], w_out_far.at[at, :], sems.at[2 + tiles + t])
        )
    for copy in copies:
        copy.start()
    scale_out[...] = jnp.zeros_like(scale_out) + scale[0] * logit_scale

    def up(t):
        copies[2 + t].wait()
        return jnp.dot(states[...], w_in_kept[:, slices[t]], preferred_element_type=f32)

    def down(t):
        copies[2 + tiles + t].wait()
        return jnp.dot(hidden[:, slices[t]], w_out_far[slices[t], :], preferred_element_type=f32)

    copies[0].wait()
    copies[1].wait()
    for t, at in enumerate(slices):
        pre = up(t)
        pre_act[:, at] = pre
        cdf = 0.5 * (1.0 + lax.erf(pre * root_half))
        hidden[:, at] = (pre * cdf).astype(bf16)
    for t in range(tiles):
        part = down(t)
        if t == 0:
            total[...] = part
        elif t < tiles - 1:
            total[...] += part
        else:
            part = total[...] + part
    send_q[...] = part[:rows].astype(bf16)
    send_p[...] = part[rows:].astype(bf16)


def in_hbm(*values):
    return [pltpu.with_memory_space_constraint(x, pltpu.HBM) for x in values]


def encode_far(me, place, scale, xq, xp, w_in, w_out):
    rows, width = xq.shape
    hidden = w_in.shape[1]
    tile = min(512, hidden)
    half = (rows, width // 2)
    return pl.pallas_call(
        functools.partial(encode_far_kernel, tile),
        in_specs=[smem] * 3 + [hbm] * 4,
        out_specs=[vmem] * 8,
        out_shape=[
            pltpu.VMEM(half, bf16),
            pltpu.VMEM(half, bf16),
            pltpu.VMEM((2 * rows, width), bf16),
            pltpu.VMEM((2 * rows, hidden), bf16),
            pltpu.VMEM((2 * rows, hidden), f32),
            pltpu.VMEM((8, rows), f32),
            pltpu.VMEM(w_in.shape, bf16),
            pltpu.VMEM((hidden, width // 2), bf16),
        ],
        scratch_shapes=[
            pltpu.VMEM((2 * rows, width // 2), f32),
            pltpu.SemaphoreType.DMA((2 + 2 * (hidden // tile),)),
        ],
        compiler_params=pltpu.CompilerParams(vmem_limit_bytes=8 << 20),
        name="encode_far",
    )(me, place, scale, *in_hbm(xq, xp, w_in, w_out))


def encode_near_kernel(
    tile, me, w_out, owner, mask, served, hidden, states,
    own_q, own_p, w_out_near, slots_out, served_out, total, owner_held, mask_held, served_held, sems,
):
    rows, half = own_q.shape
    tiles = hidden.shape[1] // tile
    near = pl.ds(pl.multiple_of(me[0] * half, 128), half)
    copies = []
    for t in range(tiles):
        at = slice(t * tile, (t + 1) * tile)
        copies.append(pltpu.make_async_copy(w_out.at[at, near], w_out_near.at[at, :], sems.at[t]))
    numbers = [
        pltpu.make_async_copy(owner, owner_held, sems.at[tiles]),
        pltpu.make_async_copy(mask, mask_held, sems.at[tiles + 1]),
        pltpu.make_async_copy(served, served_held, sems.at[tiles + 2]),
    ]
    for copy in numbers + copies:
        copy.start()
    total[...] = halves(me[0] == 0, states[...].astype(f32))[0]
    for copy in numbers:
        copy.wait()
    owners = slots_out.shape[0]
    down = lax.broadcasted_iota(jnp.int32, (owners, rows), 0)
    named = jnp.zeros((owners, rows), f32)
    live = jnp.zeros((owners, rows), f32)
    for j in range(owner.shape[0]):
        hit = (owner_held[j : j + 1, :] == down).astype(f32)
        named = named + hit
        live = live + hit * mask_held[j : j + 1, :].astype(f32)
    earlier = lax.broadcasted_iota(jnp.int32, (rows, rows), 0) < lax.broadcasted_iota(
        jnp.int32, (rows, rows), 1
    )
    slot = jnp.dot(named.astype(bf16), earlier.astype(f32).astype(bf16), preferred_element_type=f32)
    slots_out[...] = jnp.where(live > 0.5, slot, -1.0).astype(bf16)
    served_out[...] = served_held[0].astype(f32).astype(bf16)
    for t in range(tiles):
        at = slice(t * tile, (t + 1) * tile)
        copies[t].wait()
        total[...] += jnp.dot(hidden[:, at], w_out_near[at, :], preferred_element_type=f32)
    own_q[...] = total[:rows, :]
    own_p[...] = total[rows:, :]


def encode_near(me, w_out, owner, mask, served, hidden, states):
    rows, width = states.shape[0] // 2, states.shape[1]
    owners = served.shape[1]
    tile = min(512, hidden.shape[1])
    half = (rows, width // 2)
    return pl.pallas_call(
        functools.partial(encode_near_kernel, tile),
        in_specs=[smem] + [hbm] * 4 + [vmem] * 2,
        out_specs=[vmem] * 5,
        out_shape=[
            pltpu.VMEM(half, f32),
            pltpu.VMEM(half, f32),
            pltpu.VMEM((w_out.shape[0], width // 2), bf16),
            pltpu.VMEM((owners, rows), bf16),
            pltpu.VMEM((owners, served.shape[2]), bf16),
        ],
        scratch_shapes=[
            pltpu.VMEM((2 * rows, width // 2), f32),
            pltpu.VMEM(owner.T.shape, jnp.int32),
            pltpu.VMEM(mask.T.shape, jnp.int32),
            pltpu.VMEM(served.shape, jnp.int32),
            pltpu.SemaphoreType.DMA((hidden.shape[1] // tile + 3,)),
        ],
        compiler_params=pltpu.CompilerParams(vmem_limit_bytes=3 << 20),
        cost_estimate=pl.CostEstimate(flops=1, bytes_accessed=1, transcendentals=0),
        name="encode_near",
    )(
        me,
        *in_hbm(w_out, owner.T, mask.T, served),
        *[pltpu.with_memory_space_constraint(x, pltpu.VMEM) for x in (hidden, states)],
    )


def slope_kernel(pre_act, slope):
    step = 32

    def body(n, carry):
        at = pl.ds(pl.multiple_of(n * step, step), step)
        slope[at, :] = gelu_slope(pre_act[at, :]).astype(bf16)
        return carry

    lax.fori_loop(0, pre_act.shape[0] // step, body, 0)


def flip_kernel(weights, out):
    rows, columns = weights.shape
    size = 256
    eye = eye_of(size).astype(bf16)
    for i in range(0, rows, size):
        for j in range(0, columns, size):
            out[j : j + size, i : i + size] = lax.dot_general(
                eye, weights[i : i + size, j : j + size], nt, preferred_element_type=f32
            ).astype(bf16)


def flip(weights, name):
    return local(flip_kernel, name, [(weights.shape[::-1], bf16)], (weights,), 2)[0]


def flip_rows_kernel(far, me, weights, out):
    half, columns = out.shape[1], out.shape[0]
    size = 256
    eye = eye_of(size).astype(bf16)
    first = (1 - me[0] if far else me[0]) * half
    for i in range(0, half, size):
        rows = pl.ds(pl.multiple_of(first + i, size), size)
        for j in range(0, columns, size):
            out[j : j + size, i : i + size] = lax.dot_general(
                eye, weights[rows, j : j + size], nt, preferred_element_type=f32
            ).astype(bf16)


def flip_rows(me, weights, far, name):
    out = ((weights.shape[1], weights.shape[0] // 2), bf16)
    return local(functools.partial(flip_rows_kernel, far), name, [out], (weights,), 2, scalars=[me])[0]


def pack_kernel(own, other, numbers, *refs):
    out = refs[-1]
    rows = own.shape[0]
    out[:rows, :] = (own[...] + other[...].astype(f32)).astype(bf16)
    out[rows:, :] = jnp.zeros((out.shape[0] - rows, out.shape[1]), bf16)
    out[rows:, : numbers.shape[1]] = numbers[...]


def pack(own, other, numbers, *after):
    shape = (own.shape[0] + numbers.shape[0], own.shape[1])
    return local(pack_kernel, "pack", [(shape, bf16)], (own, other, numbers, *after))[0]


def score_block(a, owners, rows, place, ref, q_all, slots, table, valid, pick, p_all, served):
    npass = len(pass_at)
    p_all[a * rows : (a + 1) * rows, :] = ref[:rows, :]
    served[...] = ref[rows:, :rows].astype(f32)
    eye = eye_of(rows)
    down = lax.broadcasted_iota(jnp.int32, (rows, rows), 0).astype(f32)
    part = ref[:rows, :]
    block = part.astype(f32)
    square = jnp.sum(block * block, axis=1, keepdims=True)
    table[2 * npass + 2 : 2 * npass + 3, a * rows : (a + 1) * rows] = jnp.sum(
        eye * square, axis=0, keepdims=True
    )
    scores = lax.dot_general(part, q_all[...], nt, preferred_element_type=f32)
    if a == 0:
        table[2 * npass + 1 : 2 * npass + 2, :rows] = jnp.sum(
            eye * scores[:, :rows], axis=0, keepdims=True
        )
    for b, at in enumerate(query_at):
        lanes = slice(b * rows, (b + 1) * rows)
        row_of = served[pl.ds(place[0] ^ at, 1), :]
        slot_of = slots[pl.ds(b * owners + (place[0] ^ pass_at[a]), 1), :]
        by_slot = (down == row_of).astype(f32).astype(bf16)
        by_query = (down == slot_of).astype(f32).astype(bf16)
        chosen = jnp.dot(by_slot, by_query, preferred_element_type=f32)
        table[a : a + 1, lanes] = jnp.sum(chosen * scores[:, lanes], axis=0, keepdims=True)
        table[npass + a : npass + a + 1, lanes] = jnp.sum(chosen * square, axis=0, keepdims=True)
        valid[a : a + 1, lanes] = (slot_of >= 0.0).astype(f32)
        pick[a * rows : (a + 1) * rows, lanes] = chosen.astype(bf16)


def score_early_kernel(owners, rows, place, *refs):
    nq, npass = len(query_at), len(pass_at)
    q_refs, p_refs = refs[:nq], refs[nq : nq + npass - 1]
    table, valid, pick, p_all, q_all, slots = refs[-7:-1]
    served = refs[-1]
    table[...] = jnp.zeros_like(table)
    for n, ref in enumerate(q_refs):
        lanes = slice(n * rows, (n + 1) * rows)
        q_all[lanes, :] = ref[:rows, :]
        slots[n * owners : (n + 1) * owners, :] = ref[rows:, :rows].astype(f32)
        block = ref[:rows, :].astype(f32)
        square = jnp.sum(block * block, axis=1, keepdims=True)
        table[2 * npass : 2 * npass + 1, lanes] = jnp.sum(
            eye_of(rows) * square, axis=0, keepdims=True
        )
    for a, ref in enumerate(p_refs):
        score_block(a, owners, rows, place, ref, q_all, slots, table, valid, pick, p_all, served)


def score_last_kernel(owners, rows, place, ref, q_all, slots, *refs):
    table, valid, pick, p_all, served = refs[-5:]
    last = len(pass_at) - 1
    score_block(last, owners, rows, place, ref, q_all, slots, table, valid, pick, p_all, served)


def score(place, q_blocks, p_blocks, rows, owners, *after):
    nq, npass = len(query_at), len(pass_at)
    width = q_blocks[0].shape[1]
    outs = [
        ((-(-(2 * npass + 3) // 8) * 8, nq * rows), f32),
        ((8, nq * rows), f32),
        ((npass * rows, nq * rows), bf16),
        ((npass * rows, width), bf16),
    ]
    scratch = [pltpu.VMEM((owners, rows), f32)]
    *parts, q_all, slots = local(
        functools.partial(score_early_kernel, owners, rows),
        "score_early",
        outs + [((nq * rows, width), bf16), ((nq * owners, rows), f32)],
        (*q_blocks, *p_blocks[:-1], *after),
        3,
        scratch,
        [place],
    )
    parts = local(
        functools.partial(score_last_kernel, owners, rows),
        "score_last",
        outs,
        (p_blocks[-1], q_all, slots, *parts),
        3,
        scratch,
        [place],
        {4 + n: n for n in range(len(parts))},
    )
    return (*parts, q_all)


def weigh_kernel(rows, table, other, valid, *refs):
    coefs, sums = refs[-2:]
    nq, npass = len(query_at), len(pass_at)
    full = table[...] + other[...]
    raw, square = full[:npass], full[npass : 2 * npass]
    inv_q = lax.rsqrt(full[2 * npass : 2 * npass + 1] + norm_eps)
    inv_pass = lax.rsqrt(full[2 * npass + 2 : 2 * npass + 3] + norm_eps)
    inv_neg = lax.rsqrt(square + norm_eps)
    neg_score = raw * inv_q * inv_neg
    exp_neg = valid[:npass] * jnp.exp(logit_scale * neg_score)
    pos_score = full[2 * npass + 1 : 2 * npass + 2] * inv_q * inv_pass
    coefs[...] = jnp.zeros_like(coefs)
    coefs[:npass] = exp_neg
    coefs[npass : 2 * npass] = exp_neg * inv_neg
    coefs[2 * npass : 3 * npass] = exp_neg * neg_score
    coefs[3 * npass : 3 * npass + 1] = inv_q
    coefs[3 * npass + 1 : 3 * npass + 2] = inv_pass
    coefs[3 * npass + 2 : 3 * npass + 3] = pos_score
    neg_sum = jnp.sum(exp_neg, axis=0, keepdims=True)
    neg_dot = jnp.sum(exp_neg * neg_score, axis=0, keepdims=True)
    sums[...] = jnp.zeros_like(sums)
    for n in range(nq):
        sums[n : n + 1, :] = neg_sum[:, n * rows : (n + 1) * rows]
        sums[2 * nq + n : 2 * nq + n + 1, :] = neg_dot[:, n * rows : (n + 1) * rows]
    sums[nq : nq + 1, :] = jnp.exp(logit_scale * pos_score[:, :rows])


def weigh(table, other, valid, rows, *after):
    nq, npass = len(query_at), len(pass_at)
    return local(
        functools.partial(weigh_kernel, rows),
        "weigh",
        [((-(-(3 * npass + 3) // 8) * 8, nq * rows), f32), ((-(-3 * nq // 8) * 8, rows), f32)],
        (table, other, valid, *after),
    )


def add_sums_kernel(bit, sums, other, *refs):
    out = refs[-1]
    nq = len(query_at)
    out[...] = sums[...]
    for n, at in enumerate(query_at):
        m = query_at.index(at ^ bit)
        for first in (0, nq, 2 * nq):
            k, l = first + n, first + m
            out[k : k + 1, :] = sums[k : k + 1, :] + other[l : l + 1, :]


def exchange_sums(sums, bit, *after):
    kernel = functools.partial(add_sums_kernel, bit)
    return local(kernel, "add_sums", [(sums.shape, f32)], (sums, swap(sums, "dp", bit), *after))[0]


def spread_query_kernel(rows, far, coefs, pick, p_all, *refs):
    out = refs[-1]
    npass = len(pass_at)
    passages = p_all[...]
    blocks = [b for b, at in enumerate(query_at) if bool(at & query_bits[1]) == far]
    for n, b in enumerate(blocks):
        lanes = slice(b * rows, (b + 1) * rows)
        pieces = []
        for a in range(npass):
            piece = pick[a * rows : (a + 1) * rows, lanes].astype(f32)
            piece = piece * coefs[npass + a : npass + a + 1, lanes]
            pieces.append(piece.T.astype(bf16))
        weights = jnp.concatenate(pieces, axis=1)
        values = jnp.dot(weights, passages, preferred_element_type=f32)
        out[n * rows : (n + 1) * rows, :] = values.astype(out.dtype)


def spread_query(coefs, pick, p_all, rows, far, *after):
    half = (len(query_at) // 2 * rows, p_all.shape[1])
    return local(
        functools.partial(spread_query_kernel, rows, far),
        "spread_query",
        [(half, bf16 if far else f32)],
        (coefs, pick, p_all, *after),
        3,
    )[0]


def column_of(eye, row):
    return jnp.sum(eye * row, axis=1, keepdims=True)


def spread_pass_kernel(rows, blocks, place, scale, coefs, sums, pick, q_all, p_all, *outs):
    nq, npass = len(query_at), len(pass_at)
    eye = eye_of(rows)
    share = scale[:nq] / (sums[:nq] + sums[nq : 2 * nq])
    pos = -share[:1] * sums[:1]
    share = jnp.concatenate([share[n : n + 1] for n in range(nq)], axis=1)
    scaled = share * coefs[3 * npass : 3 * npass + 1]
    queries = q_all[...]
    found = {}
    for a in sorted({a for pair in blocks for a in pair}):
        at = slice(a * rows, (a + 1) * rows)
        chosen = pick[at, :]
        weights = chosen.astype(f32) * (coefs[a : a + 1] * scaled)
        product = share * coefs[2 * npass + a : 2 * npass + a + 1]
        high = product.astype(bf16).astype(f32)
        parts = jnp.concatenate([high, product - high, jnp.zeros((14, nq * rows), f32)], axis=0)
        dots = lax.dot_general(parts.astype(bf16), chosen, nt, preferred_element_type=f32)
        dot = jnp.sum(dots, axis=0, keepdims=True)
        if a == 0:
            own = pos * coefs[3 * npass : 3 * npass + 1, :rows]
            weights = jnp.concatenate([weights[:, :rows] + eye * own, weights[:, rows:]], axis=1)
            dot = dot + pos * coefs[3 * npass + 2 : 3 * npass + 3, :rows]
        values = jnp.dot(weights.astype(bf16), queries, preferred_element_type=f32)
        along = column_of(eye, dot * coefs[3 * npass + 1 : 3 * npass + 2, at])
        found[a] = values - along * p_all[at, :].astype(f32)
    odd = place[0] % 2 == 1
    for out, (a, b) in zip(outs, blocks):
        values = found[a] if a == b else jnp.where(odd, found[b], found[a])
        out[...] = values.astype(out.dtype)


def spread_pass(place, scale, coefs, sums, pick, q_all, p_all, rows, blocks, dtype):
    block = (rows, q_all.shape[1])
    return local(
        functools.partial(spread_pass_kernel, rows, blocks),
        "spread_pass",
        [(block, dtype)] * len(blocks),
        (scale, coefs, sums, pick, q_all, p_all),
        3,
        scalars=[place],
    )


def fold_query_kernel(own, other, kept, sent):
    rows = kept.shape[0]
    total = own[...] + other[...].astype(f32)
    kept[...] = total[:rows]
    sent[...] = total[rows:].astype(bf16)


def fold_query(own, other):
    half = (own.shape[0] // 2, own.shape[1])
    return local(fold_query_kernel, "fold_query", [(half, f32), (half, bf16)], (own, other))


def grad_query_kernel(own, other, scale, sums, coefs, raw, raw_pass, grad, rounded):
    nq, npass = len(query_at), len(pass_at)
    rows = own.shape[0]
    eye = eye_of(rows)
    inv_norm = coefs[3 * npass : 3 * npass + 1, :rows]
    share = scale[:1] / (sums[:1] + sums[nq : nq + 1])
    pos = sums[:1] * coefs[3 * npass + 1 : 3 * npass + 2, :rows]
    dot = share * (sums[2 * nq : 2 * nq + 1] - sums[:1] * coefs[3 * npass + 2 : 3 * npass + 3, :rows])
    total = own[...] + other[...].astype(f32)
    total = total - column_of(eye, pos) * raw_pass[:rows, :].astype(f32)
    values = column_of(eye, share * inv_norm) * total
    values = values - column_of(eye, dot * inv_norm * inv_norm) * raw[:rows, :].astype(f32)
    grad[...] = values
    rounded[...] = values.astype(bf16)


def grad_pass_kernel(own, first, second, third, coefs, after, grad, rounded):
    npass = len(pass_at)
    rows = own.shape[0]
    inv_norm = column_of(eye_of(rows), coefs[3 * npass + 1 : 3 * npass + 2, :rows])
    others = first[...].astype(f32) + second[...].astype(f32) + third[...].astype(f32)
    values = inv_norm * (own[...] + others)
    grad[...] = values
    rounded[...] = values.astype(bf16)


def grad_out(kernel, name, own, operands):
    return local(kernel, name, [(own.shape, f32), (own.shape, bf16)], (own, *operands))


def decode_near_kernel(tile, mine, w_out, out):
    for t in range(w_out.shape[1] // tile):
        at = slice(t * tile, (t + 1) * tile)
        out[:, at] = jnp.dot(mine[...], w_out[:, at], preferred_element_type=f32)


def decode_far_kernel(tower, tile, near, theirs, slope, w_out, w_in, *refs):
    grad_pre, send = refs[-2:]
    rows = theirs.shape[0]
    for t in range(w_out.shape[1] // tile):
        at = slice(t * tile, (t + 1) * tile)
        hidden = near[:, at] + jnp.dot(theirs[...], w_out[:, at], preferred_element_type=f32)
        grad_pre[:, at] = (hidden * slope[tower * rows : (tower + 1) * rows, at].astype(f32)).astype(bf16)
    send[...] = jnp.dot(grad_pre[...], w_in[...], preferred_element_type=f32).astype(bf16)


def decode_own_kernel(grad, grad_pre, w_in, *refs):
    refs[-1][...] = grad[...] + jnp.dot(grad_pre[...], w_in[...], preferred_element_type=f32)


def decode_far(rounded, slope, tower, w_out_near, w_out_far, w_in_far, *after):
    rows, hidden = rounded.shape[0], slope.shape[1]
    tile = min(512, hidden)
    near = local(
        functools.partial(decode_near_kernel, tile),
        "decode_near",
        [((rows, hidden), f32)],
        (rounded, w_out_near),
        2,
    )[0]
    return local(
        functools.partial(decode_far_kernel, tower, tile),
        "decode_far",
        [((rows, hidden), bf16), (rounded.shape, bf16)],
        (near, swap(rounded, "mp", 1), slope, w_out_far, w_in_far, *after),
        2,
    )


def decode_own(grad, grad_pre, w_in_near, *after):
    return local(
        decode_own_kernel, "decode_own", [(grad.shape, f32)], (grad, grad_pre, w_in_near, *after), 2
    )[0]


def finish_kernel(own, other, *refs):
    out, done = refs[-2:]
    out[...] = (own[...] + other[...].astype(f32)).astype(bf16)
    done[...] = jnp.zeros_like(done)


def finish(own, other, name, *after):
    return pl.pallas_call(
        finish_kernel,
        in_specs=[vmem] * (2 + len(after)),
        out_specs=[vmem] * 2,
        out_shape=[jax.ShapeDtypeStruct(own.shape, bf16), pltpu.VMEM((8, 128), f32)],
        compiler_params=pltpu.CompilerParams(vmem_limit_bytes=1 << 20),
        name=name,
    )(*[pltpu.with_memory_space_constraint(x, pltpu.VMEM) for x in (own, other, *after)])


def paired_shards(
    query_states, passage_states, w_in, w_out, neg_owner, neg_mask, served_rows, loss_scale
):
    rows = query_states.shape[0]
    owners = served_rows.shape[1]
    me = lax.axis_index("mp").astype(jnp.int32).reshape(1)
    place = lax.axis_index("dp").astype(jnp.int32).reshape(1)
    send_q, send_p, states, hidden, pre_act, scale, w_in, w_out_far = encode_far(
        me, place, loss_scale.reshape(1), query_states, passage_states, w_in, w_out
    )
    own_q, own_p, w_out_near, slots, served = encode_near(
        me, w_out, neg_owner, neg_mask, served_rows, hidden, states
    )
    slope = local(slope_kernel, "slope", [(pre_act.shape, bf16)], (pre_act,))[0]
    w_in_far = flip_rows(me, w_in, True, "flip_in_far")
    w_in_near = flip_rows(me, w_in, False, "flip_in_near")
    w_out_far, w_out_near = flip(w_out_far, "flip_out_far"), flip(w_out_near, "flip_out_near")
    raw_q = pack(own_q, swap(send_q, "mp", 1), slots)
    raw_p = pack(own_p, swap(send_p, "mp", 1), served)
    q_blocks = gather_blocks(raw_q, query_bits)
    p_blocks = gather_blocks(raw_p, pass_bits)

    table, valid, pick, p_all, q_all = score(
        place, q_blocks, p_blocks, rows, owners, w_out_near, slope, w_in_far
    )
    coefs, sums = weigh(table, swap(table, "mp", 1), valid, rows, w_out_far, w_in_near)
    sent_q = spread_query(coefs, pick, p_all, rows, True)
    sums = exchange_sums(sums, query_bits[1], sent_q)
    kept_q = spread_query(coefs, pick, p_all, rows, False)
    kept_q, sent_q = fold_query(kept_q, swap(sent_q, "dp", query_bits[1]))
    sums = exchange_sums(sums, query_bits[0], sent_q)
    operands = (place, scale, coefs, sums, pick, q_all, p_all, rows)
    order = tuple(zip((3, 2, 1), (2, 3, 1)))
    sent_p = spread_pass(*operands, order, bf16)
    kept_p = spread_pass(*operands, ((0, 0),), f32)[0]
    others_p = [
        swap(block, "dp", pass_at[a], pass_at[b]) for block, (a, b) in zip(sent_p, order)
    ]
    grad_q, round_q = grad_out(
        grad_query_kernel,
        "grad_query",
        kept_q,
        (swap(sent_q, "dp", query_bits[0]), scale, sums, coefs, raw_q, raw_p),
    )
    grad_p, round_p = grad_out(
        grad_pass_kernel,
        "grad_pass",
        kept_p,
        (*others_p, coefs, round_q),
    )
    pre_q, send_q = decode_far(round_q, slope, 0, w_out_near, w_out_far, w_in_far)
    pre_p, send_p = decode_far(round_p, slope, 1, w_out_near, w_out_far, w_in_far, send_q)
    own_q = decode_own(grad_q, pre_q, w_in_near, send_p)
    own_p = decode_own(grad_p, pre_p, w_in_near)
    out_q, done_q = finish(own_q, swap(send_q, "mp", 1), "out_query")
    out_p, _ = finish(own_p, swap(send_p, "mp", 1), "out_pass", done_q)
    return (out_q, out_p)


def solution(mesh):
    in_specs = (
        P("dp", None),
        P("dp", None),
        P(None, "mp"),
        P("mp", None),
        P("dp", None),
        P("dp", None),
        P("dp", None, None),
        P(),
    )
    out_specs = (P("dp", "mp"), P("dp", "mp"))
    gathered = len(query_at) * len(pass_at)
    paired = mesh.shape["mp"] == 2 and mesh.shape["dp"] == gathered
    shards = paired_shards if paired else general_shards
    return jax.shard_map(shards, mesh=mesh, in_specs=in_specs, out_specs=out_specs, check_vma=False)
```
